128 devices in a mesh: ctx: 16 (over z, y_hi, core), head: 8 (over x, y_lo).
Axes of the slice: x: 4, y: 4 (y_hi: 2, y_lo: 2; y = y_hi * 2 + y_lo), z: 4, core: 2. Of those that a mesh axis runs over, the one named last changes fastest.
Arguments:
- hidden: bfloat16 [2048, 7168], P('ctx', 'head'), may hold values from -6 to 6
- kv_down: bfloat16 [7168, 576], P('head'), may hold values from -0.0625 to 0.0625
- kv_gain: float32 [512], replicated, may hold values from 0.5 to 2
- queries: bfloat16 [2048, 128, 576], P('ctx', 'head'), may hold values from -64 to 64
- out_grad: bfloat16 [2048, 128, 512], P('ctx', 'head'), may hold values from -6 to 6
- span_table: int32 [32], replicated, may hold values from 0 to 31, each once
Outputs:
- query_grad: bfloat16 [2048, 128, 576], P('ctx', 'head')
- hidden_grad: bfloat16 [2048, 7168], P('ctx', 'head')
- down_grad: float32 [7168, 576], P('head')
- gain_grad: float32 [512], replicated
The draws below stay inside these ranges and needn't reach their ends.
Inputs may be any that keep to these rules, and one draw needn't show every extreme that they name: `span_table`: every span number appears exactly once.
All inputs are finite; a program needn't handle non-finite values.
Results may differ from the reference program's by a relative error of at most 0.03.
Values may be sent and summed in bfloat16 or wider, within the bound.
A program may use at most 128 MiB of HBM per device.

```python
import math
import jax
import jax.numpy as jnp
from jax import lax

D = 7168
HEADS = 128
LATENT = 512
ROPE = 64
SPAN = 64
TOKENS = 2048
N_CTX = 16


def draw_queries(key, part):
    key = jax.random.fold_in(key, 7)
    base_key = jax.random.fold_in(key, 0)
    full_shape = (TOKENS, HEADS, LATENT + ROPE)
    values = jnp.clip(jax.random.normal(base_key, full_shape, jnp.float32), -6.0, 6.0)
    return values.astype(jnp.bfloat16)


def level_of(own_key, extent, pieces, smallest, largest):
    factor_of, own = 1.0, jax.random.fold_in(own_key, 6)
    for axis_at, parts in pieces:
        steps = jnp.exp(jax.random.uniform(jax.random.fold_in(own, axis_at), (parts,), jnp.float32, smallest / len(pieces), largest / len(pieces)))
        factor_of = factor_of * jnp.repeat(steps, extent[axis_at] // parts).reshape([-1 if axis == axis_at else 1 for axis in range(len(extent))])
    return factor_of


def noise(own_key, dims, spread, reach, cuts=(), kind=jnp.bfloat16):
    entries = jax.random.normal(own_key, dims, jnp.float32) * spread
    if len(cuts) > 0:
        entries = level_of(own_key, dims, cuts, -0.22, 0.18) * entries
    return jnp.clip(entries, min=-reach, max=reach).astype(kind)


def setup_inputs(seed: int = 0) -> dict:
    keys = jax.random.split(jax.random.key(seed), 7)
    hidden = noise(keys[0], (TOKENS, D), 1.0, 6.0, ((0, 16), (1, 8)))
    kv_down = noise(keys[1], (D, LATENT + ROPE), D ** -0.5, 0.0625, ((0, 8),))
    kv_gain = jnp.clip(jnp.exp(jax.random.uniform(keys[2], (LATENT,), jnp.float32, math.log(0.5), math.log(2.0))), 0.5, 2.0)
    queries = draw_queries(jax.random.fold_in(keys[6], 71), 0)
    out_grad = noise(keys[4], (TOKENS, HEADS, LATENT), 1.0, 6.0, ((0, 16), (1, 8)))
    span_table = jax.random.permutation(keys[5], 2 * N_CTX).astype(jnp.int32)
    return {"hidden": hidden, "kv_down": kv_down, "kv_gain": kv_gain, "queries": queries, "out_grad": out_grad, "span_table": span_table}


eps_norm = 1e-06

def positions_of(span_table, row_total, span_rows):
    row_ids = jnp.arange(row_total, dtype=jnp.int32)
    return span_table[row_ids // span_rows] * span_rows + row_ids % span_rows

def rope_tables(token_pos, half_width):
    freq = jnp.exp(-math.log(10000.0) * jnp.arange(half_width, dtype=jnp.float32) / half_width)
    angle = token_pos.astype(jnp.float32)[:, None] * freq[None, :]
    return (jnp.cos(angle), jnp.sin(angle))

def make_keys(raw_keys, kv_gain, token_pos):
    latent_width = kv_gain.shape[0]
    latent_part = raw_keys[:, :latent_width]
    rope_part = raw_keys[:, latent_width:]
    inv_rms = lax.rsqrt(lax.optimization_barrier(jnp.mean(latent_part * latent_part, axis=1, keepdims=True)) + eps_norm)
    normed = latent_part * inv_rms * kv_gain[None, :]
    half_width = rope_part.shape[1] // 2
    cos_table, sin_table = rope_tables(token_pos, half_width)
    front_half = rope_part[:, :half_width]
    back_half = rope_part[:, half_width:]
    turned = jnp.concatenate([front_half * cos_table - back_half * sin_table, back_half * cos_table + front_half * sin_table], axis=1)
    key_rows = jnp.concatenate([normed, turned], axis=1).astype(jnp.bfloat16)
    return (key_rows, inv_rms, cos_table, sin_table)

def key_backward(raw_keys, inv_rms, cos_table, sin_table, kv_gain, key_grad):
    latent_width = kv_gain.shape[0]
    latent_part = raw_keys[:, :latent_width]
    latent_grad = key_grad[:, :latent_width]
    scaled = latent_grad * kv_gain[None, :]
    gain_term = lax.optimization_barrier(jnp.sum(latent_grad * latent_part * inv_rms, axis=0))
    cube = inv_rms * inv_rms * inv_rms
    latent_back = inv_rms * scaled - latent_part * cube * lax.optimization_barrier(jnp.mean(scaled * latent_part, axis=1, keepdims=True))
    half_width = cos_table.shape[1]
    front_grad = key_grad[:, latent_width:latent_width + half_width]
    back_grad = key_grad[:, latent_width + half_width:]
    rope_back = jnp.concatenate([front_grad * cos_table + back_grad * sin_table, back_grad * cos_table - front_grad * sin_table], axis=1)
    return (jnp.concatenate([latent_back, rope_back], axis=1), gain_term)

def reference(hidden, kv_down, kv_gain, queries, out_grad, span_table):
    row_total = hidden.shape[0]
    token_pos = positions_of(span_table, row_total, SPAN)
    raw_keys = jnp.dot(hidden, kv_down, preferred_element_type=jnp.float32)
    key_rows, inv_rms, cos_table, sin_table = make_keys(raw_keys, kv_gain, token_pos)
    score_scale = 1.0 / math.sqrt(192.0)
    latent_width = kv_gain.shape[0]
    key_width = key_rows.shape[1]
    value_rows = key_rows[:, :latent_width]
    allowed = token_pos[None, :] <= token_pos[:, None]

    def per_head(key_total, inputs):
        query_head, grad_head = inputs
        scores = jnp.dot(query_head, key_rows.T, preferred_element_type=jnp.float32) * score_scale
        scores = jnp.where(allowed, scores, -jnp.inf)
        probability = jax.nn.softmax(scores, axis=1)
        prob_grad = jnp.dot(grad_head, value_rows.T, preferred_element_type=jnp.float32)
        row_delta = lax.optimization_barrier(jnp.sum(probability * prob_grad, axis=1, keepdims=True))
        score_grad = (probability * (prob_grad - row_delta)).astype(jnp.bfloat16)
        value_weights = probability.astype(jnp.bfloat16)
        query_term = (score_scale * jnp.dot(score_grad, key_rows, preferred_element_type=jnp.float32)).astype(jnp.bfloat16)
        key_term = score_scale * jnp.dot(score_grad.T, query_head, preferred_element_type=jnp.float32)
        value_term = jnp.dot(value_weights.T, grad_head, preferred_element_type=jnp.float32)
        key_term = key_term + jnp.pad(value_term, ((0, 0), (0, key_width - latent_width)))
        return (key_total + key_term, query_term)
    key_grad, query_terms = lax.scan(per_head, jnp.zeros(key_rows.shape, jnp.float32), (jnp.swapaxes(queries, 0, 1), jnp.swapaxes(out_grad, 0, 1)))
    raw_back, gain_grad = key_backward(raw_keys, inv_rms, cos_table, sin_table, kv_gain, key_grad)
    raw_grad = raw_back.astype(jnp.bfloat16)
    hidden_grad = jnp.dot(raw_grad, kv_down.T, preferred_element_type=jnp.float32).astype(jnp.bfloat16)
    down_grad = jnp.dot(hidden.T, raw_grad, preferred_element_type=jnp.float32)
    return (jnp.swapaxes(query_terms, 0, 1), hidden_grad, down_grad, gain_grad)
```

```python
import functools
import math

import jax
import jax.numpy as jnp
import numpy as np
from jax import lax
from jax.experimental import pallas as pl
from jax.experimental.pallas import tpu as pltpu
from jax.sharding import PartitionSpec as P

MESH = pl.DeviceIdType.MESH
F32 = jnp.float32
BF16 = jnp.bfloat16
LATENT = 512
WIDTH = 576
PAD = 640
SPAN = 64
TOKENS = 2048
PIECE = 16
EPS = 1e-06
SCALE = 1.0 / math.sqrt(192.0)
KEY_BLOCK = 256
ROW_BLOCK = 512


def rope_rows():
    half = (WIDTH - LATENT) // 2
    freq = np.exp(np.float32(-math.log(10000.0)) * np.arange(half, dtype=np.float32) / np.float32(half))
    angle = np.arange(TOKENS, dtype=np.float32)[:, None] * freq.astype(np.float32)[None, :]
    cos, sin = np.cos(angle.astype(np.float64)), np.sin(angle.astype(np.float64))
    none = np.zeros((TOKENS, PAD - WIDTH))
    cos_rows = np.concatenate([cos, cos, none], axis=1)
    sin_rows = np.concatenate([-sin, sin, none], axis=1)
    return np.concatenate([cos_rows, sin_rows], axis=1).astype(np.float32)


def nt_dot(left, right):
    return lax.dot_general(left, right, (((1,), (1,)), ((), ())), preferred_element_type=F32)


class Place:
    def __init__(self):
        ctx, head = lax.axis_index("ctx"), lax.axis_index("head")
        self.ctx, self.head = ctx, head
        self.core = lax.rem(ctx, 2)
        self.x = lax.div(head, 2)
        self.y = lax.rem(lax.div(ctx, 2), 2) * 2 + lax.rem(head, 2)
        self.z = lax.div(ctx, 4)
        self.own = (
            self.pick(self.x, self.y),
            self.pick(self.y, self.z),
            self.pick(self.z, self.x),
        )

    def pick(self, first, second):
        return first + self.core * (second - first)

    def device(self, x, y, z, core):
        ctx = z * 4 + lax.div(y, 2) * 2 + core
        return (ctx, x * 2 + lax.rem(y, 2))

    def shifted(self, dx, dy, dz):
        return self.device(
            lax.rem(self.x + dx, 4), lax.rem(self.y + dy, 4), lax.rem(self.z + dz, 4), self.core
        )

    def peer(self, level, d):
        one, other = d * self.core, d * (1 - self.core)
        if level == 0:
            return self.shifted(other, one, 0)
        if level == 1:
            return self.shifted(0, other, one)
        return self.shifted(one, 0, other)

    def twin(self):
        return self.device(self.x, self.y, self.z, 1 - self.core)


def remote(src, dst, send_sem, recv_sem, device):
    return pltpu.make_async_remote_copy(
        src_ref=src, dst_ref=dst, send_sem=send_sem, recv_sem=recv_sem, device_id=device, device_id_type=MESH
    )


def meet(devices):
    barrier = pltpu.get_barrier_semaphore()
    for device in devices:
        pl.semaphore_signal(barrier, inc=1, device_id=device, device_id_type=MESH)
    return lambda: pl.semaphore_wait(barrier, len(devices))


def gather_rows(place, rows, send, recv, first, each_level=None):
    core = place.core
    a1, a2, a3 = place.own
    sent = []

    def go(region, slot, device):
        copy = remote(region, region, send.at[first + slot], recv.at[first + slot], device)
        copy.start()
        sent.append(copy)
        return copy

    small = [go(rows.at[core, a3, a2, a1], d - 1, place.peer(0, d)) for d in (1, 2, 3)]
    if each_level is not None:
        each_level(0)
    for copy in small:
        copy.wait_recv()
    middle = [go(rows.at[core, a3, a2], 2 + d, place.peer(1, d)) for d in (1, 2, 3)]
    if each_level is not None:
        each_level(1)
    for copy in middle:
        copy.wait_recv()
    up, down = place.peer(2, 1), place.peer(2, 3)
    before, after, across = lax.rem(a3 + 3, 4), lax.rem(a3 + 1, 4), lax.rem(a3 + 2, 4)
    low, high = pl.ds(0, 2), pl.ds(2, 2)
    up_low = go(rows.at[core, a3, low], 6, up)
    down_high = go(rows.at[core, a3, high], 7, down)
    up_high = go(rows.at[core, a3, high], 8, up)
    down_low = go(rows.at[core, a3, low], 9, down)
    twin = place.twin()
    pairs = [go(rows.at[core, a3], 12, twin)]
    if each_level is not None:
        each_level(2)
    up_low.wait_recv()
    far_low = go(rows.at[core, before, low], 10, up)
    down_high.wait_recv()
    far_high = go(rows.at[core, after, high], 11, down)
    up_high.wait_recv()
    pairs.append(go(rows.at[core, before], 13, twin))
    down_low.wait_recv()
    pairs.append(go(rows.at[core, after], 14, twin))
    far_low.wait_recv()
    pairs.append(go(rows.at[core, across, low], 15, twin))
    far_high.wait_recv()
    pairs.append(go(rows.at[core, across, high], 16, twin))
    for copy in pairs:
        copy.wait_recv()
    for copy in sent:
        copy.wait_send()


def swap_halves(tail):
    lane = lax.broadcasted_iota(jnp.int32, tail.shape, 1)
    return jnp.where(lane < 32, pltpu.roll(tail, 96, 1), pltpu.roll(tail, 32, 1))


def keys_kernel(hidden, kv_down, gain, rope, rows, raw_out, part, landed, send, recv):
    place = Place()
    devices = [(place.ctx, lax.rem(place.head + d, 8)) for d in range(1, 8)]
    devices += [place.shifted(0, d, 0) for d in (1, 2, 3)]
    devices += [place.shifted(0, 0, d) for d in (1, 2, 3)]
    devices += [place.shifted(d, 0, 0) for d in (1, 2, 3)]
    devices.append(place.twin())
    met = meet(devices)
    product = jnp.dot(hidden[...], kv_down[...], preferred_element_type=F32)
    part[:, :, :WIDTH] = product.reshape(8, PIECE, WIDTH)
    part[:, :, WIDTH:] = jnp.zeros((8, PIECE, PAD - WIDTH), F32)
    landed[place.head] = part[place.head]
    met()
    copies = []
    for d in range(1, 8):
        other = lax.rem(place.head + d, 8)
        copies.append(
            remote(part.at[other], landed.at[place.head], send.at[d - 1], recv.at[d - 1], (place.ctx, other))
        )
        copies[-1].start()
    cos, sin = rope[:, :128], rope[:, 128:]
    for copy in copies:
        copy.wait_recv()
    raw = landed[0]
    for k in range(1, 8):
        raw = raw + landed[k]
    raw_out[...] = raw
    latent, tail = raw[:, :LATENT], raw[:, LATENT:]
    inv_rms = lax.rsqrt(jnp.mean(latent * latent, axis=1, keepdims=True) + EPS)
    normed = latent * inv_rms * gain[...]
    turned = tail * cos + swap_halves(tail) * sin
    a1, a2, a3 = place.own
    rows[place.core, a3, a2, a1, :, :LATENT] = normed.astype(BF16)
    rows[place.core, a3, a2, a1, :, LATENT:] = turned.astype(BF16)
    gather_rows(place, rows, send, recv, 7)
    for copy in copies:
        copy.wait_send()


def make_keys(hidden, kv_down, gain, rope):
    vmem = pl.BlockSpec(memory_space=pltpu.VMEM)
    return pl.pallas_call(
        keys_kernel,
        out_shape=(
            jax.ShapeDtypeStruct((2, 4, 4, 4, PIECE, PAD), BF16),
            jax.ShapeDtypeStruct((PIECE, PAD), F32),
        ),
        in_specs=[vmem, vmem, vmem, vmem],
        out_specs=(vmem, vmem),
        scratch_shapes=[
            pltpu.VMEM((8, PIECE, PAD), F32),
            pltpu.VMEM((8, PIECE, PAD), F32),
            pltpu.SemaphoreType.DMA((24,)),
            pltpu.SemaphoreType.DMA((24,)),
        ],
        compiler_params=pltpu.CompilerParams(
            collective_id=0, has_side_effects=True, vmem_limit_bytes=32 * 2**20
        ),
        cost_estimate=pl.CostEstimate(flops=132 * 10**6, bytes_accessed=40 * 2**20, transcendentals=0),
    )(hidden, kv_down, gain, rope)


def piece_slot(core, a3, a2, a1):
    x = a1 + core * (a3 - a1)
    y = a2 + core * (a1 - a2)
    z = a3 + core * (a2 - a3)
    ctx = z * 4 + lax.div(y, 2) * 2 + core
    head = x * 2 + lax.rem(y, 2)
    return ctx * 2 + lax.div(head, 4), lax.rem(head, 4)


def split_piece(index):
    return lax.div(index, 16), lax.rem(lax.div(index, 4), 4), lax.rem(index, 4)


def attend_kernel(
    pieces, queries, grads, span, query_out, own_out, other_out, keys, keys_t, scores, prob_grads, weights, score_grads, key_total, query_total
):
    ctx = lax.axis_index("ctx")
    my_core = lax.rem(ctx, 2)
    blocks = TOKENS // KEY_BLOCK
    half_rows = queries.shape[0] // 2

    def first_row(core, index):
        slot, quarter = piece_slot(core, *split_piece(index))
        return pl.multiple_of(span[slot] * SPAN + quarter * PIECE, PIECE)

    def place_piece(index, carry):
        for core in range(2):
            keys[pl.ds(first_row(core, index), PIECE), :] = pieces[core * 64 + index]
        return carry

    lax.fori_loop(0, 64, place_piece, 0, unroll=4)

    def turn_block(block, carry):
        at = pl.multiple_of(block * KEY_BLOCK, KEY_BLOCK)
        keys_t[:, pl.ds(at, KEY_BLOCK)] = keys[pl.ds(at, KEY_BLOCK), :].T
        return carry

    lax.fori_loop(0, blocks, turn_block, 0)

    spans = [span[2 * ctx + s] for s in range(2)]
    counts = [lax.div(spans[s] * SPAN, KEY_BLOCK) + 1 for s in range(2)]
    for s in range(2):
        for r in range(half_rows // ROW_BLOCK):
            at_row = s * half_rows + r * ROW_BLOCK
            columns = pl.ds(at_row, ROW_BLOCK)
            query_pos = (
                spans[s] * SPAN
                + r * (ROW_BLOCK // 16)
                + lax.div(lax.broadcasted_iota(jnp.int32, (1, ROW_BLOCK), 1), 16)
            )

            def score_block(block, top, columns=columns, query_pos=query_pos):
                at = pl.multiple_of(block * KEY_BLOCK, KEY_BLOCK)
                key_block = keys[pl.ds(at, KEY_BLOCK), :]
                raw = nt_dot(key_block[:, :WIDTH], queries[columns, :])
                key_pos = at + lax.broadcasted_iota(jnp.int32, (KEY_BLOCK, ROW_BLOCK), 0)
                raw = jnp.where(key_pos <= query_pos, raw, -1e30)
                scores[pl.ds(at, KEY_BLOCK), :] = raw
                prob_grads[pl.ds(at, KEY_BLOCK), :] = nt_dot(key_block[:, :LATENT], grads[columns, :])
                return jnp.maximum(top, jnp.max(raw.reshape(KEY_BLOCK // 8, 8, ROW_BLOCK), axis=0))

            top = lax.fori_loop(0, counts[s], score_block, jnp.full((8, ROW_BLOCK), -1e30, F32))
            top = jnp.max(top, axis=0, keepdims=True)

            def mass_block(block, sums, top=top):
                mass, dot = sums
                at = pl.multiple_of(block * KEY_BLOCK, KEY_BLOCK)
                weight = jnp.exp2((scores[pl.ds(at, KEY_BLOCK), :] - top) * (SCALE * math.log2(math.e)))
                scores[pl.ds(at, KEY_BLOCK), :] = weight
                product = weight * prob_grads[pl.ds(at, KEY_BLOCK), :]
                mass = mass + jnp.sum(weight.reshape(KEY_BLOCK // 8, 8, ROW_BLOCK), axis=0)
                dot = dot + jnp.sum(product.reshape(KEY_BLOCK // 8, 8, ROW_BLOCK), axis=0)
                return mass, dot

            zero = jnp.zeros((8, ROW_BLOCK), F32)
            mass, dot = lax.fori_loop(0, counts[s], mass_block, (zero, zero))
            share = 1.0 / jnp.sum(mass, axis=0, keepdims=True)
            delta = jnp.sum(dot, axis=0, keepdims=True) * share
            query_total[...] = jnp.zeros_like(query_total)

            def grad_block(block, carry, columns=columns, share=share, delta=delta):
                at = pl.multiple_of(block * KEY_BLOCK, KEY_BLOCK)
                here = pl.ds(at, KEY_BLOCK)
                probability = scores[here, :] * share
                score_grad = (probability * (prob_grads[here, :] - delta)).astype(BF16)
                weights[here, columns] = probability.astype(BF16)
                score_grads[here, columns] = score_grad
                query_total[...] += jnp.dot(keys_t[:WIDTH, here], score_grad, preferred_element_type=F32)
                return carry

            lax.fori_loop(0, counts[s], grad_block, 0)
            query_out[columns, :] = (query_total[...] * SCALE).T.astype(BF16)

    def key_block(block, carry):
        here = pl.ds(pl.multiple_of(block * KEY_BLOCK, KEY_BLOCK), KEY_BLOCK)
        key_total[here, :] = jnp.zeros((KEY_BLOCK, PAD), F32)
        for s in range(2):
            rows = pl.ds(s * half_rows, half_rows)

            @pl.when(block < counts[s])
            def _():
                by_score = jnp.dot(score_grads[here, rows], queries[rows, :], preferred_element_type=F32) * SCALE
                by_value = jnp.dot(weights[here, rows], grads[rows, :], preferred_element_type=F32)
                key_total[here, :LATENT] += by_score[:, :LATENT] + by_value
                key_total[here, LATENT:WIDTH] += by_score[:, LATENT:]

        return carry

    lax.fori_loop(0, blocks, key_block, 0)

    def hand_out(index, carry):
        own_out[index] = key_total[pl.ds(first_row(my_core, index), PIECE), :]
        other_out[index] = key_total[pl.ds(first_row(1 - my_core, index), PIECE), :].astype(BF16)
        return carry

    lax.fori_loop(0, 64, hand_out, 0, unroll=4)


def attend(pieces, queries, grads, span_table):
    vmem = pl.BlockSpec(memory_space=pltpu.VMEM)
    smem = pl.BlockSpec(memory_space=pltpu.SMEM)
    rows = queries.shape[0]
    return pl.pallas_call(
        attend_kernel,
        out_shape=(
            jax.ShapeDtypeStruct((rows, WIDTH), BF16),
            jax.ShapeDtypeStruct((64, PIECE, PAD), F32),
            jax.ShapeDtypeStruct((64, PIECE, PAD), BF16),
        ),
        in_specs=[vmem, vmem, vmem, smem],
        out_specs=(vmem, vmem, vmem),
        scratch_shapes=[
            pltpu.VMEM((TOKENS, PAD), BF16),
            pltpu.VMEM((PAD, TOKENS), BF16),
            pltpu.VMEM((TOKENS, ROW_BLOCK), F32),
            pltpu.VMEM((TOKENS, ROW_BLOCK), F32),
            pltpu.VMEM((TOKENS, rows), BF16),
            pltpu.VMEM((TOKENS, rows), BF16),
            pltpu.VMEM((TOKENS, PAD), F32),
            pltpu.VMEM((WIDTH, ROW_BLOCK), F32),
        ],
        compiler_params=pltpu.CompilerParams(vmem_limit_bytes=60 * 2**20),
        cost_estimate=pl.CostEstimate(flops=23 * 10**9, bytes_accessed=20 * 2**20, transcendentals=2**22),
    )(pieces, queries, grads, span_table)


def grads_kernel(own, other, raw_ref, gain, rope, rows, gain_out, sums, twin_in, packed, relay, halves, second, third, gains, gains_in, send, recv):
    place = Place()
    a1, a2, a3 = place.own
    devices = [place.peer(level, d) for level in range(3) for d in (1, 2, 3)]
    devices.append(place.twin())
    met = meet(devices)
    met()
    sent = []

    def go(src, dst, slot, device):
        copy = remote(src, dst, send.at[slot], recv.at[slot], device)
        copy.start()
        sent.append(copy)
        return copy

    order = [lax.rem(a3 + d, 4) for d in (2, 1, 3, 0)]
    twin_own = place.pick(place.x, place.z)
    twin_order = [lax.rem(twin_own + d, 4) for d in (2, 1, 3, 0)]
    pairs = [go(other.at[target], twin_in.at[target], k, place.twin()) for k, target in enumerate(twin_order)]

    def add_twin(target, low, count):
        def body(index, carry):
            at2, at1 = lax.div(index, 4), lax.rem(index, 4)
            total = own[target, at2, at1] + twin_in[target, at2, at1].astype(F32)
            sums[target, at2, at1] = total
            packed[target, at2, at1] = total.astype(BF16)
            return carry

        lax.fori_loop(low * 4, (low + count) * 4, body, 0, unroll=4)

    def add_relay(target, side, low):
        def body(index, carry):
            at2, at1 = lax.div(index, 4), lax.rem(index, 4)
            total = sums[target, low + at2, at1] + relay[side, at2, at1].astype(F32)
            packed[target, low + at2, at1] = total.astype(BF16)
            return carry

        lax.fori_loop(0, 8, body, 0, unroll=4)

    up, down = place.peer(2, 1), place.peer(2, 3)
    across, after, before = order[0], order[1], order[2]
    low, high = pl.ds(0, 2), pl.ds(2, 2)
    pairs[0].wait_recv()
    add_twin(across, 0, 4)
    up_relay = go(packed.at[across, low], relay.at[0], 4, up)
    down_relay = go(packed.at[across, high], relay.at[1], 5, down)
    pairs[1].wait_recv()
    add_twin(after, 0, 4)
    up_high = go(packed.at[after, high], halves.at[0, high], 6, up)
    pairs[2].wait_recv()
    add_twin(before, 0, 4)
    down_low = go(packed.at[before, low], halves.at[1, low], 7, down)
    up_relay.wait_recv()
    add_relay(after, 0, 0)
    up_low = go(packed.at[after, low], halves.at[0, low], 8, up)
    down_relay.wait_recv()
    add_relay(before, 1, 2)
    down_high = go(packed.at[before, high], halves.at[1, high], 9, down)
    pairs[3].wait_recv()
    for copy in (up_high, down_low, up_low, down_high):
        copy.wait_recv()

    def add_halves(index, carry):
        at2, at1 = lax.div(index, 4), lax.rem(index, 4)
        total = own[a3, at2, at1] + twin_in[a3, at2, at1].astype(F32)
        sums[a3, at2, at1] = total + halves[0, at2, at1].astype(F32) + halves[1, at2, at1].astype(F32)
        return carry

    lax.fori_loop(0, 16, add_halves, 0, unroll=4)
    copies = [
        go(sums.at[a3, lax.rem(a2 + d, 4)], second.at[d - 1], 9 + d, place.peer(1, d)) for d in (1, 2, 3)
    ]
    for copy in copies:
        copy.wait_recv()
    for k in range(4):
        sums[a3, a2, k] = sums[a3, a2, k] + second[0, k] + second[1, k] + second[2, k]
    copies = [
        go(sums.at[a3, a2, lax.rem(a1 + d, 4)], third.at[d - 1], 12 + d, place.peer(0, d)) for d in (1, 2, 3)
    ]
    cos, sin = rope[:, :128], rope[:, 128:]
    raw = raw_ref[...]
    latent = raw[:, :LATENT]
    inv_rms = lax.rsqrt(jnp.mean(latent * latent, axis=1, keepdims=True) + EPS)
    cube = inv_rms * inv_rms * inv_rms
    for copy in copies:
        copy.wait_recv()
    key_grad = sums[a3, a2, a1] + third[0] + third[1] + third[2]
    latent_grad, tail = key_grad[:, :LATENT], key_grad[:, LATENT:]
    scaled = latent_grad * gain[...]
    latent_back = inv_rms * scaled - latent * cube * jnp.mean(scaled * latent, axis=1, keepdims=True)
    rope_back = tail * cos - swap_halves(tail) * sin
    rows[place.core, a3, a2, a1, :, :LATENT] = latent_back.astype(BF16)
    rows[place.core, a3, a2, a1, :, LATENT:] = rope_back.astype(BF16)
    term = jnp.sum(latent_grad * latent * inv_rms, axis=0, keepdims=True)

    state = {"total": jnp.broadcast_to(term, (8, LATENT)), "copies": None}

    def add_level(level):
        for copy in state["copies"]:
            copy.wait_recv()
        total = gains_in[level, 0]
        for k in range(1, 4):
            total = total + gains_in[level, k]
        state["total"] = total

    def gain_level(level):
        if level > 0:
            add_level(level - 1)
        gains[level] = state["total"]
        gains_in[level, place.own[level]] = state["total"]
        state["copies"] = [
            go(gains.at[level], gains_in.at[level, place.own[level]], 32 + level * 3 + d, place.peer(level, d))
            for d in (1, 2, 3)
        ]

    gather_rows(place, rows, send, recv, 16, gain_level)
    add_level(2)
    gains[3] = state["total"]
    gains_in[3, place.core] = state["total"]
    last = go(gains.at[3], gains_in.at[3, place.core], 42, place.twin())
    last.wait_recv()
    gain_out[...] = gains_in[3, 0] + gains_in[3, 1]
    for copy in sent:
        copy.wait_send()


def make_grads(own, other, raw, gain, rope):
    vmem = pl.BlockSpec(memory_space=pltpu.VMEM)
    return pl.pallas_call(
        grads_kernel,
        out_shape=(
            jax.ShapeDtypeStruct((2, 4, 4, 4, PIECE, PAD), BF16),
            jax.ShapeDtypeStruct((8, LATENT), F32),
        ),
        in_specs=[vmem, vmem, vmem, vmem, vmem],
        out_specs=(vmem, vmem),
        scratch_shapes=[
            pltpu.VMEM((4, 4, 4, PIECE, PAD), F32),
            pltpu.VMEM((4, 4, 4, PIECE, PAD), BF16),
            pltpu.VMEM((4, 4, 4, PIECE, PAD), BF16),
            pltpu.VMEM((2, 2, 4, PIECE, PAD), BF16),
            pltpu.VMEM((2, 4, 4, PIECE, PAD), BF16),
            pltpu.VMEM((3, 4, PIECE, PAD), F32),
            pltpu.VMEM((3, PIECE, PAD), F32),
            pltpu.VMEM((4, 8, LATENT), F32),
            pltpu.VMEM((4, 4, 8, LATENT), F32),
            pltpu.SemaphoreType.DMA((43,)),
            pltpu.SemaphoreType.DMA((43,)),
        ],
        compiler_params=pltpu.CompilerParams(
            collective_id=1, has_side_effects=True, vmem_limit_bytes=48 * 2**20
        ),
    )(own, other, raw, gain, rope)


def last_kernel(pieces, hidden, kv_down, hidden_grad, down_grad, rows):
    ctx = lax.axis_index("ctx")

    def place_piece(index, carry):
        for core in range(2):
            slot, quarter = piece_slot(core, *split_piece(index))
            at = pl.multiple_of(slot * SPAN + quarter * PIECE, PIECE)
            rows[pl.ds(at, PIECE), :] = pieces[core * 64 + index]
        return carry

    lax.fori_loop(0, 64, place_piece, 0, unroll=4)
    mine = rows[pl.ds(pl.multiple_of(ctx * 128, 128), 128), :WIDTH]
    hidden_grad[...] = nt_dot(mine, kv_down[...]).astype(BF16)
    for k in range(7):
        part = pl.ds(k * 128, 128)
        down_grad[part, :] = lax.dot_general(
            hidden[:, part], rows[:, :WIDTH], (((0,), (0,)), ((), ())), preferred_element_type=F32
        )


def finish(pieces, hidden_all, kv_down):
    vmem = pl.BlockSpec(memory_space=pltpu.VMEM)
    return pl.pallas_call(
        last_kernel,
        out_shape=(
            jax.ShapeDtypeStruct((128, 896), BF16),
            jax.ShapeDtypeStruct((896, WIDTH), F32),
        ),
        in_specs=[vmem, vmem, vmem],
        out_specs=(vmem, vmem),
        scratch_shapes=[pltpu.VMEM((TOKENS, PAD), BF16)],
        compiler_params=pltpu.CompilerParams(vmem_limit_bytes=48 * 2**20),
    )(pieces, hidden_all, kv_down)


def per_device(table, hidden, kv_down, kv_gain, queries, out_grad, span_table):
    gain = kv_gain.reshape(1, LATENT)
    ctx, head = lax.axis_index("ctx"), lax.axis_index("head")
    first = span_table[2 * ctx + head // 4] * SPAN + (head % 4) * PIECE
    rope = lax.dynamic_slice_in_dim(table, first, PIECE, 0)
    hidden_all = lax.all_gather(hidden, "ctx", axis=0, tiled=True)
    key_pieces, raw = make_keys(hidden, kv_down, gain, rope)
    rows = queries.shape[0] * queries.shape[1]
    query_grad, own, other = attend(
        key_pieces.reshape(128, PIECE, PAD),
        queries.reshape(rows, WIDTH),
        out_grad.reshape(rows, LATENT),
        span_table,
    )
    shape = (4, 4, 4, PIECE, PAD)
    grad_pieces, gain_grad = make_grads(own.reshape(shape), other.reshape(shape), raw, gain, rope)
    hidden_grad, down_grad = finish(grad_pieces.reshape(128, PIECE, PAD), hidden_all, kv_down)
    return (query_grad.reshape(queries.shape), hidden_grad, down_grad, gain_grad[0])


def solution(mesh):
    table = rope_rows()

    def run(hidden, kv_down, kv_gain, queries, out_grad, span_table):
        return jax.shard_map(
            per_device,
            mesh=mesh,
            in_specs=(
                P(),
                P("ctx", "head"),
                P("head", None),
                P(),
                P("ctx", "head", None),
                P("ctx", "head", None),
                P(),
            ),
            out_specs=(P("ctx", "head", None), P("ctx", "head"), P("head", None), P()),
            check_vma=False,
        )(jnp.asarray(table), hidden, kv_down, kv_gain, queries, out_grad, span_table)

    return run
```

```python
import functools
import math

import jax
import jax.numpy as jnp
import numpy as np
from jax import lax
from jax.experimental import pallas as pl
from jax.experimental.pallas import tpu as pltpu
from jax.sharding import PartitionSpec as P

MESH = pl.DeviceIdType.MESH
F32 = jnp.float32
BF16 = jnp.bfloat16
LATENT = 512
WIDTH = 576
PAD = 640
SPAN = 64
TOKENS = 2048
PIECE = 16
EPS = 1e-06
SCALE = 1.0 / math.sqrt(192.0)
KEY_BLOCK = 256
ROW_BLOCK = 1024
SUB = 512
BLOCKS = TOKENS // KEY_BLOCK


def rope_rows():
    half = (WIDTH - LATENT) // 2
    freq = np.exp(np.float32(-math.log(10000.0)) * np.arange(half, dtype=np.float32) / np.float32(half))
    angle = np.arange(TOKENS, dtype=np.float32)[:, None] * freq.astype(np.float32)[None, :]
    cos, sin = np.cos(angle.astype(np.float64)), np.sin(angle.astype(np.float64))
    none = np.zeros((TOKENS, PAD - WIDTH))
    cos_rows = np.concatenate([cos, cos, none], axis=1)
    sin_rows = np.concatenate([-sin, sin, none], axis=1)
    return np.concatenate([cos_rows, sin_rows], axis=1).astype(np.float32)


def nt_dot(left, right):
    return lax.dot_general(left, right, (((1,), (1,)), ((), ())), preferred_element_type=F32)


class Place:
    def __init__(self):
        ctx, head = lax.axis_index("ctx"), lax.axis_index("head")
        self.ctx, self.head = ctx, head
        self.core = lax.rem(ctx, 2)
        self.x = lax.div(head, 2)
        self.y = lax.rem(lax.div(ctx, 2), 2) * 2 + lax.rem(head, 2)
        self.z = lax.div(ctx, 4)
        self.own = (
            self.pick(self.x, self.y),
            self.pick(self.y, self.z),
            self.pick(self.z, self.x),
        )

    def pick(self, first, second):
        return first + self.core * (second - first)

    def device(self, x, y, z, core):
        ctx = z * 4 + lax.div(y, 2) * 2 + core
        return (ctx, x * 2 + lax.rem(y, 2))

    def shifted(self, dx, dy, dz):
        return self.device(
            lax.rem(self.x + dx, 4), lax.rem(self.y + dy, 4), lax.rem(self.z + dz, 4), self.core
        )

    def peer(self, level, d):
        one, other = d * self.core, d * (1 - self.core)
        if level == 0:
            return self.shifted(other, one, 0)
        if level == 1:
            return self.shifted(0, other, one)
        return self.shifted(one, 0, other)

    def twin(self):
        return self.device(self.x, self.y, self.z, 1 - self.core)


def remote(src, dst, send_sem, recv_sem, device):
    return pltpu.make_async_remote_copy(
        src_ref=src, dst_ref=dst, send_sem=send_sem, recv_sem=recv_sem, device_id=device, device_id_type=MESH
    )


def meet(devices):
    barrier = pltpu.get_barrier_semaphore()
    for device in devices:
        pl.semaphore_signal(barrier, inc=1, device_id=device, device_id_type=MESH)
    return lambda: pl.semaphore_wait(barrier, len(devices))


def gather_rows(place, rows, send, recv, first, each_level=None, use=None):
    core = place.core
    a1, a2, a3 = place.own
    sent = []

    def go(region, slot, device):
        copy = remote(region, region, send.at[first + slot], recv.at[first + slot], device)
        copy.start()
        sent.append(copy)
        return copy

    small = [go(rows.at[core, a3, a2, a1], d - 1, place.peer(0, d)) for d in (1, 2, 3)]
    if each_level is not None:
        each_level(0)
    for copy in small:
        copy.wait_recv()
    middle = [go(rows.at[core, a3, a2], 2 + d, place.peer(1, d)) for d in (1, 2, 3)]
    if each_level is not None:
        each_level(1)
    for copy in middle:
        copy.wait_recv()
    up, down = place.peer(2, 1), place.peer(2, 3)
    before, after, across = lax.rem(a3 + 3, 4), lax.rem(a3 + 1, 4), lax.rem(a3 + 2, 4)
    low, high = pl.ds(0, 2), pl.ds(2, 2)
    up_low = go(rows.at[core, a3, low], 6, up)
    down_high = go(rows.at[core, a3, high], 7, down)
    up_high = go(rows.at[core, a3, high], 8, up)
    down_low = go(rows.at[core, a3, low], 9, down)
    twin = place.twin()
    pairs = [go(rows.at[core, a3], 12, twin)]
    if each_level is not None:
        each_level(2)
    if use is not None:
        use(core, a3, True)
    up_low.wait_recv()
    far_low = go(rows.at[core, before, low], 10, up)
    down_high.wait_recv()
    far_high = go(rows.at[core, after, high], 11, down)
    up_high.wait_recv()
    pairs.append(go(rows.at[core, before], 13, twin))
    down_low.wait_recv()
    pairs.append(go(rows.at[core, after], 14, twin))
    if use is not None:
        twin_own = place.pick(place.x, place.z)
        twin_before, twin_after = lax.rem(twin_own + 3, 4), lax.rem(twin_own + 1, 4)
        use(core, before, False)
        use(core, after, False)
        pairs[0].wait_recv()
        use(1 - core, twin_own, False)
    far_low.wait_recv()
    pairs.append(go(rows.at[core, across, low], 15, twin))
    far_high.wait_recv()
    pairs.append(go(rows.at[core, across, high], 16, twin))
    if use is not None:
        use(core, across, False)
        pairs[1].wait_recv()
        use(1 - core, twin_before, False)
        pairs[2].wait_recv()
        use(1 - core, twin_after, False)
        pairs[3].wait_recv()
        pairs[4].wait_recv()
        use(1 - core, lax.rem(twin_own + 2, 4), False)
    else:
        for copy in pairs:
            copy.wait_recv()
    for copy in sent:
        copy.wait_send()


def swap_halves(tail):
    lane = lax.broadcasted_iota(jnp.int32, tail.shape, 1)
    return jnp.where(lane < 32, pltpu.roll(tail, 96, 1), pltpu.roll(tail, 32, 1))


def keys_kernel(hidden, kv_turned, gain, rope, rows, raw_out, part, landed, send, recv):
    place = Place()
    devices = [(place.ctx, lax.rem(place.head + d, 8)) for d in range(1, 8)]
    devices += [place.shifted(0, d, 0) for d in (1, 2, 3)]
    devices += [place.shifted(0, 0, d) for d in (1, 2, 3)]
    devices += [place.shifted(d, 0, 0) for d in (1, 2, 3)]
    devices.append(place.twin())
    met = meet(devices)
    product = nt_dot(hidden[...], kv_turned[...])
    part[:, :, :WIDTH] = product.reshape(8, PIECE, WIDTH)
    part[:, :, WIDTH:] = jnp.zeros((8, PIECE, PAD - WIDTH), F32)
    landed[place.head] = part[place.head]
    met()
    copies = []
    for d in range(1, 8):
        other = lax.rem(place.head + d, 8)
        copies.append(
            remote(part.at[other], landed.at[place.head], send.at[d - 1], recv.at[d - 1], (place.ctx, other))
        )
        copies[-1].start()
    cos, sin = rope[:, :128], rope[:, 128:]
    for copy in copies:
        copy.wait_recv()
    raw = landed[0]
    for k in range(1, 8):
        raw = raw + landed[k]
    raw_out[...] = raw
    latent, tail = raw[:, :LATENT], raw[:, LATENT:]
    inv_rms = lax.rsqrt(jnp.mean(latent * latent, axis=1, keepdims=True) + EPS)
    normed = latent * inv_rms * gain[...]
    turned = tail * cos + swap_halves(tail) * sin
    a1, a2, a3 = place.own
    rows[place.core, a3, a2, a1, :, :LATENT] = normed.astype(BF16)
    rows[place.core, a3, a2, a1, :, LATENT:] = turned.astype(BF16)
    gather_rows(place, rows, send, recv, 7)
    for copy in copies:
        copy.wait_send()


def make_keys(hidden, kv_turned, gain, rope):
    vmem = pl.BlockSpec(memory_space=pltpu.VMEM)
    return pl.pallas_call(
        keys_kernel,
        out_shape=(
            jax.ShapeDtypeStruct((2, 4, 4, 4, PIECE, PAD), BF16),
            jax.ShapeDtypeStruct((PIECE, PAD), F32),
        ),
        in_specs=[vmem, vmem, vmem, vmem],
        out_specs=(vmem, vmem),
        scratch_shapes=[
            pltpu.VMEM((8, PIECE, PAD), F32),
            pltpu.VMEM((8, PIECE, PAD), F32),
            pltpu.SemaphoreType.DMA((24,)),
            pltpu.SemaphoreType.DMA((24,)),
        ],
        compiler_params=pltpu.CompilerParams(
            collective_id=0, has_side_effects=True, vmem_limit_bytes=32 * 2**20
        ),
        cost_estimate=pl.CostEstimate(flops=132 * 10**6, bytes_accessed=40 * 2**20, transcendentals=0),
    )(hidden, kv_turned, gain, rope)


def piece_slot(core, a3, a2, a1):
    x = a1 + core * (a3 - a1)
    y = a2 + core * (a1 - a2)
    z = a3 + core * (a2 - a3)
    ctx = z * 4 + lax.div(y, 2) * 2 + core
    head = x * 2 + lax.rem(y, 2)
    return ctx * 2 + lax.div(head, 4), lax.rem(head, 4)


def split_piece(index):
    return lax.div(index, 16), lax.rem(lax.div(index, 4), 4), lax.rem(index, 4)


def attend_kernel(
    pieces,
    queries,
    grads,
    span,
    query_out,
    own_out,
    other_out,
    keys,
    keys_t,
    query_cols,
    grad_rows,
    scores,
    prob_grads,
    tops,
    masses,
    dots,
    weights,
    score_grads,
    key_total,
    query_done,
):
    ctx = lax.axis_index("ctx")
    my_core = lax.rem(ctx, 2)
    heads = queries.shape[0]
    half = heads * SPAN
    factor = SCALE * math.log2(math.e)

    def first_row(core, index):
        slot, quarter = piece_slot(core, *split_piece(index))
        return pl.multiple_of(span[slot] * SPAN + quarter * PIECE, PIECE)

    def place_piece(index, carry):
        for core in range(2):
            keys[pl.ds(first_row(core, index), PIECE), :] = pieces[core * 64 + index]
        return carry

    lax.fori_loop(0, 64, place_piece, 0, unroll=4)

    def block_rows(block):
        return pl.ds(pl.multiple_of(block * KEY_BLOCK, KEY_BLOCK), KEY_BLOCK)

    def turn_block(block, carry):
        keys_t[:, block_rows(block)] = keys[block_rows(block), :].T
        return carry

    lax.fori_loop(0, BLOCKS, turn_block, 0)

    for k in range(heads // 2):
        first, second = queries[2 * k], queries[2 * k + 1]
        at = pl.ds(k * 128, 128)
        query_cols[:, at] = jnp.concatenate([first[:, :SPAN], second[:, :SPAN]], axis=1)
        at = pl.ds(half + k * 128, 128)
        query_cols[:, at] = jnp.concatenate([first[:, SPAN:], second[:, SPAN:]], axis=1)

    to = lax.broadcasted_iota(jnp.int32, (256, 256), 0)
    at = lax.broadcasted_iota(jnp.int32, (256, 256), 1)
    swap = (lax.div(to, 16) == lax.rem(at, 16)) & (lax.rem(to, 16) == lax.div(at, 16))
    swap = jnp.where(swap, 1.0, 0.0).astype(BF16)
    for i in range(8):
        turned = jnp.dot(swap, grads[i * 256 : (i + 1) * 256, :], preferred_element_type=F32).astype(BF16)
        for h in range(heads):
            at = (i // 4) * half + h * SPAN + (i % 4) * 16
            grad_rows[at : at + 16, :] = turned[h * 16 : (h + 1) * 16, :]

    spans = [span[2 * ctx + s] for s in range(2)]
    counts = [lax.div(spans[s] * SPAN, KEY_BLOCK) + 1 for s in range(2)]
    for s in range(2):
        rows = pl.ds(s * half, half)
        for r in range(half // ROW_BLOCK):
            columns = pl.ds(s * half + r * ROW_BLOCK, ROW_BLOCK)
            local = pl.ds(r * ROW_BLOCK, ROW_BLOCK)
            tops[...] = jnp.full_like(tops, -1e30)
            masses[...] = jnp.zeros_like(masses)
            dots[...] = jnp.zeros_like(dots)

            def score_block(block, masked, s=s, columns=columns):
                here = block_rows(block)
                one = pl.ds(block, 1)
                for part in range(ROW_BLOCK // SUB):
                    at = s * half + r * ROW_BLOCK + part * SUB
                    local = pl.ds(part * SUB, SUB)
                    raw = jnp.dot(keys[here, :WIDTH], query_cols[:, at : at + SUB], preferred_element_type=F32)
                    prob_grad = nt_dot(keys[here, :LATENT], grad_rows[at : at + SUB, :])
                    if masked:
                        key_pos = block * KEY_BLOCK + lax.broadcasted_iota(jnp.int32, (KEY_BLOCK, SUB), 0)
                        token = lax.rem(lax.broadcasted_iota(jnp.int32, (1, SUB), 1), SPAN)
                        raw = jnp.where(key_pos <= spans[s] * SPAN + token, raw, -1e30)
                    top = jnp.max(raw, axis=0, keepdims=True)
                    weight = jnp.exp2((raw - top) * factor)
                    scores[here, local] = weight
                    prob_grads[here, local] = prob_grad
                    tops[one, local] = top
                    masses[one, local] = jnp.sum(weight, axis=0, keepdims=True)
                    dots[one, local] = jnp.sum(weight * prob_grad, axis=0, keepdims=True)

            def score_step(block, carry):
                score_block(block, False)
                return carry

            lax.fori_loop(0, counts[s] - 1, score_step, 0)
            score_block(counts[s] - 1, True)
            top = jnp.max(tops[...], axis=0, keepdims=True)
            level = jnp.exp2((tops[...] - top) * factor)
            share = 1.0 / jnp.sum(level * masses[...], axis=0, keepdims=True)
            delta = jnp.sum(level * dots[...], axis=0, keepdims=True) * share
            tops[...] = level * share

            def grad_step(block, carry, local=local, delta=delta):
                here = block_rows(block)
                probability = scores[here, :] * tops[pl.ds(block, 1), :]
                weights[here, local] = probability.astype(BF16)
                score_grads[here, local] = (probability * (prob_grads[here, :] - delta)).astype(BF16)
                return carry

            lax.fori_loop(0, counts[s], grad_step, 0)

        def key_rows(here, s=s, rows=rows):
            by_score = nt_dot(score_grads[here, :], query_cols[:, rows]) * SCALE
            by_value = jnp.dot(weights[here, :], grad_rows[rows, :], preferred_element_type=F32)
            latent = by_score[:, :LATENT] + by_value
            rotary = by_score[:, LATENT:]
            if s == 0:
                key_total[here, :LATENT] = latent
                key_total[here, LATENT:WIDTH] = rotary
            else:
                key_total[here, :LATENT] += latent
                key_total[here, LATENT:WIDTH] += rotary

        def key_step(pair, carry):
            key_rows(pl.ds(pl.multiple_of(pair * 2 * KEY_BLOCK, 2 * KEY_BLOCK), 2 * KEY_BLOCK))
            return carry

        if s == 0:

            def clear_step(block, carry):
                key_total[block_rows(block), :] = jnp.zeros((KEY_BLOCK, PAD), F32)
                return carry

            lax.fori_loop(0, BLOCKS, clear_step, 0)
        lax.fori_loop(0, lax.div(counts[s], 2), key_step, 0)

        @pl.when(lax.rem(counts[s], 2) == 1)
        def _(s=s):
            key_rows(block_rows(counts[s] - 1))

        for blocks in range(1, BLOCKS + 1):

            @pl.when(counts[s] == blocks)
            def _(blocks=blocks, s=s):
                for r in range(half // 512):
                    total = jnp.dot(
                        keys_t[:WIDTH, : blocks * KEY_BLOCK],
                        score_grads[: blocks * KEY_BLOCK, r * 512 : (r + 1) * 512],
                        preferred_element_type=F32,
                    )
                    query_done[:, s * half + r * 512 : s * half + (r + 1) * 512] = (total * SCALE).astype(BF16)

    for k in range(heads // 2):
        first, second = query_done[:, pl.ds(k * 128, 128)], query_done[:, pl.ds(half + k * 128, 128)]
        query_out[2 * k] = jnp.concatenate([first[:, :SPAN], second[:, :SPAN]], axis=1)
        query_out[2 * k + 1] = jnp.concatenate([first[:, SPAN:], second[:, SPAN:]], axis=1)

    def hand_out(index, carry):
        own_out[index] = key_total[pl.ds(first_row(my_core, index), PIECE), :]
        other_out[index] = key_total[pl.ds(first_row(1 - my_core, index), PIECE), :].astype(BF16)
        return carry

    lax.fori_loop(0, 64, hand_out, 0, unroll=4)


def attend(pieces, queries, grads, span_table):
    vmem = pl.BlockSpec(memory_space=pltpu.VMEM)
    smem = pl.BlockSpec(memory_space=pltpu.SMEM)
    rows = grads.shape[0]
    return pl.pallas_call(
        attend_kernel,
        out_shape=(
            jax.ShapeDtypeStruct(queries.shape, BF16),
            jax.ShapeDtypeStruct((64, PIECE, PAD), F32),
            jax.ShapeDtypeStruct((64, PIECE, PAD), BF16),
        ),
        in_specs=[vmem, vmem, vmem, smem],
        out_specs=(vmem, vmem, vmem),
        scratch_shapes=[
            pltpu.VMEM((TOKENS, PAD), BF16),
            pltpu.VMEM((PAD, TOKENS), BF16),
            pltpu.VMEM((WIDTH, rows), BF16),
            pltpu.VMEM((rows, LATENT), BF16),
            pltpu.VMEM((TOKENS, ROW_BLOCK), F32),
            pltpu.VMEM((TOKENS, ROW_BLOCK), F32),
            pltpu.VMEM((BLOCKS, ROW_BLOCK), F32),
            pltpu.VMEM((BLOCKS, ROW_BLOCK), F32),
            pltpu.VMEM((BLOCKS, ROW_BLOCK), F32),
            pltpu.VMEM((TOKENS, rows // 2), BF16),
            pltpu.VMEM((TOKENS, rows // 2), BF16),
            pltpu.VMEM((TOKENS, PAD), F32),
            pltpu.VMEM((WIDTH, rows), BF16),
        ],
        compiler_params=pltpu.CompilerParams(vmem_limit_bytes=62 * 2**20),
        cost_estimate=pl.CostEstimate(flops=23 * 10**9, bytes_accessed=20 * 2**20, transcendentals=2**22),
    )(pieces, queries, grads, span_table)


def grads_kernel(
    own,
    other,
    raw_ref,
    gain,
    rope,
    hidden_all,
    kv_turned,
    gain_out,
    hidden_grad,
    down_grad,
    rows,
    hidden_rows,
    sums,
    twin_in,
    packed,
    relay,
    halves,
    second,
    third,
    gains,
    gains_in,
    send,
    recv,
    local_sem,
):
    place = Place()
    core = place.core
    a1, a2, a3 = place.own
    devices = [place.peer(level, d) for level in range(3) for d in (1, 2, 3)]
    devices.append(place.twin())
    met = meet(devices)

    for z in range(4):
        for y in range(4):
            pltpu.make_async_copy(hidden_all.at[z, y // 2, 0, :, y % 2], hidden_rows.at[0, z, y], local_sem).start()
        for x in range(4):
            for y_hi in range(2):
                pltpu.make_async_copy(
                    hidden_all.at[z, y_hi, 1, x], hidden_rows.at[1, x, z, pl.ds(2 * y_hi, 2)], local_sem
                ).start()
    met()
    sent = []

    def go(src, dst, slot, device):
        copy = remote(src, dst, send.at[slot], recv.at[slot], device)
        copy.start()
        sent.append(copy)
        return copy

    order = [lax.rem(a3 + d, 4) for d in (2, 1, 3, 0)]
    twin_own = place.pick(place.x, place.z)
    twin_order = [lax.rem(twin_own + d, 4) for d in (2, 1, 3, 0)]
    pairs = [go(other.at[target], twin_in.at[target], k, place.twin()) for k, target in enumerate(twin_order)]

    def add_twin(target):
        def body(index, carry):
            at2, at1 = lax.div(index, 4), lax.rem(index, 4)
            total = own[target, at2, at1] + twin_in[target, at2, at1].astype(F32)
            sums[target, at2, at1] = total
            packed[target, at2, at1] = total.astype(BF16)
            return carry

        lax.fori_loop(0, 16, body, 0, unroll=4)

    def add_relay(target, side, low):
        def body(index, carry):
            at2, at1 = lax.div(index, 4), lax.rem(index, 4)
            total = sums[target, low + at2, at1] + relay[side, at2, at1].astype(F32)
            packed[target, low + at2, at1] = total.astype(BF16)
            return carry

        lax.fori_loop(0, 8, body, 0, unroll=4)

    up, down = place.peer(2, 1), place.peer(2, 3)
    across, after, before = order[0], order[1], order[2]
    low, high = pl.ds(0, 2), pl.ds(2, 2)
    pairs[0].wait_recv()
    add_twin(across)
    up_relay = go(packed.at[across, low], relay.at[0], 4, up)
    down_relay = go(packed.at[across, high], relay.at[1], 5, down)
    pairs[1].wait_recv()
    add_twin(after)
    up_high = go(packed.at[after, high], halves.at[0, high], 6, up)
    pairs[2].wait_recv()
    add_twin(before)
    down_low = go(packed.at[before, low], halves.at[1, low], 7, down)
    up_relay.wait_recv()
    add_relay(after, 0, 0)
    up_low = go(packed.at[after, low], halves.at[0, low], 8, up)
    down_relay.wait_recv()
    add_relay(before, 1, 2)
    down_high = go(packed.at[before, high], halves.at[1, high], 9, down)
    pairs[3].wait_recv()
    for copy in (up_high, down_low, up_low, down_high):
        copy.wait_recv()

    def add_halves(index, carry):
        at2, at1 = lax.div(index, 4), lax.rem(index, 4)
        total = own[a3, at2, at1] + twin_in[a3, at2, at1].astype(F32)
        sums[a3, at2, at1] = total + halves[0, at2, at1].astype(F32) + halves[1, at2, at1].astype(F32)
        return carry

    lax.fori_loop(0, 16, add_halves, 0, unroll=4)
    copies = [go(sums.at[a3, lax.rem(a2 + d, 4)], second.at[d - 1], 9 + d, place.peer(1, d)) for d in (1, 2, 3)]
    for copy in copies:
        copy.wait_recv()
    for k in range(4):
        sums[a3, a2, k] = sums[a3, a2, k] + second[0, k] + second[1, k] + second[2, k]
    copies = [
        go(sums.at[a3, a2, lax.rem(a1 + d, 4)], third.at[d - 1], 12 + d, place.peer(0, d)) for d in (1, 2, 3)
    ]
    cos, sin = rope[:, :128], rope[:, 128:]
    raw = raw_ref[...]
    latent = raw[:, :LATENT]
    inv_rms = lax.rsqrt(jnp.mean(latent * latent, axis=1, keepdims=True) + EPS)
    cube = inv_rms * inv_rms * inv_rms
    for copy in copies:
        copy.wait_recv()
    key_grad = sums[a3, a2, a1] + third[0] + third[1] + third[2]
    latent_grad, tail = key_grad[:, :LATENT], key_grad[:, LATENT:]
    scaled = latent_grad * gain[...]
    latent_back = inv_rms * scaled - latent * cube * jnp.mean(scaled * latent, axis=1, keepdims=True)
    rope_back = tail * cos - swap_halves(tail) * sin
    rows[core, a3, a2, a1, :, :LATENT] = latent_back.astype(BF16)
    rows[core, a3, a2, a1, :, LATENT:] = rope_back.astype(BF16)
    term = jnp.sum(latent_grad * latent * inv_rms, axis=0, keepdims=True)

    state = {"total": jnp.broadcast_to(term, (8, LATENT)), "copies": None}

    def add_level(level):
        for copy in state["copies"]:
            copy.wait_recv()
        total = gains_in[level, 0]
        for k in range(1, 4):
            total = total + gains_in[level, k]
        state["total"] = total

    def gain_level(level):
        if level > 0:
            add_level(level - 1)
        gains[level] = state["total"]
        gains_in[level, place.own[level]] = state["total"]
        state["copies"] = [
            go(gains.at[level], gains_in.at[level, place.own[level]], 32 + level * 3 + d, place.peer(level, d))
            for d in (1, 2, 3)
        ]
        if level == 2:
            pltpu.make_async_copy(hidden_rows, hidden_rows, local_sem).wait()

    def use(owner, plane, first):
        turned = rows[owner, plane].reshape(256, PAD).T
        term = jnp.dot(turned[:WIDTH], hidden_rows[owner, plane].reshape(256, -1), preferred_element_type=F32)
        if first:
            down_grad[...] = term
        else:
            down_grad[...] += term

    gather_rows(place, rows, send, recv, 16, gain_level, use)
    add_level(2)
    gains[3] = state["total"]
    gains_in[3, core] = state["total"]
    last = go(gains.at[3], gains_in.at[3, core], 42, place.twin())

    mine = []
    for head in range(8):
        x, y = head // 2, lax.div(place.y, 2) * 2 + head % 2
        mine.append(rows[core, place.pick(place.z, x), place.pick(y, place.z), place.pick(x, y)])
    mine = jnp.concatenate(mine, axis=0)
    hidden_grad[...] = jnp.dot(mine[:, :WIDTH], kv_turned[...], preferred_element_type=F32).astype(BF16)
    last.wait_recv()
    gain_out[...] = (gains_in[3, 0] + gains_in[3, 1])[:1]
    for copy in sent:
        copy.wait_send()


def make_grads(own, other, raw, gain, rope, hidden_all, kv_turned):
    vmem = pl.BlockSpec(memory_space=pltpu.VMEM)
    width = hidden_all.shape[-1]
    return pl.pallas_call(
        grads_kernel,
        out_shape=(
            jax.ShapeDtypeStruct((1, LATENT), F32),
            jax.ShapeDtypeStruct((128, width), BF16),
            jax.ShapeDtypeStruct((WIDTH, width), F32),
        ),
        in_specs=[vmem, vmem, vmem, vmem, vmem, pl.BlockSpec(memory_space=pl.ANY), vmem],
        out_specs=(vmem, vmem, vmem),
        scratch_shapes=[
            pltpu.VMEM((2, 4, 4, 4, PIECE, PAD), BF16),
            pltpu.VMEM((2, 4, 4, 4, PIECE, width), BF16),
            pltpu.VMEM((4, 4, 4, PIECE, PAD), F32),
            pltpu.VMEM((4, 4, 4, PIECE, PAD), BF16),
            pltpu.VMEM((4, 4, 4, PIECE, PAD), BF16),
            pltpu.VMEM((2, 2, 4, PIECE, PAD), BF16),
            pltpu.VMEM((2, 4, 4, PIECE, PAD), BF16),
            pltpu.VMEM((3, 4, PIECE, PAD), F32),
            pltpu.VMEM((3, PIECE, PAD), F32),
            pltpu.VMEM((4, 8, LATENT), F32),
            pltpu.VMEM((4, 4, 8, LATENT), F32),
            pltpu.SemaphoreType.DMA((43,)),
            pltpu.SemaphoreType.DMA((43,)),
            pltpu.SemaphoreType.DMA,
        ],
        compiler_params=pltpu.CompilerParams(
            collective_id=1, has_side_effects=True, vmem_limit_bytes=48 * 2**20
        ),
    )(own, other, raw, gain, rope, hidden_all, kv_turned)


def per_device(table, hidden, kv_down, kv_gain, queries, out_grad, span_table):
    gain = kv_gain.reshape(1, LATENT)
    kv_turned = kv_down.T
    ctx, head = lax.axis_index("ctx"), lax.axis_index("head")
    first = span_table[2 * ctx + head // 4] * SPAN + (head % 4) * PIECE
    rope = lax.dynamic_slice_in_dim(table, first, PIECE, 0)
    hidden_all = lax.all_gather(hidden, "ctx", axis=0, tiled=True)
    key_pieces, raw = make_keys(hidden, kv_turned, gain, rope)
    rows = queries.shape[0] * queries.shape[1]
    query_grad, own, other = attend(
        key_pieces.reshape(128, PIECE, PAD),
        queries.transpose(1, 2, 0),
        out_grad.reshape(rows, LATENT),
        span_table,
    )
    shape = (4, 4, 4, PIECE, PAD)
    gain_grad, hidden_grad, down_grad = make_grads(
        own.reshape(shape),
        other.reshape(shape),
        raw,
        gain,
        rope,
        hidden_all.reshape(4, 2, 2, 4, 2, PIECE, hidden.shape[1]),
        kv_turned,
    )
    return (query_grad.transpose(2, 0, 1), hidden_grad, down_grad.T, gain_grad[0])


def solution(mesh):
    table = rope_rows()

    def run(hidden, kv_down, kv_gain, queries, out_grad, span_table):
        return jax.shard_map(
            per_device,
            mesh=mesh,
            in_specs=(
                P(),
                P("ctx", "head"),
                P("head", None),
                P(),
                P("ctx", "head", None),
                P("ctx", "head", None),
                P(),
            ),
            out_specs=(P("ctx", "head", None), P("ctx", "head"), P("head", None), P()),
            check_vma=False,
        )(jnp.asarray(table), hidden, kv_down, kv_gain, queries, out_grad, span_table)

    return run
```

```python
import functools
import math

import jax
import jax.numpy as jnp
import numpy as np
from jax import lax
from jax.experimental import pallas as pl
from jax.experimental.pallas import tpu as pltpu
from jax.sharding import PartitionSpec as P

MESH = pl.DeviceIdType.MESH
F32 = jnp.float32
BF16 = jnp.bfloat16
LATENT = 512
WIDTH = 576
PAD = 640
SPAN = 64
TOKENS = 2048
PIECE = 16
HEADS = 16
ROWS = 2048
MODEL = 896
EPS = 1e-06
SCALE = 1.0 / math.sqrt(192.0)
FACTOR = SCALE * math.log2(math.e)
BLOCK = 256
BLOCKS = TOKENS // BLOCK
HALF = ROWS // 2
SUB = 512


def rope_rows():
    half = (WIDTH - LATENT) // 2
    freq = np.exp(np.float32(-math.log(10000.0)) * np.arange(half, dtype=np.float32) / np.float32(half))
    angle = np.arange(TOKENS, dtype=np.float32)[:, None] * freq.astype(np.float32)[None, :]
    cos, sin = np.cos(angle.astype(np.float64)), np.sin(angle.astype(np.float64))
    none = np.zeros((TOKENS, PAD - WIDTH))
    cos_rows = np.concatenate([cos, cos, none], axis=1)
    sin_rows = np.concatenate([-sin, sin, none], axis=1)
    return np.concatenate([cos_rows, sin_rows], axis=1).astype(np.float32)


def nt_dot(left, right):
    return lax.dot_general(left, right, (((1,), (1,)), ((), ())), preferred_element_type=F32)


def rem4(value):
    return lax.rem(value, 4)


class Place:
    def __init__(self):
        ctx, head = lax.axis_index("ctx"), lax.axis_index("head")
        self.ctx, self.head = ctx, head
        self.core = lax.rem(ctx, 2)
        self.x = lax.div(head, 2)
        self.y_lo = lax.rem(head, 2)
        self.y_hi = lax.rem(lax.div(ctx, 2), 2)
        self.y = self.y_hi * 2 + self.y_lo
        self.z = lax.div(ctx, 4)
        self.a1 = self.pick(self.x, self.y)
        self.a2 = self.pick(self.y, self.z)
        self.a3 = self.pick(self.z, self.x)
        self.twin_a3 = self.pick(self.x, self.z)

    def pick(self, first, second):
        return first + self.core * (second - first)

    def device(self, x, y, z, core):
        return (z * 4 + lax.div(y, 2) * 2 + core, x * 2 + lax.rem(y, 2))

    def shifted(self, dx, dy, dz):
        return self.device(rem4(self.x + dx), rem4(self.y + dy), rem4(self.z + dz), self.core)

    def in_plane(self, d2, d1):
        return self.shifted(d1 * (1 - self.core), self.pick(d2, d1), d2 * self.core)

    def across(self, d3):
        return self.shifted(d3 * self.core, 0, d3 * (1 - self.core))

    def beside(self, d):
        return self.shifted(d * self.core, self.pick(2, 5 - 2 * self.y_lo), d * (1 - self.core))

    def twin(self):
        return self.device(self.x, self.y, self.z, 1 - self.core)


def remote(src, dst, send_sem, recv_sem, device):
    return pltpu.make_async_remote_copy(
        src_ref=src, dst_ref=dst, send_sem=send_sem, recv_sem=recv_sem, device_id=device, device_id_type=MESH
    )


def swap_halves(tail):
    lane = lax.broadcasted_iota(jnp.int32, tail.shape, 1)
    return jnp.where(lane < 32, pltpu.roll(tail, 96, 1), pltpu.roll(tail, 32, 1))


def block_rows(block):
    return pl.ds(pl.multiple_of(block * BLOCK, BLOCK), BLOCK)


PLANE_SHIFTS = [(d2, d1) for d2 in range(4) for d1 in range(4) if d2 or d1]

SUM_RAW = 0
KEYS_PLANE = 7
KEYS_ACROSS = 22
KEYS_TWIN = 25
HIDDEN = 29
HIDDEN_TWIN = 36
GRADS_TWIN = 37
GRADS_ACROSS = 41
GRADS_PLANE = 44
ROWS_PLANE = 59
ROWS_ACROSS = 74
ROWS_TWIN = 77
GAIN_PLANE = 81
GAIN_ACROSS = 96
GAIN_TWIN = 99
SEMAPHORES = 100


def whole_kernel(
    hidden,
    kv_turned,
    gain,
    rope,
    queries,
    grads,
    span,
    query_out,
    gain_out,
    hidden_grad,
    down_grad,
    hidden_all,
    part,
    landed,
    raw_rows,
    rows,
    keys_t,
    query_cols,
    grad_rows,
    bias,
    scores,
    prob_grads,
    tops,
    masses,
    dots,
    weights,
    score_grads,
    key_total,
    twin_in,
    packed,
    from_across,
    from_plane,
    back_rows,
    gains,
    gain_plane,
    gain_across,
    gain_twin,
    send,
    recv,
    local,
):
    place = Place()
    core, a1, a2, a3 = place.core, place.a1, place.a2, place.a3
    twin = place.twin()
    devices = [place.in_plane(d2, d1) for d2, d1 in PLANE_SHIFTS]
    devices += [place.across(d) for d in (1, 2, 3)] + [place.beside(d) for d in (1, 2, 3)] + [twin]
    barrier = pltpu.get_barrier_semaphore()
    for device in devices:
        pl.semaphore_signal(barrier, inc=1, device_id=device, device_id_type=MESH)

    sent = []

    def copy_of(src, dst, slot, device):
        return remote(src, dst, send.at[slot], recv.at[slot], device)

    def go(src, dst, slot, device):
        copy = copy_of(src, dst, slot, device)
        copy.start()
        sent.append(copy)
        return copy

    def later(src, dst, slot, device):
        copy = copy_of(src, dst, slot, device)
        sent.append(copy)
        return copy

    fetched = [
        pltpu.make_async_copy(queries.at[h], query_cols.at[:, pl.ds(h * 128, 128)], local.at[0]) for h in range(HEADS)
    ]
    for copy in fetched:
        copy.start()
    raw_grads = score_grads.at[:, pl.ds(0, LATENT)]
    grads_fetch = pltpu.make_async_copy(grads, raw_grads, local.at[1])
    grads_fetch.start()
    own_hidden = hidden_all.at[place.z, place.y_hi, core]
    hidden_own_copy = pltpu.make_async_copy(hidden, own_hidden, local.at[2])
    hidden_own_copy.start()

    product = nt_dot(hidden[...].reshape(128, MODEL), kv_turned[...])
    part[:, :, :WIDTH] = product.reshape(8, PIECE, WIDTH)
    part[:, :, WIDTH:] = jnp.zeros((8, PIECE, PAD - WIDTH), F32)
    landed[place.head] = part[place.head]
    pl.semaphore_wait(barrier, len(devices))
    raw_copies = []
    for d in range(1, 8):
        other = lax.rem(place.head + d, 8)
        raw_copies.append(go(part.at[other], landed.at[place.head], SUM_RAW + d - 1, (place.ctx, other)))

    token = lax.broadcasted_iota(jnp.int32, (1, 128), 1)
    query_pos = jnp.where(token < SPAN, span[2 * place.ctx] * SPAN, span[2 * place.ctx + 1] * SPAN) + lax.rem(token, SPAN)
    row = lax.broadcasted_iota(jnp.int32, (PIECE, 128), 0)

    def bias_piece(index, carry):
        at3, at2, at1 = lax.div(index, 16), rem4(lax.div(index, 4)), rem4(index)
        for owner, (x, y, z) in enumerate(((at1, at2, at3), (at3, at1, at2))):
            head = x * 2 + lax.rem(y, 2)
            slot = (z * 4 + lax.div(y, 2) * 2 + owner) * 2 + lax.div(head, 4)
            key_pos = span[slot] * SPAN + rem4(head) * PIECE + row
            at = pl.ds(pl.multiple_of((owner * 64 + index) * PIECE, PIECE), PIECE)
            bias[at, :] = jnp.where(key_pos <= query_pos, 0.0, -1e30)
        return carry

    lax.fori_loop(0, 64, bias_piece, 0)
    to = lax.broadcasted_iota(jnp.int32, (256, 256), 0)
    at = lax.broadcasted_iota(jnp.int32, (256, 256), 1)
    swap = (lax.div(to, 16) == lax.rem(at, 16)) & (lax.rem(to, 16) == lax.div(at, 16))
    swap = jnp.where(swap, 1.0, 0.0).astype(BF16)
    grads_fetch.wait()

    def order_grads(index, carry):
        here = pl.ds(pl.multiple_of(index * 256, 256), 256)
        turned = jnp.dot(swap, score_grads[here, :LATENT], preferred_element_type=F32).astype(BF16)
        for h in range(HEADS):
            to_rows = pl.ds(pl.multiple_of(h * 128 + index * 16, 16), 16)
            grad_rows[to_rows, :] = turned[h * 16 : (h + 1) * 16, :]
        return carry

    lax.fori_loop(0, 8, order_grads, 0)

    for copy in raw_copies:
        copy.wait_recv()
    raw = landed[0]
    for k in range(1, 8):
        raw = raw + landed[k]
    raw_rows[...] = raw
    latent, tail = raw[:, :LATENT], raw[:, LATENT:]
    inv_rms = lax.rsqrt(jnp.mean(latent * latent, axis=1, keepdims=True) + EPS)
    turned = tail * rope[:, :128] + swap_halves(tail) * rope[:, 128:]
    rows[core, a3, a2, a1, :, :LATENT] = (latent * inv_rms * gain[...]).astype(BF16)
    rows[core, a3, a2, a1, :, LATENT:] = turned.astype(BF16)

    before, after, opposite = rem4(a3 + 3), rem4(a3 + 1), rem4(a3 + 2)
    twin_a3 = place.twin_a3
    own_planes = [a3, before, after, opposite]
    twin_planes = [twin_a3, rem4(twin_a3 + 3), rem4(twin_a3 + 1), rem4(twin_a3 + 2)]

    def spread(ref, plane_sem, across_sem, twin_sem):
        piece = ref.at[core, a3, a2, a1]
        copies = [go(piece, piece, plane_sem + k, place.in_plane(*d)) for k, d in enumerate(PLANE_SHIFTS)]

        def rest():
            for copy in copies:
                copy.wait_recv()
            plane = ref.at[core, a3]
            across = {d: go(plane, plane, across_sem + d - 1, place.across(d)) for d in (1, 3, 2)}
            pairs = [go(plane, plane, twin_sem, twin)]
            for k in (1, 2, 3):
                plane = ref.at[core, own_planes[k]]
                pairs.append(later(plane, plane, twin_sem + k, twin))

            def arrive(step):
                if step == 1:
                    pairs[0].wait_recv()
                if step in (2, 3, 6):
                    k = {2: 1, 3: 2, 6: 3}[step]
                    across[{1: 1, 2: 3, 3: 2}[k]].wait_recv()
                    pairs[k].start()
                if step in (4, 5, 7):
                    pairs[{4: 1, 5: 2, 7: 3}[step]].wait_recv()

            return arrive

        return rest

    def plane_of(step):
        by_step = [(0, 0), (1, 0), (0, 3), (0, 1), (1, 3), (1, 1), (0, 2), (1, 2)]
        owner, shift = 0, 0
        for k, (twins, d) in enumerate(by_step):
            here = jnp.where(step == k, 1, 0)
            owner, shift = owner + here * twins, shift + here * d
        base = a3 + owner * (twin_a3 - a3)
        return core + owner * (1 - 2 * core), rem4(base + shift)

    arrive = spread(rows, KEYS_PLANE, KEYS_ACROSS, KEYS_TWIN)()
    for copy in fetched:
        copy.wait()

    def score_block(owner, plane, half):
        block = owner * 4 + plane
        here, one = block_rows(block), pl.ds(block, 1)
        keys = rows[owner, plane].reshape(BLOCK, PAD)
        seen = bias[here, :]
        seen = jnp.concatenate([seen] * (SUB // 128), axis=1)
        for k in range(HALF // SUB):
            first = half * HALF + k * SUB
            at = pl.ds(k * SUB, SUB)
            score = jnp.dot(keys[:, :WIDTH], query_cols[:, first : first + SUB], preferred_element_type=F32) + seen
            prob_grad = nt_dot(keys[:, :LATENT], grad_rows[first : first + SUB, :])
            top = jnp.max(score, axis=0, keepdims=True)
            weight = jnp.exp2((score - top) * FACTOR)
            scores[here, at] = weight
            prob_grads[here, at] = prob_grad
            tops[one, at] = top
            masses[one, at] = jnp.sum(weight, axis=0, keepdims=True)
            dots[one, at] = jnp.sum(weight * prob_grad, axis=0, keepdims=True)

    def finish_half(half):
        top = jnp.max(tops[...], axis=0, keepdims=True)
        level = jnp.exp2((tops[...] - top) * FACTOR)
        share = 1.0 / jnp.sum(level * masses[...], axis=0, keepdims=True)
        delta = jnp.sum(level * dots[...], axis=0, keepdims=True) * share
        tops[...] = level * share
        dots[...] = jnp.broadcast_to(delta, dots.shape)

        def grad_step(block, carry):
            here = block_rows(block)
            probability = scores[here, :] * tops[pl.ds(block, 1), :]
            weights[lax.div(block, 4), rem4(block)] = probability.astype(BF16).reshape(4, 4, PIECE, HALF)
            score_grad = probability * (prob_grads[here, :] - dots[pl.ds(0, 1), :])
            score_grads[here, half * HALF : (half + 1) * HALF] = score_grad.astype(BF16)
            return carry

        lax.fori_loop(0, BLOCKS, grad_step, 0)

    def key_terms(owner, plane, half):
        columns = slice(half * HALF, (half + 1) * HALF)
        here = block_rows(owner * 4 + plane)
        by_score = nt_dot(score_grads[here, columns], query_cols[:, columns]) * SCALE
        by_value = jnp.dot(
            weights[owner, plane].reshape(BLOCK, HALF), grad_rows[columns, :], preferred_element_type=F32
        )
        return by_score[:, :LATENT] + by_value, by_score[:, LATENT:]

    def first_score_step(step, carry):
        for k in range(1, 8):

            @pl.when(step == k)
            def _(k=k):
                arrive(k)

        owner, plane = plane_of(step)
        keys_t[:, block_rows(owner * 4 + plane)] = rows[owner, plane].reshape(BLOCK, PAD).T
        score_block(owner, plane, 0)
        return carry

    lax.fori_loop(0, BLOCKS, first_score_step, 0)

    hidden_own_copy.wait()
    hidden_copies = []
    for k in range(7):
        dz, flip = (k + 1) // 2, (k + 1) % 2
        device = place.shifted(0, 2 * flip, dz)
        hidden_copies.append(go(own_hidden, own_hidden, HIDDEN + k, device))

    finish_half(0)

    def first_key_step(block, carry):
        owner, plane = lax.div(block, 4), rem4(block)
        latent_term, rope_term = key_terms(owner, plane, 0)
        key_total[owner, plane, :, :, :, :LATENT] = latent_term.reshape(4, 4, PIECE, LATENT)
        key_total[owner, plane, :, :, :, LATENT:WIDTH] = rope_term.reshape(4, 4, PIECE, WIDTH - LATENT)
        key_total[owner, plane, :, :, :, WIDTH:] = jnp.zeros((4, 4, PIECE, PAD - WIDTH), F32)
        return carry

    lax.fori_loop(0, BLOCKS, first_key_step, 0)

    def second_score_step(block, carry):
        score_block(lax.div(block, 4), rem4(block), 1)
        return carry

    lax.fori_loop(0, BLOCKS, second_score_step, 0)
    finish_half(1)

    for copy in hidden_copies:
        copy.wait_recv()
    hidden_to_twin = go(hidden_all.at[:, :, core], hidden_all.at[:, :, core], HIDDEN_TWIN, twin)

    def second_key(owner, plane):
        latent_term, rope_term = key_terms(owner, plane, 1)
        key_total[owner, plane, :, :, :, :LATENT] += latent_term.reshape(4, 4, PIECE, LATENT)
        key_total[owner, plane, :, :, :, LATENT:WIDTH] += rope_term.reshape(4, 4, PIECE, WIDTH - LATENT)

    shifts = [2, 1, 3, 0]
    pairs = []
    for k, d in enumerate(shifts):
        plane = rem4(twin_a3 + d)
        pairs.append(later(key_total.at[1 - core, plane], twin_in.at[plane], GRADS_TWIN + k, twin))

    def twin_key_step(step, carry):
        shift = jnp.where(step == 0, 2, jnp.where(step == 3, 0, 2 * step - 1))
        second_key(1 - core, rem4(twin_a3 + shift))
        for k in range(4):

            @pl.when(step == k)
            def _(k=k):
                pairs[k].start()

        return carry

    lax.fori_loop(0, 4, twin_key_step, 0)
    across = []
    for k, d in enumerate(shifts[:3]):
        across.append(later(packed.at[k], from_across.at[k], GRADS_ACROSS + k, place.across(d)))

    def own_key_step(step, carry):
        shift = jnp.where(step == 0, 2, jnp.where(step == 3, 0, 2 * step - 1))
        plane = rem4(a3 + shift)
        second_key(core, plane)
        for k in range(4):

            @pl.when(step == k)
            def _(k=k):
                pairs[k].wait_recv()

        for at2 in range(4):
            total = key_total[core, plane, at2] + twin_in[plane, at2]
            key_total[core, plane, at2] = total
            packed[step, at2] = total.astype(BF16)
        for k in range(3):

            @pl.when(step == k)
            def _(k=k):
                across[k].start()

        return carry

    lax.fori_loop(0, 4, own_key_step, 0)

    query_copies = []
    for k in range(4):
        columns = slice(k * SUB, (k + 1) * SUB)
        total = jnp.dot(keys_t[:WIDTH, :], score_grads[:, columns], preferred_element_type=F32)
        query_cols[:, columns] = (total * SCALE).astype(BF16)
        for h in range(4 * k, 4 * k + 4):
            copy = pltpu.make_async_copy(query_cols.at[:, pl.ds(h * 128, 128)], query_out.at[h], local.at[3])
            copy.start()
            query_copies.append(copy)

    hidden_to_twin.wait_recv()
    hidden_rows = weights
    width = pl.ds(0, MODEL)
    moved = []
    for z in range(4):
        for y in range(4):
            moved.append((hidden_all.at[z, y // 2, 0, :, y % 2], hidden_rows.at[0, z, y, :, :, width]))
        for x in range(4):
            for y_hi in range(2):
                to = hidden_rows.at[1, x, z, pl.ds(2 * y_hi, 2), :, width]
                moved.append((hidden_all.at[z, y_hi, 1, x], to))
    moved = [pltpu.make_async_copy(src, dst, local.at[4]) for src, dst in moved]
    for copy in moved:
        copy.start()

    for copy in across:
        copy.wait_recv()

    def add_across(at2, carry):
        total = key_total[core, a3, at2]
        for k in range(3):
            total = total + from_across[k, at2].astype(F32)
        key_total[core, a3, at2] = total
        return carry

    lax.fori_loop(0, 4, add_across, 0)
    plane_copies = []
    for k, (d2, d1) in enumerate(PLANE_SHIFTS):
        src = key_total.at[core, a3, rem4(a2 + d2), rem4(a1 + d1)]
        plane_copies.append(go(src, from_plane.at[k], GRADS_PLANE + k, place.in_plane(d2, d1)))
    raw = raw_rows[...]
    latent = raw[:, :LATENT]
    inv_rms = lax.rsqrt(jnp.mean(latent * latent, axis=1, keepdims=True) + EPS)
    cube = inv_rms * inv_rms * inv_rms
    for copy in plane_copies:
        copy.wait_recv()
    key_grad = key_total[core, a3, a2, a1]
    for k in range(15):
        key_grad = key_grad + from_plane[k]
    latent_grad, tail = key_grad[:, :LATENT], key_grad[:, LATENT:]
    scaled = latent_grad * gain[...]
    latent_back = inv_rms * scaled - latent * cube * jnp.mean(scaled * latent, axis=1, keepdims=True)
    rope_back = tail * rope[:, :128] - swap_halves(tail) * rope[:, 128:]
    back_rows[core, a3, a2, a1, :, :LATENT] = latent_back.astype(BF16)
    back_rows[core, a3, a2, a1, :, LATENT:] = rope_back.astype(BF16)
    spread_rest = spread(back_rows, ROWS_PLANE, ROWS_ACROSS, ROWS_TWIN)

    term = jnp.broadcast_to(jnp.sum(latent_grad * latent * inv_rms, axis=0, keepdims=True), (8, LATENT))
    gains[0] = term
    gain_plane[a2, a1] = term
    gain_copies = [
        go(gains.at[0], gain_plane.at[a2, a1], GAIN_PLANE + k, place.in_plane(*d)) for k, d in enumerate(PLANE_SHIFTS)
    ]
    for copy in moved:
        copy.wait()
    arrive_back = spread_rest()
    for copy in gain_copies:
        copy.wait_recv()
    term = gain_plane[0, 0]
    for k in range(1, 16):
        term = term + gain_plane[k // 4, k % 4]
    gains[1] = term
    gain_across[a3] = term
    gain_copies = [go(gains.at[1], gain_across.at[a3], GAIN_ACROSS + d - 1, place.across(d)) for d in (1, 2, 3)]
    down_grad[...] = jnp.zeros_like(down_grad)

    def down_step(step, carry):
        for k in range(1, 8):

            @pl.when(step == k)
            def _(k=k):
                arrive_back(k)

        owner, plane = plane_of(step)
        turned = back_rows[owner, plane].reshape(BLOCK, PAD).T
        down_grad[...] += jnp.dot(
            turned[:WIDTH], hidden_rows[owner, plane, :, :, :, :MODEL].reshape(BLOCK, MODEL), preferred_element_type=F32
        )
        return carry

    lax.fori_loop(0, BLOCKS, down_step, 0)
    for copy in gain_copies:
        copy.wait_recv()
    term = gain_across[0] + gain_across[1] + gain_across[2] + gain_across[3]
    gains[2] = term
    gain_twin[core] = term
    last = go(gains.at[2], gain_twin.at[core], GAIN_TWIN, twin)

    mine = []
    for head in range(8):
        x, y = head // 2, place.y_hi * 2 + head % 2
        mine.append(back_rows[core, place.pick(place.z, x), place.pick(y, place.z), place.pick(x, y)])
    mine = jnp.concatenate(mine, axis=0)
    hidden_grad[...] = jnp.dot(mine[:, :WIDTH], kv_turned[...], preferred_element_type=F32).astype(BF16)
    last.wait_recv()
    gain_out[...] = (gain_twin[0] + gain_twin[1])[:1]
    for copy in query_copies:
        copy.wait()
    for copy in sent:
        copy.wait_send()


def whole(hidden, kv_turned, gain, rope, queries, grads, span_table):
    vmem = pl.BlockSpec(memory_space=pltpu.VMEM)
    smem = pl.BlockSpec(memory_space=pltpu.SMEM)
    anywhere = pl.BlockSpec(memory_space=pl.ANY)
    pieces = (2, 4, 4, 4, PIECE)
    return pl.pallas_call(
        whole_kernel,
        out_shape=(
            jax.ShapeDtypeStruct((HEADS, WIDTH, 128), BF16),
            jax.ShapeDtypeStruct((1, LATENT), F32),
            jax.ShapeDtypeStruct((128, MODEL), BF16),
            jax.ShapeDtypeStruct((WIDTH, MODEL), F32),
            jax.ShapeDtypeStruct((4, 2, 2, 4, 2, PIECE, MODEL), BF16),
        ),
        in_specs=[vmem, vmem, vmem, vmem, anywhere, anywhere, smem],
        out_specs=(anywhere, vmem, vmem, vmem, anywhere),
        scratch_shapes=[
            pltpu.VMEM((8, PIECE, PAD), F32),
            pltpu.VMEM((8, PIECE, PAD), F32),
            pltpu.VMEM((PIECE, PAD), F32),
            pltpu.VMEM(pieces + (PAD,), BF16),
            pltpu.VMEM((PAD, TOKENS), BF16),
            pltpu.VMEM((WIDTH, ROWS), BF16),
            pltpu.VMEM((ROWS, LATENT), BF16),
            pltpu.VMEM((TOKENS, 128), F32),
            pltpu.VMEM((TOKENS, HALF), F32),
            pltpu.VMEM((TOKENS, HALF), F32),
            pltpu.VMEM((BLOCKS, HALF), F32),
            pltpu.VMEM((BLOCKS, HALF), F32),
            pltpu.VMEM((BLOCKS, HALF), F32),
            pltpu.VMEM(pieces + (HALF,), BF16),
            pltpu.VMEM((TOKENS, ROWS), BF16),
            pltpu.VMEM(pieces + (PAD,), F32),
            pltpu.VMEM(pieces[1:] + (PAD,), F32),
            pltpu.VMEM((4, 4, 4, PIECE, PAD), BF16),
            pltpu.VMEM((3, 4, 4, PIECE, PAD), BF16),
            pltpu.VMEM((15, PIECE, PAD), F32),
            pltpu.VMEM(pieces + (PAD,), BF16),
            pltpu.VMEM((3, 8, LATENT), F32),
            pltpu.VMEM((4, 4, 8, LATENT), F32),
            pltpu.VMEM((4, 8, LATENT), F32),
            pltpu.VMEM((2, 8, LATENT), F32),
            pltpu.SemaphoreType.DMA((SEMAPHORES,)),
            pltpu.SemaphoreType.DMA((SEMAPHORES,)),
            pltpu.SemaphoreType.DMA((5,)),
        ],
        compiler_params=pltpu.CompilerParams(
            collective_id=0, has_side_effects=True, vmem_limit_bytes=63 * 2**20
        ),
    )(hidden, kv_turned, gain, rope, queries, grads, span_table)


def per_device(table, hidden, kv_down, kv_gain, queries, out_grad, span_table):
    ctx, head = lax.axis_index("ctx"), lax.axis_index("head")
    first = span_table[2 * ctx + head // 4] * SPAN + (head % 4) * PIECE
    rope = lax.dynamic_slice_in_dim(table, first, PIECE, 0)
    query_grad, gain_grad, hidden_grad, down_grad, _ = whole(
        hidden.reshape(4, 2, PIECE, MODEL),
        kv_down.T,
        kv_gain.reshape(1, LATENT),
        rope,
        queries.transpose(1, 2, 0),
        out_grad.reshape(ROWS, LATENT),
        span_table,
    )
    return (query_grad.transpose(2, 0, 1), hidden_grad, down_grad.T, gain_grad[0])


def solution(mesh):
    table = rope_rows()

    def run(hidden, kv_down, kv_gain, queries, out_grad, span_table):
        return jax.shard_map(
            per_device,
            mesh=mesh,
            in_specs=(
                P(),
                P("ctx", "head"),
                P("head", None),
                P(),
                P("ctx", "head", None),
                P("ctx", "head", None),
                P(),
            ),
            out_specs=(P("ctx", "head", None), P("ctx", "head"), P("head", None), P()),
            check_vma=False,
        )(jnp.asarray(table), hidden, kv_down, kv_gain, queries, out_grad, span_table)

    return run
```

```python
import functools
import math

import jax
import jax.numpy as jnp
import numpy as np
from jax import lax
from jax.experimental import pallas as pl
from jax.experimental.pallas import tpu as pltpu
from jax.sharding import PartitionSpec as P

MESH = pl.DeviceIdType.MESH
F32 = jnp.float32
BF16 = jnp.bfloat16
LATENT = 512
WIDTH = 576
PAD = 640
SPAN = 64
SPANS = 32
TOKENS = 2048
PIECE = 16
HEADS = 16
ROWS = 2048
MODEL = 896
EPS = 1e-06
SCALE = 1.0 / math.sqrt(192.0)
FACTOR = SCALE * math.log2(math.e)
BLOCK = 256
BLOCKS = TOKENS // BLOCK
HALF = ROWS // 2
SUB = 512


def rope_rows():
    half = (WIDTH - LATENT) // 2
    freq = np.exp(np.float32(-math.log(10000.0)) * np.arange(half, dtype=np.float32) / np.float32(half))
    angle = np.arange(TOKENS, dtype=np.float32)[:, None] * freq.astype(np.float32)[None, :]
    cos, sin = np.cos(angle.astype(np.float64)), np.sin(angle.astype(np.float64))
    both = np.concatenate([cos, cos, -sin, sin], axis=1).astype(np.float32)
    return np.ascontiguousarray(both.reshape(SPANS, 4, PIECE, 128).transpose(1, 0, 2, 3))


def nt_dot(left, right):
    return lax.dot_general(left, right, (((1,), (1,)), ((), ())), preferred_element_type=F32)


def rem4(value):
    return lax.rem(value, 4)


class Place:
    def __init__(self):
        ctx, head = lax.axis_index("ctx"), lax.axis_index("head")
        self.ctx, self.head = ctx, head
        self.core = lax.rem(ctx, 2)
        self.x = lax.div(head, 2)
        self.y_lo = lax.rem(head, 2)
        self.y_hi = lax.rem(lax.div(ctx, 2), 2)
        self.y = self.y_hi * 2 + self.y_lo
        self.z = lax.div(ctx, 4)
        self.a1 = self.pick(self.x, self.y)
        self.a2 = self.pick(self.y, self.z)
        self.a3 = self.pick(self.z, self.x)
        self.twin_a3 = self.pick(self.x, self.z)

    def pick(self, first, second):
        return first + self.core * (second - first)

    def device(self, x, y, z, core):
        return (z * 4 + lax.div(y, 2) * 2 + core, x * 2 + lax.rem(y, 2))

    def shifted(self, dx, dy, dz):
        return self.device(rem4(self.x + dx), rem4(self.y + dy), rem4(self.z + dz), self.core)

    def in_plane(self, d2, d1):
        return self.shifted(d1 * (1 - self.core), self.pick(d2, d1), d2 * self.core)

    def across(self, d3):
        return self.shifted(d3 * self.core, 0, d3 * (1 - self.core))

    def beside(self, d):
        return self.shifted(d * self.core, self.pick(2, 5 - 2 * self.y_lo), d * (1 - self.core))

    def twin(self):
        return self.device(self.x, self.y, self.z, 1 - self.core)


def remote(src, dst, send_sem, recv_sem, device):
    return pltpu.make_async_remote_copy(
        src_ref=src, dst_ref=dst, send_sem=send_sem, recv_sem=recv_sem, device_id=device, device_id_type=MESH
    )


def swap_halves(tail):
    lane = lax.broadcasted_iota(jnp.int32, tail.shape, 1)
    return jnp.where(lane < 32, pltpu.roll(tail, 96, 1), pltpu.roll(tail, 32, 1))


def block_rows(block):
    return pl.ds(pl.multiple_of(block * BLOCK, BLOCK), BLOCK)


PLANE_SHIFTS = [(d2, d1) for d2 in range(4) for d1 in range(4) if d2 or d1]

SUM_RAW = 0
KEYS_PLANE = 7
KEYS_ACROSS = 22
KEYS_TWIN = 25
HIDDEN = 29
HIDDEN_TWIN = 36
GRADS_TWIN = 37
GRADS_ACROSS = 41
GRADS_PLANE = 44
ROWS_PLANE = 59
ROWS_ACROSS = 74
ROWS_TWIN = 77
GAIN_PLANE = 81
GAIN_ACROSS = 96
GAIN_TWIN = 99
SEMAPHORES = 100


def whole_kernel(
    hidden,
    kv_turned,
    gain,
    rope,
    queries,
    grads,
    span,
    query_out,
    gain_out,
    hidden_grad,
    down_grad,
    hidden_all,
    part,
    landed,
    raw_rows,
    rope_part,
    angles,
    rows,
    keys_t,
    query_cols,
    grad_rows,
    bias,
    scores,
    prob_grads,
    tops,
    masses,
    dots,
    weights,
    score_grads,
    key_total,
    twin_in,
    packed,
    from_near,
    from_far,
    from_plane,
    back_rows,
    gains,
    gain_plane,
    gain_across,
    gain_twin,
    send,
    recv,
    local,
):
    place = Place()
    core, a1, a2, a3 = place.core, place.a1, place.a2, place.a3
    twin = place.twin()
    devices = [place.in_plane(d2, d1) for d2, d1 in PLANE_SHIFTS]
    devices += [place.across(d) for d in (1, 2, 3)] + [place.beside(d) for d in (1, 2, 3)] + [twin]
    barrier = pltpu.get_barrier_semaphore()
    for device in devices:
        pl.semaphore_signal(barrier, inc=1, device_id=device, device_id_type=MESH)

    sent = []

    def copy_of(src, dst, slot, device):
        return remote(src, dst, send.at[slot], recv.at[slot], device)

    def go(src, dst, slot, device):
        copy = copy_of(src, dst, slot, device)
        copy.start()
        sent.append(copy)
        return copy

    def later(src, dst, slot, device):
        copy = copy_of(src, dst, slot, device)
        sent.append(copy)
        return copy

    fetched = [
        pltpu.make_async_copy(queries.at[h], query_cols.at[:, pl.ds(h * 128, 128)], local.at[0]) for h in range(HEADS)
    ]
    for copy in fetched:
        copy.start()
    raw_grads = score_grads.at[:, pl.ds(0, LATENT)]
    grads_fetch = pltpu.make_async_copy(grads, raw_grads, local.at[1])
    grads_fetch.start()
    own_hidden = hidden_all.at[place.z, place.y_hi, core]
    hidden_own_copy = pltpu.make_async_copy(hidden, own_hidden, local.at[2])
    hidden_own_copy.start()
    rope_fetch = pltpu.make_async_copy(rope.at[rem4(place.head)], rope_part, local.at[5])
    rope_fetch.start()

    product = nt_dot(hidden[...].reshape(128, MODEL), kv_turned[...])
    part[:, :, :WIDTH] = product.reshape(8, PIECE, WIDTH)
    part[:, :, WIDTH:] = jnp.zeros((8, PIECE, PAD - WIDTH), F32)
    landed[place.head] = part[place.head]
    pl.semaphore_wait(barrier, len(devices))
    raw_copies = []
    for d in range(1, 8):
        other = lax.rem(place.head + d, 8)
        raw_copies.append(go(part.at[other], landed.at[place.head], SUM_RAW + d - 1, (place.ctx, other)))

    token = lax.broadcasted_iota(jnp.int32, (1, 128), 1)
    query_pos = jnp.where(token < SPAN, span[2 * place.ctx] * SPAN, span[2 * place.ctx + 1] * SPAN) + lax.rem(token, SPAN)
    seen_from = query_pos - lax.broadcasted_iota(jnp.int32, (PIECE, 128), 0)
    starts = [span[slot] * SPAN for slot in range(SPANS)]
    for owner in range(2):
        for index in range(64):
            at3, at2, at1 = index // 16, index // 4 % 4, index % 4
            x, y, z = ((at1, at2, at3), (at3, at1, at2))[owner]
            head = x * 2 + y % 2
            start = starts[(z * 4 + y // 2 * 2 + owner) * 2 + head // 4] + head % 4 * PIECE
            bias[pl.ds((owner * 64 + index) * PIECE, PIECE), :] = jnp.where(seen_from >= start, 0.0, -1e30)
    rope_fetch.wait()
    mine = span[2 * place.ctx + lax.div(place.head, 4)]
    both = jnp.zeros((PIECE, 128), F32)
    for k in range(SPANS):
        both = jnp.where(mine == k, rope_part[k], both)
    lane = lax.broadcasted_iota(jnp.int32, (PIECE, 128), 1)
    angles[0] = jnp.where(lane < 64, both, 0.0)
    angles[1] = jnp.where(lane < 64, pltpu.roll(both, 64, 1), 0.0)
    to = lax.broadcasted_iota(jnp.int32, (256, 256), 0)
    at = lax.broadcasted_iota(jnp.int32, (256, 256), 1)
    swap = (lax.div(to, 16) == lax.rem(at, 16)) & (lax.rem(to, 16) == lax.div(at, 16))
    swap = jnp.where(swap, 1.0, 0.0).astype(BF16)
    grads_fetch.wait()

    def order_grads(index, carry):
        here = pl.ds(pl.multiple_of(index * 256, 256), 256)
        turned = jnp.dot(swap, score_grads[here, :LATENT], preferred_element_type=F32).astype(BF16)
        for h in range(HEADS):
            to_rows = pl.ds(pl.multiple_of(h * 128 + index * 16, 16), 16)
            grad_rows[to_rows, :] = turned[h * 16 : (h + 1) * 16, :]
        return carry

    lax.fori_loop(0, 8, order_grads, 0)

    for copy in raw_copies:
        copy.wait_recv()
    raw = landed[0]
    for k in range(1, 8):
        raw = raw + landed[k]
    raw_rows[...] = raw
    latent, tail = raw[:, :LATENT], raw[:, LATENT:]
    inv_rms = lax.rsqrt(jnp.mean(latent * latent, axis=1, keepdims=True) + EPS)
    turned = tail * angles[0] + swap_halves(tail) * angles[1]
    rows[core, a3, a2, a1, :, :LATENT] = (latent * inv_rms * gain[...]).astype(BF16)
    rows[core, a3, a2, a1, :, LATENT:] = turned.astype(BF16)

    before, after, opposite = rem4(a3 + 3), rem4(a3 + 1), rem4(a3 + 2)
    twin_a3 = place.twin_a3
    own_planes = [a3, before, after, opposite]
    twin_planes = [twin_a3, rem4(twin_a3 + 3), rem4(twin_a3 + 1), rem4(twin_a3 + 2)]

    def spread(ref, plane_sem, across_sem, twin_sem):
        piece = ref.at[core, a3, a2, a1]
        copies = [go(piece, piece, plane_sem + k, place.in_plane(*d)) for k, d in enumerate(PLANE_SHIFTS)]

        def rest():
            for copy in copies:
                copy.wait_recv()
            plane = ref.at[core, a3]
            across = {d: go(plane, plane, across_sem + d - 1, place.across(d)) for d in (1, 3, 2)}
            pairs = [go(plane, plane, twin_sem, twin)]
            for k in (1, 2, 3):
                plane = ref.at[core, own_planes[k]]
                pairs.append(later(plane, plane, twin_sem + k, twin))

            def arrive(step):
                if step == 1:
                    pairs[0].wait_recv()
                if step in (2, 3, 6):
                    k = {2: 1, 3: 2, 6: 3}[step]
                    across[{1: 1, 2: 3, 3: 2}[k]].wait_recv()
                    pairs[k].start()
                if step in (4, 5, 7):
                    pairs[{4: 1, 5: 2, 7: 3}[step]].wait_recv()

            return arrive

        return rest

    def plane_of(step):
        by_step = [(0, 0), (1, 0), (0, 3), (0, 1), (1, 3), (1, 1), (0, 2), (1, 2)]
        owner, shift = 0, 0
        for k, (twins, d) in enumerate(by_step):
            here = jnp.where(step == k, 1, 0)
            owner, shift = owner + here * twins, shift + here * d
        base = a3 + owner * (twin_a3 - a3)
        return core + owner * (1 - 2 * core), rem4(base + shift)

    arrive = spread(rows, KEYS_PLANE, KEYS_ACROSS, KEYS_TWIN)()
    for copy in fetched:
        copy.wait()

    def score_block(owner, plane, half):
        block = owner * 4 + plane
        here, one = block_rows(block), pl.ds(block, 1)
        keys = rows[owner, plane].reshape(BLOCK, PAD)
        seen = bias[here, :]
        seen = jnp.concatenate([seen] * (SUB // 128), axis=1)
        for k in range(HALF // SUB):
            first = half * HALF + k * SUB
            at = pl.ds(k * SUB, SUB)
            score = jnp.dot(keys[:, :WIDTH], query_cols[:, first : first + SUB], preferred_element_type=F32) + seen
            prob_grad = nt_dot(keys[:, :LATENT], grad_rows[first : first + SUB, :])
            top = jnp.max(score, axis=0, keepdims=True)
            weight = jnp.exp2((score - top) * FACTOR)
            scores[here, at] = weight
            prob_grads[here, at] = prob_grad
            tops[one, at] = top
            masses[one, at] = jnp.sum(weight, axis=0, keepdims=True)
            dots[one, at] = jnp.sum(weight * prob_grad, axis=0, keepdims=True)

    def finish_half(half):
        top = jnp.max(tops[...], axis=0, keepdims=True)
        level = jnp.exp2((tops[...] - top) * FACTOR)
        share = 1.0 / jnp.sum(level * masses[...], axis=0, keepdims=True)
        delta = jnp.sum(level * dots[...], axis=0, keepdims=True) * share
        tops[...] = level * share
        dots[...] = jnp.broadcast_to(delta, dots.shape)

        def grad_step(block, carry):
            here = block_rows(block)
            probability = scores[here, :] * tops[pl.ds(block, 1), :]
            weights[lax.div(block, 4), rem4(block)] = probability.astype(BF16).reshape(4, 4, PIECE, HALF)
            score_grad = probability * (prob_grads[here, :] - dots[pl.ds(0, 1), :])
            score_grads[here, half * HALF : (half + 1) * HALF] = score_grad.astype(BF16)
            return carry

        lax.fori_loop(0, BLOCKS, grad_step, 0)

    def key_terms(owner, plane, half):
        columns = slice(half * HALF, (half + 1) * HALF)
        here = block_rows(owner * 4 + plane)
        by_score = nt_dot(score_grads[here, columns], query_cols[:, columns]) * SCALE
        by_value = jnp.dot(
            weights[owner, plane].reshape(BLOCK, HALF), grad_rows[columns, :], preferred_element_type=F32
        )
        return by_score[:, :LATENT] + by_value, by_score[:, LATENT:]

    def first_score_step(step, carry):
        for k in range(1, 8):

            @pl.when(step == k)
            def _(k=k):
                arrive(k)

        owner, plane = plane_of(step)
        keys_t[:, block_rows(owner * 4 + plane)] = rows[owner, plane].reshape(BLOCK, PAD).T
        score_block(owner, plane, 0)
        return carry

    lax.fori_loop(0, BLOCKS, first_score_step, 0)

    hidden_own_copy.wait()
    hidden_copies = []
    for k in range(7):
        dz, flip = (k + 1) // 2, (k + 1) % 2
        device = place.shifted(0, 2 * flip, dz)
        hidden_copies.append(go(own_hidden, own_hidden, HIDDEN + k, device))

    finish_half(0)

    def first_key_step(block, carry):
        owner, plane = lax.div(block, 4), rem4(block)
        latent_term, rope_term = key_terms(owner, plane, 0)
        key_total[owner, plane, :, :, :, :LATENT] = latent_term.reshape(4, 4, PIECE, LATENT)
        key_total[owner, plane, :, :, :, LATENT:WIDTH] = rope_term.reshape(4, 4, PIECE, WIDTH - LATENT)
        key_total[owner, plane, :, :, :, WIDTH:] = jnp.zeros((4, 4, PIECE, PAD - WIDTH), F32)
        return carry

    lax.fori_loop(0, BLOCKS, first_key_step, 0)

    def second_score_step(block, carry):
        score_block(lax.div(block, 4), rem4(block), 1)
        return carry

    lax.fori_loop(0, BLOCKS, second_score_step, 0)
    finish_half(1)

    def second_key(owner, plane):
        latent_term, rope_term = key_terms(owner, plane, 1)
        key_total[owner, plane, :, :, :, :LATENT] += latent_term.reshape(4, 4, PIECE, LATENT)
        key_total[owner, plane, :, :, :, LATENT:WIDTH] += rope_term.reshape(4, 4, PIECE, WIDTH - LATENT)

    pairs, across = [], []
    for k, d in enumerate((2, 1, 3, 0)):
        plane = rem4(twin_a3 + d)
        pairs.append(later(key_total.at[1 - core, plane], twin_in.at[plane], GRADS_TWIN + k, twin))
    across.append(later(packed, from_far, GRADS_ACROSS, place.across(2)))
    for k, d in ((1, 1), (2, 3)):
        src = key_total.at[core, rem4(a3 + d)]
        across.append(later(src, from_near.at[k - 1], GRADS_ACROSS + k, place.across(d)))
    twins_turn = (1, 1, 0, 1, 0, 1, 0, 0)
    turn_shift = (2, 1, 2, 3, 1, 0, 3, 0)

    def second_key_step(step, carry):
        twins, shift = 0, 0
        for k in range(BLOCKS):
            here = jnp.where(step == k, 1, 0)
            twins, shift = twins + here * twins_turn[k], shift + here * turn_shift[k]
        owner = core + twins * (1 - 2 * core)
        plane = rem4(a3 + twins * (twin_a3 - a3) + shift)
        second_key(owner, plane)
        for k in range(BLOCKS):
            turn = (2, 1, 3, 0).index(turn_shift[k])

            @pl.when(step == k)
            def _(k=k, turn=turn):
                if twins_turn[k]:
                    pairs[turn].start()
                else:
                    pairs[turn].wait_recv()

        @pl.when(twins == 0)
        def _():
            for at2 in range(4):
                key_total[core, plane, at2] = key_total[core, plane, at2] + twin_in[plane, at2]

        @pl.when(step == 2)
        def _():
            packed[...] = key_total[core, plane].astype(BF16)
            across[0].start()

        for k, turn in ((4, 1), (6, 2)):

            @pl.when(step == k)
            def _(turn=turn):
                across[turn].start()

        return carry

    lax.fori_loop(0, BLOCKS, second_key_step, 0)
    for copy in hidden_copies:
        copy.wait_recv()
    hidden_to_twin = go(hidden_all.at[:, :, core], hidden_all.at[:, :, core], HIDDEN_TWIN, twin)

    query_copies = []
    for k in range(4):
        columns = slice(k * SUB, (k + 1) * SUB)
        total = jnp.dot(keys_t[:WIDTH, :], score_grads[:, columns], preferred_element_type=F32)
        query_cols[:, columns] = (total * SCALE).astype(BF16)
        for h in range(4 * k, 4 * k + 4):
            copy = pltpu.make_async_copy(query_cols.at[:, pl.ds(h * 128, 128)], query_out.at[h], local.at[3])
            copy.start()
            query_copies.append(copy)

    hidden_to_twin.wait_recv()
    hidden_rows = weights
    width = pl.ds(0, MODEL)
    moved = []
    for z in range(4):
        for y in range(4):
            moved.append((hidden_all.at[z, y // 2, 0, :, y % 2], hidden_rows.at[0, z, y, :, :, width]))
        for x in range(4):
            for y_hi in range(2):
                to = hidden_rows.at[1, x, z, pl.ds(2 * y_hi, 2), :, width]
                moved.append((hidden_all.at[z, y_hi, 1, x], to))
    moved = [pltpu.make_async_copy(src, dst, local.at[4]) for src, dst in moved]
    for copy in moved:
        copy.start()

    for copy in across:
        copy.wait_recv()

    def add_across(at2, carry):
        total = key_total[core, a3, at2] + from_near[0, at2] + from_near[1, at2]
        key_total[core, a3, at2] = total + from_far[at2].astype(F32)
        return carry

    lax.fori_loop(0, 4, add_across, 0)
    plane_copies = []
    for k, (d2, d1) in enumerate(PLANE_SHIFTS):
        src = key_total.at[core, a3, rem4(a2 + d2), rem4(a1 + d1)]
        plane_copies.append(go(src, from_plane.at[k], GRADS_PLANE + k, place.in_plane(d2, d1)))
    raw = raw_rows[...]
    latent = raw[:, :LATENT]
    inv_rms = lax.rsqrt(jnp.mean(latent * latent, axis=1, keepdims=True) + EPS)
    cube = inv_rms * inv_rms * inv_rms
    for copy in plane_copies:
        copy.wait_recv()
    key_grad = key_total[core, a3, a2, a1]
    for k in range(15):
        key_grad = key_grad + from_plane[k]
    latent_grad, tail = key_grad[:, :LATENT], key_grad[:, LATENT:]
    scaled = latent_grad * gain[...]
    latent_back = inv_rms * scaled - latent * cube * jnp.mean(scaled * latent, axis=1, keepdims=True)
    rope_back = tail * angles[0] - swap_halves(tail) * angles[1]
    back_rows[core, a3, a2, a1, :, :LATENT] = latent_back.astype(BF16)
    back_rows[core, a3, a2, a1, :, LATENT:] = rope_back.astype(BF16)
    spread_rest = spread(back_rows, ROWS_PLANE, ROWS_ACROSS, ROWS_TWIN)

    term = jnp.broadcast_to(jnp.sum(latent_grad * latent * inv_rms, axis=0, keepdims=True), (8, LATENT))
    gains[0] = term
    gain_plane[a2, a1] = term
    gain_copies = [
        go(gains.at[0], gain_plane.at[a2, a1], GAIN_PLANE + k, place.in_plane(*d)) for k, d in enumerate(PLANE_SHIFTS)
    ]
    for copy in moved:
        copy.wait()
    arrive_back = spread_rest()
    for copy in gain_copies:
        copy.wait_recv()
    term = gain_plane[0, 0]
    for k in range(1, 16):
        term = term + gain_plane[k // 4, k % 4]
    gains[1] = term
    gain_across[a3] = term
    gain_copies = [go(gains.at[1], gain_across.at[a3], GAIN_ACROSS + d - 1, place.across(d)) for d in (1, 2, 3)]
    down_grad[...] = jnp.zeros_like(down_grad)

    def down_step(step, carry):
        @pl.when(step == BLOCKS - 1)
        def _():
            mine = []
            for head in range(8):
                x, y = head // 2, place.y_hi * 2 + head % 2
                mine.append(back_rows[core, place.pick(place.z, x), place.pick(y, place.z), place.pick(x, y)])
            mine = jnp.concatenate(mine, axis=0)
            hidden_grad[...] = jnp.dot(mine[:, :WIDTH], kv_turned[...], preferred_element_type=F32).astype(BF16)

        for k in range(1, 8):

            @pl.when(step == k)
            def _(k=k):
                arrive_back(k)

        owner, plane = plane_of(step)
        turned = back_rows[owner, plane].reshape(BLOCK, PAD).T
        down_grad[...] += jnp.dot(
            turned[:WIDTH], hidden_rows[owner, plane, :, :, :, :MODEL].reshape(BLOCK, MODEL), preferred_element_type=F32
        )
        return carry

    lax.fori_loop(0, BLOCKS, down_step, 0)
    for copy in gain_copies:
        copy.wait_recv()
    term = gain_across[0] + gain_across[1] + gain_across[2] + gain_across[3]
    gains[2] = term
    gain_twin[core] = term
    last = go(gains.at[2], gain_twin.at[core], GAIN_TWIN, twin)

    last.wait_recv()
    gain_out[...] = (gain_twin[0] + gain_twin[1])[:1]
    for copy in query_copies:
        copy.wait()
    for copy in sent:
        copy.wait_send()


def whole(hidden, kv_turned, gain, rope, queries, grads, span_table):
    vmem = pl.BlockSpec(memory_space=pltpu.VMEM)
    smem = pl.BlockSpec(memory_space=pltpu.SMEM)
    anywhere = pl.BlockSpec(memory_space=pl.ANY)
    pieces = (2, 4, 4, 4, PIECE)
    return pl.pallas_call(
        whole_kernel,
        out_shape=(
            jax.ShapeDtypeStruct((HEADS, WIDTH, 128), BF16),
            jax.ShapeDtypeStruct((1, LATENT), F32),
            jax.ShapeDtypeStruct((128, MODEL), BF16),
            jax.ShapeDtypeStruct((WIDTH, MODEL), F32),
            jax.ShapeDtypeStruct((4, 2, 2, 4, 2, PIECE, MODEL), BF16),
        ),
        in_specs=[vmem, vmem, vmem, anywhere, anywhere, anywhere, smem],
        out_specs=(anywhere, vmem, vmem, vmem, anywhere),
        scratch_shapes=[
            pltpu.VMEM((8, PIECE, PAD), F32),
            pltpu.VMEM((8, PIECE, PAD), F32),
            pltpu.VMEM((PIECE, PAD), F32),
            pltpu.VMEM((SPANS, PIECE, 128), F32),
            pltpu.VMEM((2, PIECE, 128), F32),
            pltpu.VMEM(pieces + (PAD,), BF16),
            pltpu.VMEM((PAD, TOKENS), BF16),
            pltpu.VMEM((WIDTH, ROWS), BF16),
            pltpu.VMEM((ROWS, LATENT), BF16),
            pltpu.VMEM((TOKENS, 128), F32),
            pltpu.VMEM((TOKENS, HALF), F32),
            pltpu.VMEM((TOKENS, HALF), F32),
            pltpu.VMEM((BLOCKS, HALF), F32),
            pltpu.VMEM((BLOCKS, HALF), F32),
            pltpu.VMEM((BLOCKS, HALF), F32),
            pltpu.VMEM(pieces + (HALF,), BF16),
            pltpu.VMEM((TOKENS, ROWS), BF16),
            pltpu.VMEM(pieces + (PAD,), F32),
            pltpu.VMEM(pieces[1:] + (PAD,), F32),
            pltpu.VMEM((4, 4, PIECE, PAD), BF16),
            pltpu.VMEM((2, 4, 4, PIECE, PAD), F32),
            pltpu.VMEM((4, 4, PIECE, PAD), BF16),
            pltpu.VMEM((15, PIECE, PAD), F32),
            pltpu.VMEM(pieces + (PAD,), BF16),
            pltpu.VMEM((3, 8, LATENT), F32),
            pltpu.VMEM((4, 4, 8, LATENT), F32),
            pltpu.VMEM((4, 8, LATENT), F32),
            pltpu.VMEM((2, 8, LATENT), F32),
            pltpu.SemaphoreType.DMA((SEMAPHORES,)),
            pltpu.SemaphoreType.DMA((SEMAPHORES,)),
            pltpu.SemaphoreType.DMA((6,)),
        ],
        compiler_params=pltpu.CompilerParams(
            collective_id=0, has_side_effects=True, vmem_limit_bytes=63 * 2**20
        ),
    )(hidden, kv_turned, gain, rope, queries, grads, span_table)


def hand_on_kernel(*refs):
    count = 4
    sems = refs[-1]
    copies = []
    for src, dst in zip(refs[:count], refs[count : 2 * count]):
        rows = src.shape[0]
        parts = 8 if rows % 64 == 0 else 16 if rows == HEADS else 1
        for k in range(parts):
            at = pl.ds(k * (rows // parts), rows // parts)
            copies.append(pltpu.make_async_copy(src.at[at], dst.at[at], sems.at[len(copies)]))
    for copy in copies:
        copy.start()
    for copy in copies:
        copy.wait()


def hand_on(*arrays):
    anywhere = pl.BlockSpec(memory_space=pl.ANY)
    return pl.pallas_call(
        hand_on_kernel,
        out_shape=tuple(jax.ShapeDtypeStruct(a.shape, a.dtype) for a in arrays),
        in_specs=[anywhere] * len(arrays),
        out_specs=(anywhere,) * len(arrays),
        scratch_shapes=[pltpu.SemaphoreType.DMA((40,))],
    )(*arrays)


def per_device(table, hidden, kv_down, kv_gain, queries, out_grad, span_table):
    query_grad, gain_grad, hidden_grad, down_grad, _ = whole(
        hidden.reshape(4, 2, PIECE, MODEL),
        kv_down.T,
        kv_gain.reshape(1, LATENT),
        table,
        queries.transpose(1, 2, 0),
        out_grad.reshape(ROWS, LATENT),
        span_table,
    )
    query_grad, gain_grad, hidden_grad, down_grad = hand_on(query_grad, gain_grad, hidden_grad, down_grad)
    return (query_grad.transpose(2, 0, 1), hidden_grad, down_grad.T, gain_grad[0])


def solution(mesh):
    table = rope_rows()

    def run(hidden, kv_down, kv_gain, queries, out_grad, span_table):
        return jax.shard_map(
            per_device,
            mesh=mesh,
            in_specs=(
                P(),
                P("ctx", "head"),
                P("head", None),
                P(),
                P("ctx", "head", None),
                P("ctx", "head", None),
                P(),
            ),
            out_specs=(P("ctx", "head", None), P("ctx", "head"), P("head", None), P()),
            check_vma=False,
        )(jnp.asarray(table), hidden, kv_down, kv_gain, queries, out_grad, span_table)

    return run
```

```python
import functools
import math

import jax
import jax.numpy as jnp
import numpy as np
from jax import lax
from jax.experimental import pallas as pl
from jax.experimental.pallas import tpu as pltpu
from jax.sharding import PartitionSpec as P

MESH = pl.DeviceIdType.MESH
F32 = jnp.float32
BF16 = jnp.bfloat16
LATENT = 512
WIDTH = 576
PAD = 640
SPAN = 64
SPANS = 32
TOKENS = 2048
PIECE = 16
HEADS = 16
ROWS = 2048
MODEL = 896
EPS = 1e-06
SCALE = 1.0 / math.sqrt(192.0)
FACTOR = SCALE * math.log2(math.e)
BLOCK = 256
BLOCKS = TOKENS // BLOCK
HALF = ROWS // 2
SUB = 512


def rope_rows():
    half = (WIDTH - LATENT) // 2
    freq = np.exp(np.float32(-math.log(10000.0)) * np.arange(half, dtype=np.float32) / np.float32(half))
    angle = np.arange(TOKENS, dtype=np.float32)[:, None] * freq.astype(np.float32)[None, :]
    cos, sin = np.cos(angle.astype(np.float64)), np.sin(angle.astype(np.float64))
    both = np.concatenate([cos, cos, -sin, sin], axis=1).astype(np.float32)
    return np.ascontiguousarray(both.reshape(SPANS, 4, PIECE, 128).transpose(1, 0, 2, 3))


def nt_dot(left, right):
    return lax.dot_general(left, right, (((1,), (1,)), ((), ())), preferred_element_type=F32)


def rem4(value):
    return lax.rem(value, 4)


class Place:
    def __init__(self):
        ctx, head = lax.axis_index("ctx"), lax.axis_index("head")
        self.ctx, self.head = ctx, head
        self.core = lax.rem(ctx, 2)
        self.x = lax.div(head, 2)
        self.y_lo = lax.rem(head, 2)
        self.y_hi = lax.rem(lax.div(ctx, 2), 2)
        self.y = self.y_hi * 2 + self.y_lo
        self.z = lax.div(ctx, 4)
        self.a1 = self.pick(self.x, self.y)
        self.a2 = self.pick(self.y, self.z)
        self.a3 = self.pick(self.z, self.x)
        self.twin_a3 = self.pick(self.x, self.z)

    def pick(self, first, second):
        return first + self.core * (second - first)

    def device(self, x, y, z, core):
        return (z * 4 + lax.div(y, 2) * 2 + core, x * 2 + lax.rem(y, 2))

    def shifted(self, dx, dy, dz):
        return self.device(rem4(self.x + dx), rem4(self.y + dy), rem4(self.z + dz), self.core)

    def in_plane(self, d2, d1):
        return self.shifted(d1 * (1 - self.core), self.pick(d2, d1), d2 * self.core)

    def across(self, d3):
        return self.shifted(d3 * self.core, 0, d3 * (1 - self.core))

    def beside(self, d):
        return self.shifted(d * self.core, self.pick(2, 5 - 2 * self.y_lo), d * (1 - self.core))

    def twin(self):
        return self.device(self.x, self.y, self.z, 1 - self.core)


def remote(src, dst, send_sem, recv_sem, device):
    return pltpu.make_async_remote_copy(
        src_ref=src, dst_ref=dst, send_sem=send_sem, recv_sem=recv_sem, device_id=device, device_id_type=MESH
    )


def swap_halves(tail):
    lane = lax.broadcasted_iota(jnp.int32, tail.shape, 1)
    return jnp.where(lane < 32, pltpu.roll(tail, 96, 1), pltpu.roll(tail, 32, 1))


def block_rows(block):
    return pl.ds(pl.multiple_of(block * BLOCK, BLOCK), BLOCK)


PLANE_SHIFTS = [(d2, d1) for d2 in range(4) for d1 in range(4) if d2 or d1]

SUM_RAW = 0
KEYS_PLANE = 7
KEYS_ACROSS = 22
KEYS_TWIN = 25
HIDDEN = 29
HIDDEN_TWIN = 36
GRADS_TWIN = 37
GRADS_ACROSS = 41
GRADS_PLANE = 44
ROWS_PLANE = 59
ROWS_ACROSS = 74
ROWS_TWIN = 77
GAIN_PLANE = 81
GAIN_ACROSS = 96
GAIN_TWIN = 99
SEMAPHORES = 100


def whole_kernel(
    hidden,
    kv_turned,
    gain,
    rope,
    queries,
    grads,
    span,
    query_out,
    gain_out,
    hidden_grad,
    down_grad,
    hidden_rows,
    part,
    landed,
    raw_rows,
    rope_part,
    angles,
    rows,
    keys_t,
    query_cols,
    grad_rows,
    bias,
    scores,
    prob_grads,
    tops,
    masses,
    dots,
    weights,
    score_grads,
    key_total,
    twin_in,
    packed,
    from_near,
    from_far,
    from_plane,
    back_rows,
    gains,
    gain_plane,
    gain_across,
    gain_twin,
    send,
    recv,
    local,
):
    place = Place()
    core, a1, a2, a3 = place.core, place.a1, place.a2, place.a3
    twin = place.twin()
    devices = [place.in_plane(d2, d1) for d2, d1 in PLANE_SHIFTS]
    devices += [place.across(d) for d in (1, 2, 3)] + [place.beside(d) for d in (1, 2, 3)] + [twin]
    barrier = pltpu.get_barrier_semaphore()
    for device in devices:
        pl.semaphore_signal(barrier, inc=1, device_id=device, device_id_type=MESH)

    sent = []

    def copy_of(src, dst, slot, device):
        return remote(src, dst, send.at[slot], recv.at[slot], device)

    def go(src, dst, slot, device):
        copy = copy_of(src, dst, slot, device)
        copy.start()
        sent.append(copy)
        return copy

    def later(src, dst, slot, device):
        copy = copy_of(src, dst, slot, device)
        sent.append(copy)
        return copy

    fetched = [
        pltpu.make_async_copy(queries.at[h], query_cols.at[:, pl.ds(h * 128, 128)], local.at[0]) for h in range(HEADS)
    ]
    for copy in fetched:
        copy.start()
    raw_grads = score_grads.at[:, pl.ds(0, LATENT)]
    grads_fetch = pltpu.make_async_copy(grads, raw_grads, local.at[1])
    grads_fetch.start()

    def hidden_parts():
        first = 2 * place.y_hi
        by_core = [[(hidden.at[:, k], hidden_rows.at[0, place.z, first + k]) for k in range(2)]]
        by_core.append([(hidden.at[k], hidden_rows.at[1, k, place.z, pl.ds(first, 2)]) for k in range(4)])
        return by_core

    rope_fetch = pltpu.make_async_copy(rope.at[rem4(place.head)], rope_part, local.at[5])
    rope_fetch.start()

    product = nt_dot(hidden[...].reshape(128, MODEL), kv_turned[...])
    part[:, :, :WIDTH] = product.reshape(8, PIECE, WIDTH)
    part[:, :, WIDTH:] = jnp.zeros((8, PIECE, PAD - WIDTH), F32)
    landed[place.head] = part[place.head]
    pl.semaphore_wait(barrier, len(devices))
    raw_copies = []
    for d in range(1, 8):
        other = lax.rem(place.head + d, 8)
        raw_copies.append(go(part.at[other], landed.at[place.head], SUM_RAW + d - 1, (place.ctx, other)))

    for owner, parts in enumerate(hidden_parts()):

        @pl.when(core == owner)
        def _(parts=parts):
            copies = [pltpu.make_async_copy(src, dst, local.at[2]) for src, dst in parts]
            for copy in copies:
                copy.start()
            for copy in copies:
                copy.wait()

    token = lax.broadcasted_iota(jnp.int32, (1, 128), 1)
    query_pos = jnp.where(token < SPAN, span[2 * place.ctx] * SPAN, span[2 * place.ctx + 1] * SPAN) + lax.rem(token, SPAN)
    seen_from = query_pos - lax.broadcasted_iota(jnp.int32, (PIECE, 128), 0)
    starts = [span[slot] * SPAN for slot in range(SPANS)]
    for owner in range(2):
        for index in range(64):
            at3, at2, at1 = index // 16, index // 4 % 4, index % 4
            x, y, z = ((at1, at2, at3), (at3, at1, at2))[owner]
            head = x * 2 + y % 2
            start = starts[(z * 4 + y // 2 * 2 + owner) * 2 + head // 4] + head % 4 * PIECE
            bias[pl.ds((owner * 64 + index) * PIECE, PIECE), :] = jnp.where(seen_from >= start, 0.0, -1e30)
    rope_fetch.wait()
    mine = span[2 * place.ctx + lax.div(place.head, 4)]
    both = jnp.zeros((PIECE, 128), F32)
    for k in range(SPANS):
        both = jnp.where(mine == k, rope_part[k], both)
    lane = lax.broadcasted_iota(jnp.int32, (PIECE, 128), 1)
    angles[0] = jnp.where(lane < 64, both, 0.0)
    angles[1] = jnp.where(lane < 64, pltpu.roll(both, 64, 1), 0.0)
    to = lax.broadcasted_iota(jnp.int32, (256, 256), 0)
    at = lax.broadcasted_iota(jnp.int32, (256, 256), 1)
    swap = (lax.div(to, 16) == lax.rem(at, 16)) & (lax.rem(to, 16) == lax.div(at, 16))
    swap = jnp.where(swap, 1.0, 0.0).astype(BF16)
    grads_fetch.wait()

    def order_grads(index, carry):
        here = pl.ds(pl.multiple_of(index * 256, 256), 256)
        turned = jnp.dot(swap, score_grads[here, :LATENT], preferred_element_type=F32).astype(BF16)
        for h in range(HEADS):
            to_rows = pl.ds(pl.multiple_of(h * 128 + index * 16, 16), 16)
            grad_rows[to_rows, :] = turned[h * 16 : (h + 1) * 16, :]
        return carry

    lax.fori_loop(0, 8, order_grads, 0)

    for copy in raw_copies:
        copy.wait_recv()
    raw = landed[0]
    for k in range(1, 8):
        raw = raw + landed[k]
    raw_rows[...] = raw
    latent, tail = raw[:, :LATENT], raw[:, LATENT:]
    inv_rms = lax.rsqrt(jnp.mean(latent * latent, axis=1, keepdims=True) + EPS)
    turned = tail * angles[0] + swap_halves(tail) * angles[1]
    rows[core, a3, a2, a1, :, :LATENT] = (latent * inv_rms * gain[...]).astype(BF16)
    rows[core, a3, a2, a1, :, LATENT:] = turned.astype(BF16)

    before, after, opposite = rem4(a3 + 3), rem4(a3 + 1), rem4(a3 + 2)
    twin_a3 = place.twin_a3
    own_planes = [a3, before, after, opposite]
    twin_planes = [twin_a3, rem4(twin_a3 + 3), rem4(twin_a3 + 1), rem4(twin_a3 + 2)]

    def spread(ref, plane_sem, across_sem, twin_sem):
        piece = ref.at[core, a3, a2, a1]
        copies = [go(piece, piece, plane_sem + k, place.in_plane(*d)) for k, d in enumerate(PLANE_SHIFTS)]

        def rest():
            for copy in copies:
                copy.wait_recv()
            plane = ref.at[core, a3]
            across = {d: go(plane, plane, across_sem + d - 1, place.across(d)) for d in (1, 3)}
            across[2] = later(plane, plane, across_sem + 1, place.across(2))
            pairs = [go(plane, plane, twin_sem, twin)]
            for k in (1, 2, 3):
                plane = ref.at[core, own_planes[k]]
                pairs.append(later(plane, plane, twin_sem + k, twin))

            def arrive(step):
                if step == 1:
                    pairs[0].wait_recv()
                    across[2].start()
                if step in (2, 3, 6):
                    k = {2: 1, 3: 2, 6: 3}[step]
                    across[{1: 1, 2: 3, 3: 2}[k]].wait_recv()
                    pairs[k].start()
                if step in (4, 5, 7):
                    pairs[{4: 1, 5: 2, 7: 3}[step]].wait_recv()

            return arrive

        return rest

    def plane_of(step):
        by_step = [(0, 0), (1, 0), (0, 3), (0, 1), (1, 3), (1, 1), (0, 2), (1, 2)]
        owner, shift = 0, 0
        for k, (twins, d) in enumerate(by_step):
            here = jnp.where(step == k, 1, 0)
            owner, shift = owner + here * twins, shift + here * d
        base = a3 + owner * (twin_a3 - a3)
        return core + owner * (1 - 2 * core), rem4(base + shift)

    arrive = spread(rows, KEYS_PLANE, KEYS_ACROSS, KEYS_TWIN)()
    for copy in fetched:
        copy.wait()

    def score_block(owner, plane, half):
        block = owner * 4 + plane
        here, one = block_rows(block), pl.ds(block, 1)
        keys = rows[owner, plane].reshape(BLOCK, PAD)
        seen = bias[here, :]
        seen = jnp.concatenate([seen] * (SUB // 128), axis=1)
        for k in range(HALF // SUB):
            first = half * HALF + k * SUB
            at = pl.ds(k * SUB, SUB)
            score = jnp.dot(keys[:, :WIDTH], query_cols[:, first : first + SUB], preferred_element_type=F32) + seen
            prob_grad = nt_dot(keys[:, :LATENT], grad_rows[first : first + SUB, :])
            top = jnp.max(score, axis=0, keepdims=True)
            weight = jnp.exp2((score - top) * FACTOR)
            scores[here, at] = weight
            prob_grads[here, at] = prob_grad
            tops[one, at] = top
            masses[one, at] = jnp.sum(weight, axis=0, keepdims=True)
            dots[one, at] = jnp.sum(weight * prob_grad, axis=0, keepdims=True)

    def finish_half(half):
        top = jnp.max(tops[...], axis=0, keepdims=True)
        level = jnp.exp2((tops[...] - top) * FACTOR)
        share = 1.0 / jnp.sum(level * masses[...], axis=0, keepdims=True)
        delta = jnp.sum(level * dots[...], axis=0, keepdims=True) * share
        tops[...] = level * share
        dots[...] = jnp.broadcast_to(delta, dots.shape)

        def grad_step(block, carry):
            here = block_rows(block)
            probability = scores[here, :] * tops[pl.ds(block, 1), :]
            weights[lax.div(block, 4), rem4(block)] = probability.astype(BF16).reshape(4, 4, PIECE, HALF)
            score_grad = probability * (prob_grads[here, :] - dots[pl.ds(0, 1), :])
            score_grads[here, half * HALF : (half + 1) * HALF] = score_grad.astype(BF16)
            return carry

        lax.fori_loop(0, BLOCKS, grad_step, 0)

    def key_terms(owner, plane, half):
        columns = slice(half * HALF, (half + 1) * HALF)
        here = block_rows(owner * 4 + plane)
        by_score = nt_dot(score_grads[here, columns], query_cols[:, columns]) * SCALE
        by_value = jnp.dot(
            weights[owner, plane].reshape(BLOCK, HALF), grad_rows[columns, :], preferred_element_type=F32
        )
        return by_score[:, :LATENT] + by_value, by_score[:, LATENT:]

    def first_score_step(step, carry):
        for k in range(1, 8):

            @pl.when(step == k)
            def _(k=k):
                arrive(k)

        owner, plane = plane_of(step)
        keys_t[:, block_rows(owner * 4 + plane)] = rows[owner, plane].reshape(BLOCK, PAD).T
        score_block(owner, plane, 0)
        return carry

    lax.fori_loop(0, BLOCKS, first_score_step, 0)

    hidden_copies = []
    for k in range(7):
        dz, flip = (k + 1) // 2, (k + 1) % 2
        device = place.shifted(0, 2 * flip, dz)
        for owner, parts in enumerate(hidden_parts()):

            @pl.when(core == owner)
            def _(parts=parts, k=k, device=device):
                for src, dst in parts:
                    copy_of(src, dst, HIDDEN + k, device).start()

        like = hidden_rows.at[0, 0, pl.ds(0, 2)]
        hidden_copies.append(later(like, like, HIDDEN + k, device))

    finish_half(0)

    def first_key_step(block, carry):
        owner, plane = lax.div(block, 4), rem4(block)
        latent_term, rope_term = key_terms(owner, plane, 0)
        key_total[owner, plane, :, :, :, :LATENT] = latent_term.reshape(4, 4, PIECE, LATENT)
        key_total[owner, plane, :, :, :, LATENT:WIDTH] = rope_term.reshape(4, 4, PIECE, WIDTH - LATENT)
        key_total[owner, plane, :, :, :, WIDTH:] = jnp.zeros((4, 4, PIECE, PAD - WIDTH), F32)
        return carry

    lax.fori_loop(0, BLOCKS, first_key_step, 0)

    def second_score_step(block, carry):
        score_block(lax.div(block, 4), rem4(block), 1)
        return carry

    lax.fori_loop(0, BLOCKS, second_score_step, 0)
    finish_half(1)

    def second_key(owner, plane):
        latent_term, rope_term = key_terms(owner, plane, 1)
        key_total[owner, plane, :, :, :, :LATENT] += latent_term.reshape(4, 4, PIECE, LATENT)
        key_total[owner, plane, :, :, :, LATENT:WIDTH] += rope_term.reshape(4, 4, PIECE, WIDTH - LATENT)

    pairs, across = [], []
    for k, d in enumerate((2, 1, 3, 0)):
        plane = rem4(twin_a3 + d)
        pairs.append(later(key_total.at[1 - core, plane], twin_in.at[plane], GRADS_TWIN + k, twin))
    across.append(later(packed, from_far, GRADS_ACROSS, place.across(2)))
    for k, d in ((1, 1), (2, 3)):
        src = key_total.at[core, rem4(a3 + d)]
        across.append(later(src, from_near.at[k - 1], GRADS_ACROSS + k, place.across(d)))
    twins_turn = (1, 1, 0, 1, 0, 1, 0, 0)
    turn_shift = (2, 1, 2, 3, 1, 0, 3, 0)

    def second_key_step(step, carry):
        twins, shift = 0, 0
        for k in range(BLOCKS):
            here = jnp.where(step == k, 1, 0)
            twins, shift = twins + here * twins_turn[k], shift + here * turn_shift[k]
        owner = core + twins * (1 - 2 * core)
        plane = rem4(a3 + twins * (twin_a3 - a3) + shift)
        second_key(owner, plane)
        for k in range(BLOCKS):
            turn = (2, 1, 3, 0).index(turn_shift[k])

            @pl.when(step == k)
            def _(k=k, turn=turn):
                if twins_turn[k]:
                    pairs[turn].start()
                else:
                    pairs[turn].wait_recv()

        @pl.when(twins == 0)
        def _():
            for at2 in range(4):
                key_total[core, plane, at2] = key_total[core, plane, at2] + twin_in[plane, at2]

        @pl.when(step == 2)
        def _():
            packed[...] = key_total[core, plane].astype(BF16)
            across[0].start()

        for k, turn in ((4, 1), (6, 2)):

            @pl.when(step == k)
            def _(turn=turn):
                across[turn].start()

        return carry

    lax.fori_loop(0, BLOCKS, second_key_step, 0)
    for copy in hidden_copies:
        copy.wait_recv()
    hidden_to_twin = go(hidden_rows.at[core], hidden_rows.at[core], HIDDEN_TWIN, twin)

    query_copies = []
    for k in range(4):
        columns = slice(k * SUB, (k + 1) * SUB)
        total = jnp.dot(keys_t[:WIDTH, :], score_grads[:, columns], preferred_element_type=F32)
        query_cols[:, columns] = (total * SCALE).astype(BF16)
        for h in range(4 * k, 4 * k + 4):
            copy = pltpu.make_async_copy(query_cols.at[:, pl.ds(h * 128, 128)], query_out.at[h], local.at[3])
            copy.start()
            query_copies.append(copy)

    for copy in across:
        copy.wait_recv()

    def add_across(at2, carry):
        total = key_total[core, a3, at2] + from_near[0, at2] + from_near[1, at2]
        key_total[core, a3, at2] = total + from_far[at2].astype(F32)
        return carry

    lax.fori_loop(0, 4, add_across, 0)
    plane_copies = []
    for k, (d2, d1) in enumerate(PLANE_SHIFTS):
        src = key_total.at[core, a3, rem4(a2 + d2), rem4(a1 + d1)]
        plane_copies.append(go(src, from_plane.at[k], GRADS_PLANE + k, place.in_plane(d2, d1)))
    raw = raw_rows[...]
    latent = raw[:, :LATENT]
    inv_rms = lax.rsqrt(jnp.mean(latent * latent, axis=1, keepdims=True) + EPS)
    cube = inv_rms * inv_rms * inv_rms
    for copy in plane_copies:
        copy.wait_recv()
    key_grad = key_total[core, a3, a2, a1]
    for k in range(15):
        key_grad = key_grad + from_plane[k]
    latent_grad, tail = key_grad[:, :LATENT], key_grad[:, LATENT:]
    scaled = latent_grad * gain[...]
    latent_back = inv_rms * scaled - latent * cube * jnp.mean(scaled * latent, axis=1, keepdims=True)
    rope_back = tail * angles[0] - swap_halves(tail) * angles[1]
    back_rows[core, a3, a2, a1, :, :LATENT] = latent_back.astype(BF16)
    back_rows[core, a3, a2, a1, :, LATENT:] = rope_back.astype(BF16)
    spread_rest = spread(back_rows, ROWS_PLANE, ROWS_ACROSS, ROWS_TWIN)

    term = jnp.broadcast_to(jnp.sum(latent_grad * latent * inv_rms, axis=0, keepdims=True), (8, LATENT))
    gains[0] = term
    gain_plane[a2, a1] = term
    gain_copies = [
        go(gains.at[0], gain_plane.at[a2, a1], GAIN_PLANE + k, place.in_plane(*d)) for k, d in enumerate(PLANE_SHIFTS)
    ]
    hidden_to_twin.wait_recv()
    arrive_back = spread_rest()
    for copy in gain_copies:
        copy.wait_recv()
    term = gain_plane[0, 0]
    for k in range(1, 16):
        term = term + gain_plane[k // 4, k % 4]
    gains[1] = term
    gain_across[a3] = term
    gain_copies = [go(gains.at[1], gain_across.at[a3], GAIN_ACROSS + d - 1, place.across(d)) for d in (1, 2, 3)]
    down_grad[...] = jnp.zeros_like(down_grad)

    def down_step(step, carry):
        @pl.when(step == BLOCKS - 1)
        def _():
            mine = []
            for head in range(8):
                x, y = head // 2, place.y_hi * 2 + head % 2
                mine.append(back_rows[core, place.pick(place.z, x), place.pick(y, place.z), place.pick(x, y)])
            mine = jnp.concatenate(mine, axis=0)
            hidden_grad[...] = jnp.dot(mine[:, :WIDTH], kv_turned[...], preferred_element_type=F32).astype(BF16)

        for k in range(1, 8):

            @pl.when(step == k)
            def _(k=k):
                arrive_back(k)

        owner, plane = plane_of(step)
        turned = back_rows[owner, plane].reshape(BLOCK, PAD).T
        down_grad[...] += jnp.dot(
            turned[:WIDTH], hidden_rows[owner, plane].reshape(BLOCK, MODEL), preferred_element_type=F32
        )
        return carry

    lax.fori_loop(0, BLOCKS, down_step, 0)
    for copy in gain_copies:
        copy.wait_recv()
    term = gain_across[0] + gain_across[1] + gain_across[2] + gain_across[3]
    gains[2] = term
    gain_twin[core] = term
    last = go(gains.at[2], gain_twin.at[core], GAIN_TWIN, twin)

    last.wait_recv()
    gain_out[...] = (gain_twin[0] + gain_twin[1])[:1]
    for copy in query_copies:
        copy.wait()
    for copy in sent:
        copy.wait_send()


def whole(hidden, kv_turned, gain, rope, queries, grads, span_table):
    vmem = pl.BlockSpec(memory_space=pltpu.VMEM)
    smem = pl.BlockSpec(memory_space=pltpu.SMEM)
    anywhere = pl.BlockSpec(memory_space=pl.ANY)
    pieces = (2, 4, 4, 4, PIECE)
    return pl.pallas_call(
        whole_kernel,
        out_shape=(
            jax.ShapeDtypeStruct((HEADS, WIDTH, 128), BF16),
            jax.ShapeDtypeStruct((1, LATENT), F32),
            jax.ShapeDtypeStruct((128, MODEL), BF16),
            jax.ShapeDtypeStruct((WIDTH, MODEL), F32),
        ),
        in_specs=[vmem, vmem, vmem, anywhere, anywhere, anywhere, smem],
        out_specs=(anywhere, vmem, vmem, vmem),
        scratch_shapes=[
            pltpu.VMEM(pieces + (MODEL,), BF16),
            pltpu.VMEM((8, PIECE, PAD), F32),
            pltpu.VMEM((8, PIECE, PAD), F32),
            pltpu.VMEM((PIECE, PAD), F32),
            pltpu.VMEM((SPANS, PIECE, 128), F32),
            pltpu.VMEM((2, PIECE, 128), F32),
            pltpu.VMEM(pieces + (PAD,), BF16),
            pltpu.VMEM((PAD, TOKENS), BF16),
            pltpu.VMEM((WIDTH, ROWS), BF16),
            pltpu.VMEM((ROWS, LATENT), BF16),
            pltpu.VMEM((TOKENS, 128), F32),
            pltpu.VMEM((TOKENS, HALF), F32),
            pltpu.VMEM((TOKENS, HALF), F32),
            pltpu.VMEM((BLOCKS, HALF), F32),
            pltpu.VMEM((BLOCKS, HALF), F32),
            pltpu.VMEM((BLOCKS, HALF), F32),
            pltpu.VMEM(pieces + (HALF,), BF16),
            pltpu.VMEM((TOKENS, ROWS), BF16),
            pltpu.VMEM(pieces + (PAD,), F32),
            pltpu.VMEM(pieces[1:] + (PAD,), F32),
            pltpu.VMEM((4, 4, PIECE, PAD), BF16),
            pltpu.VMEM((2, 4, 4, PIECE, PAD), F32),
            pltpu.VMEM((4, 4, PIECE, PAD), BF16),
            pltpu.VMEM((15, PIECE, PAD), F32),
            pltpu.VMEM(pieces + (PAD,), BF16),
            pltpu.VMEM((3, 8, LATENT), F32),
            pltpu.VMEM((4, 4, 8, LATENT), F32),
            pltpu.VMEM((4, 8, LATENT), F32),
            pltpu.VMEM((2, 8, LATENT), F32),
            pltpu.SemaphoreType.DMA((SEMAPHORES,)),
            pltpu.SemaphoreType.DMA((SEMAPHORES,)),
            pltpu.SemaphoreType.DMA((6,)),
        ],
        compiler_params=pltpu.CompilerParams(
            collective_id=0, has_side_effects=True, vmem_limit_bytes=64 * 2**20 - 2**18
        ),
    )(hidden, kv_turned, gain, rope, queries, grads, span_table)


def hand_on_kernel(*refs):
    count = 4
    arrivals, departures = refs[-2:]
    steps = []
    for src, dst, held in zip(refs[:count], refs[count : 2 * count], refs[2 * count : 3 * count]):
        rows = src.shape[0]
        parts = 8 if rows == WIDTH else 16 if rows == HEADS else 1
        for k in range(parts):
            at, n = pl.ds(k * (rows // parts), rows // parts), len(steps)
            steps.append(
                (
                    pltpu.make_async_copy(src.at[at], held.at[at], arrivals.at[n]),
                    pltpu.make_async_copy(held.at[at], dst.at[at], departures.at[n]),
                )
            )
    for arrival, _ in steps:
        arrival.start()
    for arrival, departure in steps:
        arrival.wait()
        departure.start()
    for _, departure in steps:
        departure.wait()


def hand_on(*arrays):
    anywhere = pl.BlockSpec(memory_space=pl.ANY)
    return pl.pallas_call(
        hand_on_kernel,
        out_shape=tuple(jax.ShapeDtypeStruct(a.shape, a.dtype) for a in arrays),
        in_specs=[anywhere] * len(arrays),
        out_specs=(anywhere,) * len(arrays),
        scratch_shapes=[pltpu.VMEM(a.shape, a.dtype) for a in arrays] + [pltpu.SemaphoreType.DMA((26,))] * 2,
        compiler_params=pltpu.CompilerParams(vmem_limit_bytes=63 * 2**20),
    )(*arrays)


def per_device(table, hidden, kv_down, kv_gain, queries, out_grad, span_table):
    query_grad, gain_grad, hidden_grad, down_grad = whole(
        hidden.reshape(4, 2, PIECE, MODEL),
        kv_down.T,
        kv_gain.reshape(1, LATENT),
        table,
        queries.transpose(1, 2, 0),
        out_grad.reshape(ROWS, LATENT),
        span_table,
    )
    query_grad, gain_grad, hidden_grad, down_grad = hand_on(query_grad, gain_grad, hidden_grad, down_grad)
    return (query_grad.transpose(2, 0, 1), hidden_grad, down_grad.T, gain_grad[0])


def solution(mesh):
    table = rope_rows()

    def run(hidden, kv_down, kv_gain, queries, out_grad, span_table):
        return jax.shard_map(
            per_device,
            mesh=mesh,
            in_specs=(
                P(),
                P("ctx", "head"),
                P("head", None),
                P(),
                P("ctx", "head", None),
                P("ctx", "head", None),
                P(),
            ),
            out_specs=(P("ctx", "head", None), P("ctx", "head"), P("head", None), P()),
            check_vma=False,
        )(jnp.asarray(table), hidden, kv_down, kv_gain, queries, out_grad, span_table)

    return run
```

```python
import functools
import math

import jax
import jax.numpy as jnp
import numpy as np
from jax import lax
from jax.experimental import pallas as pl
from jax.experimental.pallas import tpu as pltpu
from jax.sharding import PartitionSpec as P

MESH = pl.DeviceIdType.MESH
F32 = jnp.float32
BF16 = jnp.bfloat16
LATENT = 512
WIDTH = 576
PAD = 640
SPAN = 64
SPANS = 32
TOKENS = 2048
PIECE = 16
HEADS = 16
ROWS = 2048
MODEL = 896
EPS = 1e-06
SCALE = 1.0 / math.sqrt(192.0)
FACTOR = SCALE * math.log2(math.e)
BLOCK = 256
BLOCKS = TOKENS // BLOCK
HALF = ROWS // 2
SUB = 512


def rope_rows():
    half = (WIDTH - LATENT) // 2
    freq = np.exp(np.float32(-math.log(10000.0)) * np.arange(half, dtype=np.float32) / np.float32(half))
    angle = np.arange(TOKENS, dtype=np.float32)[:, None] * freq.astype(np.float32)[None, :]
    cos, sin = np.cos(angle.astype(np.float64)), np.sin(angle.astype(np.float64))
    both = np.concatenate([cos, cos, -sin, sin], axis=1).astype(np.float32)
    return np.ascontiguousarray(both.reshape(SPANS, 4, PIECE, 128).transpose(1, 0, 2, 3))


def nt_dot(left, right):
    return lax.dot_general(left, right, (((1,), (1,)), ((), ())), preferred_element_type=F32)


def rem4(value):
    return lax.rem(value, 4)


class Place:
    def __init__(self):
        ctx, head = lax.axis_index("ctx"), lax.axis_index("head")
        self.ctx, self.head = ctx, head
        self.core = lax.rem(ctx, 2)
        self.x = lax.div(head, 2)
        self.y_lo = lax.rem(head, 2)
        self.y_hi = lax.rem(lax.div(ctx, 2), 2)
        self.y = self.y_hi * 2 + self.y_lo
        self.z = lax.div(ctx, 4)
        self.a1 = self.pick(self.x, self.y)
        self.a2 = self.pick(self.y, self.z)
        self.a3 = self.pick(self.z, self.x)
        self.twin_a3 = self.pick(self.x, self.z)

    def pick(self, first, second):
        return first + self.core * (second - first)

    def device(self, x, y, z, core):
        return (z * 4 + lax.div(y, 2) * 2 + core, x * 2 + lax.rem(y, 2))

    def shifted(self, dx, dy, dz):
        return self.device(rem4(self.x + dx), rem4(self.y + dy), rem4(self.z + dz), self.core)

    def in_plane(self, d2, d1):
        return self.shifted(d1 * (1 - self.core), self.pick(d2, d1), d2 * self.core)

    def across(self, d3):
        return self.shifted(d3 * self.core, 0, d3 * (1 - self.core))

    def beside(self, d):
        return self.shifted(d * self.core, self.pick(2, 5 - 2 * self.y_lo), d * (1 - self.core))

    def twin(self):
        return self.device(self.x, self.y, self.z, 1 - self.core)


def remote(src, dst, send_sem, recv_sem, device):
    return pltpu.make_async_remote_copy(
        src_ref=src, dst_ref=dst, send_sem=send_sem, recv_sem=recv_sem, device_id=device, device_id_type=MESH
    )


def swap_halves(tail):
    lane = lax.broadcasted_iota(jnp.int32, tail.shape, 1)
    return jnp.where(lane < 32, pltpu.roll(tail, 96, 1), pltpu.roll(tail, 32, 1))


def block_rows(block):
    return pl.ds(pl.multiple_of(block * BLOCK, BLOCK), BLOCK)


PLANE_SHIFTS = [(d2, d1) for d2 in range(4) for d1 in range(4) if d2 or d1]

SUM_RAW = 0
KEYS_PLANE = 7
KEYS_ACROSS = 22
KEYS_TWIN = 34
HIDDEN = 38
HIDDEN_TWIN = 45
GRADS_TWIN = 46
GRADS_ACROSS = 50
GRADS_PLANE = 53
ROWS_PLANE = 68
ROWS_ACROSS = 83
ROWS_TWIN = 95
GAIN_PLANE = 99
GAIN_ACROSS = 114
GAIN_TWIN = 117
SEMAPHORES = 118


def whole_kernel(
    hidden_in,
    kv_in,
    gain,
    rope,
    queries,
    grads,
    span,
    query_out,
    gain_out,
    hidden_grad,
    down_grad,
    hidden,
    kv_turned,
    hidden_rows,
    part,
    landed,
    raw_rows,
    rope_part,
    angles,
    rows,
    keys_t,
    query_cols,
    grad_rows,
    bias,
    scores,
    prob_grads,
    tops,
    masses,
    dots,
    weights,
    score_grads,
    key_total,
    twin_in,
    packed,
    from_near,
    from_far,
    from_plane,
    back_rows,
    gains,
    gain_plane,
    gain_across,
    gain_twin,
    send,
    recv,
    local,
):
    place = Place()
    core, a1, a2, a3 = place.core, place.a1, place.a2, place.a3
    twin = place.twin()
    devices = [place.in_plane(d2, d1) for d2, d1 in PLANE_SHIFTS]
    devices += [place.across(d) for d in (1, 2, 3)] + [place.beside(d) for d in (1, 2, 3)] + [twin]
    barrier = pltpu.get_barrier_semaphore()
    for device in devices:
        pl.semaphore_signal(barrier, inc=1, device_id=device, device_id_type=MESH)

    inputs = [pltpu.make_async_copy(hidden_in, hidden, local.at[4]), pltpu.make_async_copy(kv_in, kv_turned, local.at[6])]
    for copy in inputs:
        copy.start()

    sent = []

    def copy_of(src, dst, slot, device):
        return remote(src, dst, send.at[slot], recv.at[slot], device)

    def go(src, dst, slot, device):
        copy = copy_of(src, dst, slot, device)
        copy.start()
        sent.append(copy)
        return copy

    def later(src, dst, slot, device):
        copy = copy_of(src, dst, slot, device)
        sent.append(copy)
        return copy

    fetched = [
        pltpu.make_async_copy(queries.at[h], query_cols.at[:, pl.ds(h * 128, 128)], local.at[0]) for h in range(HEADS)
    ]
    for copy in fetched:
        copy.start()
    raw_grads = score_grads.at[:, pl.ds(0, LATENT)]
    grads_fetch = pltpu.make_async_copy(grads, raw_grads, local.at[1])
    grads_fetch.start()

    def hidden_parts():
        first = 2 * place.y_hi
        by_core = [[(hidden.at[:, k], hidden_rows.at[0, place.z, first + k]) for k in range(2)]]
        by_core.append([(hidden.at[k], hidden_rows.at[1, k, place.z, pl.ds(first, 2)]) for k in range(4)])
        return by_core

    rope_fetch = pltpu.make_async_copy(rope.at[rem4(place.head)], rope_part, local.at[5])
    rope_fetch.start()

    for copy in inputs:
        copy.wait()

    product = nt_dot(hidden[...].reshape(128, MODEL), kv_turned[...])
    part[:, :, :WIDTH] = product.reshape(8, PIECE, WIDTH)
    part[:, :, WIDTH:] = jnp.zeros((8, PIECE, PAD - WIDTH), F32)
    landed[place.head] = part[place.head]
    pl.semaphore_wait(barrier, len(devices))
    raw_copies = []
    for d in range(1, 8):
        other = lax.rem(place.head + d, 8)
        raw_copies.append(go(part.at[other], landed.at[place.head], SUM_RAW + d - 1, (place.ctx, other)))

    for owner, parts in enumerate(hidden_parts()):

        @pl.when(core == owner)
        def _(parts=parts):
            copies = [pltpu.make_async_copy(src, dst, local.at[2]) for src, dst in parts]
            for copy in copies:
                copy.start()
            for copy in copies:
                copy.wait()

    token = lax.broadcasted_iota(jnp.int32, (1, 128), 1)
    query_pos = jnp.where(token < SPAN, span[2 * place.ctx] * SPAN, span[2 * place.ctx + 1] * SPAN) + lax.rem(token, SPAN)
    seen_from = query_pos - lax.broadcasted_iota(jnp.int32, (PIECE, 128), 0)
    starts = [span[slot] * SPAN for slot in range(SPANS)]
    for owner in range(2):
        for index in range(64):
            at3, at2, at1 = index // 16, index // 4 % 4, index % 4
            x, y, z = ((at1, at2, at3), (at3, at1, at2))[owner]
            head = x * 2 + y % 2
            start = starts[(z * 4 + y // 2 * 2 + owner) * 2 + head // 4] + head % 4 * PIECE
            bias[pl.ds((owner * 64 + index) * PIECE, PIECE), :] = jnp.where(seen_from >= start, 0.0, -1e30)
    rope_fetch.wait()
    mine = span[2 * place.ctx + lax.div(place.head, 4)]
    both = jnp.zeros((PIECE, 128), F32)
    for k in range(SPANS):
        both = jnp.where(mine == k, rope_part[k], both)
    lane = lax.broadcasted_iota(jnp.int32, (PIECE, 128), 1)
    angles[0] = jnp.where(lane < 64, both, 0.0)
    angles[1] = jnp.where(lane < 64, pltpu.roll(both, 64, 1), 0.0)
    to = lax.broadcasted_iota(jnp.int32, (256, 256), 0)
    at = lax.broadcasted_iota(jnp.int32, (256, 256), 1)
    swap = (lax.div(to, 16) == lax.rem(at, 16)) & (lax.rem(to, 16) == lax.div(at, 16))
    swap = jnp.where(swap, 1.0, 0.0).astype(BF16)
    grads_fetch.wait()

    def order_grads(index, carry):
        here = pl.ds(pl.multiple_of(index * 256, 256), 256)
        turned = jnp.dot(swap, score_grads[here, :LATENT], preferred_element_type=F32).astype(BF16)
        for h in range(HEADS):
            to_rows = pl.ds(pl.multiple_of(h * 128 + index * 16, 16), 16)
            grad_rows[to_rows, :] = turned[h * 16 : (h + 1) * 16, :]
        return carry

    lax.fori_loop(0, 8, order_grads, 0)

    for copy in raw_copies:
        copy.wait_recv()
    raw = landed[0]
    for k in range(1, 8):
        raw = raw + landed[k]
    raw_rows[...] = raw
    latent, tail = raw[:, :LATENT], raw[:, LATENT:]
    inv_rms = lax.rsqrt(jnp.mean(latent * latent, axis=1, keepdims=True) + EPS)
    turned = tail * angles[0] + swap_halves(tail) * angles[1]
    rows[core, a3, a2, a1, :, :LATENT] = (latent * inv_rms * gain[...]).astype(BF16)
    rows[core, a3, a2, a1, :, LATENT:] = turned.astype(BF16)

    before, after, opposite = rem4(a3 + 3), rem4(a3 + 1), rem4(a3 + 2)
    twin_a3 = place.twin_a3
    own_planes = [a3, before, after, opposite]
    twin_planes = [twin_a3, rem4(twin_a3 + 3), rem4(twin_a3 + 1), rem4(twin_a3 + 2)]

    def spread(ref, plane_sem, across_sem, twin_sem):
        piece = ref.at[core, a3, a2, a1]
        copies = [go(piece, piece, plane_sem + k, place.in_plane(*d)) for k, d in enumerate(PLANE_SHIFTS)]

        def rest():
            across = {d: [] for d in (1, 2, 3)}
            for r in (0, 1, 3, 2):
                for copy, (d2, _) in zip(copies, PLANE_SHIFTS):
                    if (d2 + r) % 4 == 0:
                        copy.wait_recv()
                line = ref.at[core, a3, rem4(a2 + r)]
                for d in (1, 3, 2):
                    make = later if d == 2 else go
                    across[d].append(make(line, line, across_sem + 4 * (d - 1) + r, place.across(d)))
            plane = ref.at[core, a3]
            pairs = [go(plane, plane, twin_sem, twin)]
            for k in (1, 2, 3):
                plane = ref.at[core, own_planes[k]]
                pairs.append(later(plane, plane, twin_sem + k, twin))

            def arrive(step):
                if step == 1:
                    pairs[0].wait_recv()
                    for copy in across[2]:
                        copy.start()
                if step in (2, 3, 6):
                    k = {2: 1, 3: 2, 6: 3}[step]
                    for copy in across[{1: 1, 2: 3, 3: 2}[k]]:
                        copy.wait_recv()
                    pairs[k].start()
                if step in (4, 5, 7):
                    pairs[{4: 1, 5: 2, 7: 3}[step]].wait_recv()

            return arrive

        return rest

    def plane_of(step):
        by_step = [(0, 0), (1, 0), (0, 3), (0, 1), (1, 3), (1, 1), (0, 2), (1, 2)]
        owner, shift = 0, 0
        for k, (twins, d) in enumerate(by_step):
            here = jnp.where(step == k, 1, 0)
            owner, shift = owner + here * twins, shift + here * d
        base = a3 + owner * (twin_a3 - a3)
        return core + owner * (1 - 2 * core), rem4(base + shift)

    arrive = spread(rows, KEYS_PLANE, KEYS_ACROSS, KEYS_TWIN)()
    for copy in fetched:
        copy.wait()

    def score_block(owner, plane, half):
        block = owner * 4 + plane
        here, one = block_rows(block), pl.ds(block, 1)
        keys = rows[owner, plane].reshape(BLOCK, PAD)
        seen = bias[here, :]
        seen = jnp.concatenate([seen] * (SUB // 128), axis=1)
        for k in range(HALF // SUB):
            first = half * HALF + k * SUB
            at = pl.ds(k * SUB, SUB)
            score = jnp.dot(keys[:, :WIDTH], query_cols[:, first : first + SUB], preferred_element_type=F32) + seen
            prob_grad = nt_dot(keys[:, :LATENT], grad_rows[first : first + SUB, :])
            top = jnp.max(score, axis=0, keepdims=True)
            weight = jnp.exp2((score - top) * FACTOR)
            scores[here, at] = weight
            prob_grads[here, at] = prob_grad
            tops[one, at] = top
            masses[one, at] = jnp.sum(weight, axis=0, keepdims=True)
            dots[one, at] = jnp.sum(weight * prob_grad, axis=0, keepdims=True)

    def finish_half(half):
        top = jnp.max(tops[...], axis=0, keepdims=True)
        level = jnp.exp2((tops[...] - top) * FACTOR)
        share = 1.0 / jnp.sum(level * masses[...], axis=0, keepdims=True)
        delta = jnp.sum(level * dots[...], axis=0, keepdims=True) * share
        tops[...] = level * share
        dots[...] = jnp.broadcast_to(delta, dots.shape)

        def grad_step(block, carry):
            here = block_rows(block)
            probability = scores[here, :] * tops[pl.ds(block, 1), :]
            weights[lax.div(block, 4), rem4(block)] = probability.astype(BF16).reshape(4, 4, PIECE, HALF)
            score_grad = probability * (prob_grads[here, :] - dots[pl.ds(0, 1), :])
            score_grads[here, half * HALF : (half + 1) * HALF] = score_grad.astype(BF16)
            return carry

        lax.fori_loop(0, BLOCKS, grad_step, 0)

    def key_terms(owner, plane, half):
        columns = slice(half * HALF, (half + 1) * HALF)
        here = block_rows(owner * 4 + plane)
        by_score = nt_dot(score_grads[here, columns], query_cols[:, columns]) * SCALE
        by_value = jnp.dot(
            weights[owner, plane].reshape(BLOCK, HALF), grad_rows[columns, :], preferred_element_type=F32
        )
        return by_score[:, :LATENT] + by_value, by_score[:, LATENT:]

    def first_score_step(step, carry):
        for k in range(1, 8):

            @pl.when(step == k)
            def _(k=k):
                arrive(k)

        owner, plane = plane_of(step)
        keys_t[:, block_rows(owner * 4 + plane)] = rows[owner, plane].reshape(BLOCK, PAD).T
        score_block(owner, plane, 0)
        return carry

    lax.fori_loop(0, BLOCKS, first_score_step, 0)

    hidden_copies = []
    for k in range(7):
        dz, flip = (k + 1) // 2, (k + 1) % 2
        device = place.shifted(0, 2 * flip, dz)
        for owner, parts in enumerate(hidden_parts()):

            @pl.when(core == owner)
            def _(parts=parts, k=k, device=device):
                for src, dst in parts:
                    copy_of(src, dst, HIDDEN + k, device).start()

        like = hidden_rows.at[0, 0, pl.ds(0, 2)]
        hidden_copies.append(later(like, like, HIDDEN + k, device))

    finish_half(0)

    def first_key_step(block, carry):
        owner, plane = lax.div(block, 4), rem4(block)
        latent_term, rope_term = key_terms(owner, plane, 0)
        key_total[owner, plane, :, :, :, :LATENT] = latent_term.reshape(4, 4, PIECE, LATENT)
        key_total[owner, plane, :, :, :, LATENT:WIDTH] = rope_term.reshape(4, 4, PIECE, WIDTH - LATENT)
        key_total[owner, plane, :, :, :, WIDTH:] = jnp.zeros((4, 4, PIECE, PAD - WIDTH), F32)
        return carry

    lax.fori_loop(0, BLOCKS, first_key_step, 0)

    def second_score_step(block, carry):
        score_block(lax.div(block, 4), rem4(block), 1)
        return carry

    lax.fori_loop(0, BLOCKS, second_score_step, 0)
    finish_half(1)

    def second_key(owner, plane):
        latent_term, rope_term = key_terms(owner, plane, 1)
        key_total[owner, plane, :, :, :, :LATENT] += latent_term.reshape(4, 4, PIECE, LATENT)
        key_total[owner, plane, :, :, :, LATENT:WIDTH] += rope_term.reshape(4, 4, PIECE, WIDTH - LATENT)

    pairs, across = [], []
    for k, d in enumerate((2, 1, 3, 0)):
        plane = rem4(twin_a3 + d)
        pairs.append(later(key_total.at[1 - core, plane], twin_in.at[plane], GRADS_TWIN + k, twin))
    across.append(later(packed, from_far, GRADS_ACROSS, place.across(2)))
    for k, d in ((1, 1), (2, 3)):
        src = key_total.at[core, rem4(a3 + d)]
        across.append(later(src, from_near.at[k - 1], GRADS_ACROSS + k, place.across(d)))
    twins_turn = (1, 1, 0, 1, 0, 1, 0, 0)
    turn_shift = (2, 1, 2, 3, 1, 0, 3, 0)

    def second_key_step(step, carry):
        twins, shift = 0, 0
        for k in range(BLOCKS):
            here = jnp.where(step == k, 1, 0)
            twins, shift = twins + here * twins_turn[k], shift + here * turn_shift[k]
        owner = core + twins * (1 - 2 * core)
        plane = rem4(a3 + twins * (twin_a3 - a3) + shift)
        second_key(owner, plane)
        for k in range(BLOCKS):
            turn = (2, 1, 3, 0).index(turn_shift[k])

            @pl.when(step == k)
            def _(k=k, turn=turn):
                if twins_turn[k]:
                    pairs[turn].start()
                else:
                    pairs[turn].wait_recv()

        @pl.when(twins == 0)
        def _():
            for at2 in range(4):
                key_total[core, plane, at2] = key_total[core, plane, at2] + twin_in[plane, at2]

        @pl.when(step == 2)
        def _():
            packed[...] = key_total[core, plane].astype(BF16)
            across[0].start()

        for k, turn in ((4, 1), (6, 2)):

            @pl.when(step == k)
            def _(turn=turn):
                across[turn].start()

        return carry

    lax.fori_loop(0, BLOCKS, second_key_step, 0)
    for copy in hidden_copies:
        copy.wait_recv()
    hidden_to_twin = go(hidden_rows.at[core], hidden_rows.at[core], HIDDEN_TWIN, twin)

    query_copies = []
    for k in range(4):
        columns = slice(k * SUB, (k + 1) * SUB)
        total = jnp.dot(keys_t[:WIDTH, :], score_grads[:, columns], preferred_element_type=F32)
        query_cols[:, columns] = (total * SCALE).astype(BF16)
        for h in range(4 * k, 4 * k + 4):
            copy = pltpu.make_async_copy(query_cols.at[:, pl.ds(h * 128, 128)], query_out.at[h], local.at[3])
            copy.start()
            query_copies.append(copy)

    for copy in across:
        copy.wait_recv()

    def add_across(at2, carry):
        total = key_total[core, a3, at2] + from_near[0, at2] + from_near[1, at2]
        key_total[core, a3, at2] = total + from_far[at2].astype(F32)
        return carry

    lax.fori_loop(0, 4, add_across, 0)
    plane_copies = []
    for k, (d2, d1) in enumerate(PLANE_SHIFTS):
        src = key_total.at[core, a3, rem4(a2 + d2), rem4(a1 + d1)]
        plane_copies.append(go(src, from_plane.at[k], GRADS_PLANE + k, place.in_plane(d2, d1)))
    raw = raw_rows[...]
    latent = raw[:, :LATENT]
    inv_rms = lax.rsqrt(jnp.mean(latent * latent, axis=1, keepdims=True) + EPS)
    cube = inv_rms * inv_rms * inv_rms
    for copy in plane_copies:
        copy.wait_recv()
    key_grad = key_total[core, a3, a2, a1]
    for k in range(15):
        key_grad = key_grad + from_plane[k]
    latent_grad, tail = key_grad[:, :LATENT], key_grad[:, LATENT:]
    scaled = latent_grad * gain[...]
    latent_back = inv_rms * scaled - latent * cube * jnp.mean(scaled * latent, axis=1, keepdims=True)
    rope_back = tail * angles[0] - swap_halves(tail) * angles[1]
    back_rows[core, a3, a2, a1, :, :LATENT] = latent_back.astype(BF16)
    back_rows[core, a3, a2, a1, :, LATENT:] = rope_back.astype(BF16)
    spread_rest = spread(back_rows, ROWS_PLANE, ROWS_ACROSS, ROWS_TWIN)

    term = jnp.broadcast_to(jnp.sum(latent_grad * latent * inv_rms, axis=0, keepdims=True), (8, LATENT))
    gains[0] = term
    gain_plane[a2, a1] = term
    gain_copies = [
        go(gains.at[0], gain_plane.at[a2, a1], GAIN_PLANE + k, place.in_plane(*d)) for k, d in enumerate(PLANE_SHIFTS)
    ]
    hidden_to_twin.wait_recv()
    arrive_back = spread_rest()
    for copy in gain_copies:
        copy.wait_recv()
    term = gain_plane[0, 0]
    for k in range(1, 16):
        term = term + gain_plane[k // 4, k % 4]
    gains[1] = term
    gain_across[a3] = term
    gain_copies = [go(gains.at[1], gain_across.at[a3], GAIN_ACROSS + d - 1, place.across(d)) for d in (1, 2, 3)]
    last = later(gains.at[2], gain_twin.at[core], GAIN_TWIN, twin)
    down_grad[...] = jnp.zeros_like(down_grad)

    def down_step(step, carry):
        @pl.when(step == 4)
        def _():
            for copy in gain_copies:
                copy.wait_recv()
            term = gain_across[0] + gain_across[1] + gain_across[2] + gain_across[3]
            gains[2] = term
            gain_twin[core] = term
            last.start()

        @pl.when(step == BLOCKS - 1)
        def _():
            mine = []
            for head in range(8):
                x, y = head // 2, place.y_hi * 2 + head % 2
                mine.append(back_rows[core, place.pick(place.z, x), place.pick(y, place.z), place.pick(x, y)])
            mine = jnp.concatenate(mine, axis=0)
            hidden_grad[...] = jnp.dot(mine[:, :WIDTH], kv_turned[...], preferred_element_type=F32).astype(BF16)

        for k in range(1, 8):

            @pl.when(step == k)
            def _(k=k):
                arrive_back(k)

        owner, plane = plane_of(step)
        turned = back_rows[owner, plane].reshape(BLOCK, PAD).T
        down_grad[...] += jnp.dot(
            turned[:WIDTH], hidden_rows[owner, plane].reshape(BLOCK, MODEL), preferred_element_type=F32
        )
        return carry

    lax.fori_loop(0, BLOCKS, down_step, 0)
    last.wait_recv()
    gain_out[...] = (gain_twin[0] + gain_twin[1])[:1]
    for copy in query_copies:
        copy.wait()
    for copy in sent:
        copy.wait_send()


def whole(hidden, kv_turned, gain, rope, queries, grads, span_table):
    vmem = pl.BlockSpec(memory_space=pltpu.VMEM)
    smem = pl.BlockSpec(memory_space=pltpu.SMEM)
    anywhere = pl.BlockSpec(memory_space=pl.ANY)
    pieces = (2, 4, 4, 4, PIECE)
    return pl.pallas_call(
        whole_kernel,
        out_shape=(
            jax.ShapeDtypeStruct((HEADS, WIDTH, 128), BF16),
            jax.ShapeDtypeStruct((1, LATENT), F32),
            jax.ShapeDtypeStruct((128, MODEL), BF16),
            jax.ShapeDtypeStruct((WIDTH, MODEL), F32),
        ),
        in_specs=[anywhere, anywhere, vmem, anywhere, anywhere, anywhere, smem],
        out_specs=(anywhere, vmem, vmem, vmem),
        scratch_shapes=[
            pltpu.VMEM(hidden.shape, BF16),
            pltpu.VMEM(kv_turned.shape, BF16),
            pltpu.VMEM(pieces + (MODEL,), BF16),
            pltpu.VMEM((8, PIECE, PAD), F32),
            pltpu.VMEM((8, PIECE, PAD), F32),
            pltpu.VMEM((PIECE, PAD), F32),
            pltpu.VMEM((SPANS, PIECE, 128), F32),
            pltpu.VMEM((2, PIECE, 128), F32),
            pltpu.VMEM(pieces + (PAD,), BF16),
            pltpu.VMEM((PAD, TOKENS), BF16),
            pltpu.VMEM((WIDTH, ROWS), BF16),
            pltpu.VMEM((ROWS, LATENT), BF16),
            pltpu.VMEM((TOKENS, 128), F32),
            pltpu.VMEM((TOKENS, HALF), F32),
            pltpu.VMEM((TOKENS, HALF), F32),
            pltpu.VMEM((BLOCKS, HALF), F32),
            pltpu.VMEM((BLOCKS, HALF), F32),
            pltpu.VMEM((BLOCKS, HALF), F32),
            pltpu.VMEM(pieces + (HALF,), BF16),
            pltpu.VMEM((TOKENS, ROWS), BF16),
            pltpu.VMEM(pieces + (PAD,), F32),
            pltpu.VMEM(pieces[1:] + (PAD,), F32),
            pltpu.VMEM((4, 4, PIECE, PAD), BF16),
            pltpu.VMEM((2, 4, 4, PIECE, PAD), F32),
            pltpu.VMEM((4, 4, PIECE, PAD), BF16),
            pltpu.VMEM((15, PIECE, PAD), F32),
            pltpu.VMEM(pieces + (PAD,), BF16),
            pltpu.VMEM((3, 8, LATENT), F32),
            pltpu.VMEM((4, 4, 8, LATENT), F32),
            pltpu.VMEM((4, 8, LATENT), F32),
            pltpu.VMEM((2, 8, LATENT), F32),
            pltpu.SemaphoreType.DMA((SEMAPHORES,)),
            pltpu.SemaphoreType.DMA((SEMAPHORES,)),
            pltpu.SemaphoreType.DMA((7,)),
        ],
        compiler_params=pltpu.CompilerParams(
            collective_id=0, has_side_effects=True, vmem_limit_bytes=64 * 2**20 - 2**18
        ),
    )(hidden, kv_turned, gain, rope, queries, grads, span_table)


def hand_on_kernel(*refs):
    count = 4
    arrivals, departures = refs[-2:]
    steps = []
    for src, dst, held in zip(refs[:count], refs[count : 2 * count], refs[2 * count : 3 * count]):
        rows = src.shape[0]
        parts = 8 if rows == WIDTH else 16 if rows == HEADS else 1
        for k in range(parts):
            at, n = pl.ds(k * (rows // parts), rows // parts), len(steps)
            steps.append(
                (
                    pltpu.make_async_copy(src.at[at], held.at[at], arrivals.at[n]),
                    pltpu.make_async_copy(held.at[at], dst.at[at], departures.at[n]),
                )
            )
    for arrival, _ in steps:
        arrival.start()
    for arrival, departure in steps:
        arrival.wait()
        departure.start()
    for _, departure in steps:
        departure.wait()


def hand_on(*arrays):
    anywhere = pl.BlockSpec(memory_space=pl.ANY)
    return pl.pallas_call(
        hand_on_kernel,
        out_shape=tuple(jax.ShapeDtypeStruct(a.shape, a.dtype) for a in arrays),
        in_specs=[anywhere] * len(arrays),
        out_specs=(anywhere,) * len(arrays),
        scratch_shapes=[pltpu.VMEM(a.shape, a.dtype) for a in arrays] + [pltpu.SemaphoreType.DMA((26,))] * 2,
        compiler_params=pltpu.CompilerParams(vmem_limit_bytes=63 * 2**20),
    )(*arrays)


def per_device(table, hidden, kv_down, kv_gain, queries, out_grad, span_table):
    query_grad, gain_grad, hidden_grad, down_grad = whole(
        hidden.reshape(4, 2, PIECE, MODEL),
        kv_down.T,
        kv_gain.reshape(1, LATENT),
        table,
        queries.transpose(1, 2, 0),
        out_grad.reshape(ROWS, LATENT),
        span_table,
    )
    query_grad, gain_grad, hidden_grad, down_grad = hand_on(query_grad, gain_grad, hidden_grad, down_grad)
    return (query_grad.transpose(2, 0, 1), hidden_grad, down_grad.T, gain_grad[0])


def solution(mesh):
    table = rope_rows()

    def run(hidden, kv_down, kv_gain, queries, out_grad, span_table):
        return jax.shard_map(
            per_device,
            mesh=mesh,
            in_specs=(
                P(),
                P("ctx", "head"),
                P("head", None),
                P(),
                P("ctx", "head", None),
                P("ctx", "head", None),
                P(),
            ),
            out_specs=(P("ctx", "head", None), P("ctx", "head"), P("head", None), P()),
            check_vma=False,
        )(jnp.asarray(table), hidden, kv_down, kv_gain, queries, out_grad, span_table)

    return run
```

```python
import functools
import math

import jax
import jax.numpy as jnp
import numpy as np
from jax import lax
from jax.experimental import pallas as pl
from jax.experimental.pallas import tpu as pltpu
from jax.sharding import PartitionSpec as P

MESH = pl.DeviceIdType.MESH
F32 = jnp.float32
BF16 = jnp.bfloat16
LATENT = 512
WIDTH = 576
PAD = 640
SPAN = 64
SPANS = 32
TOKENS = 2048
PIECE = 16
HEADS = 16
ROWS = 2048
MODEL = 896
EPS = 1e-06
SCALE = 1.0 / math.sqrt(192.0)
FACTOR = SCALE * math.log2(math.e)
BLOCK = 256
BLOCKS = TOKENS // BLOCK
HALF = ROWS // 2
SUB = 512


def rope_rows():
    half = (WIDTH - LATENT) // 2
    freq = np.exp(np.float32(-math.log(10000.0)) * np.arange(half, dtype=np.float32) / np.float32(half))
    angle = np.arange(TOKENS, dtype=np.float32)[:, None] * freq.astype(np.float32)[None, :]
    cos, sin = np.cos(angle.astype(np.float64)), np.sin(angle.astype(np.float64))
    both = np.concatenate([cos, cos, -sin, sin], axis=1).astype(np.float32)
    return np.ascontiguousarray(both.reshape(SPANS, 4, PIECE, 128).transpose(1, 0, 2, 3))


def nt_dot(left, right):
    return lax.dot_general(left, right, (((1,), (1,)), ((), ())), preferred_element_type=F32)


def rem4(value):
    return lax.rem(value, 4)


class Place:
    def __init__(self):
        ctx, head = lax.axis_index("ctx"), lax.axis_index("head")
        self.ctx, self.head = ctx, head
        self.core = lax.rem(ctx, 2)
        self.x = lax.div(head, 2)
        self.y_lo = lax.rem(head, 2)
        self.y_hi = lax.rem(lax.div(ctx, 2), 2)
        self.y = self.y_hi * 2 + self.y_lo
        self.z = lax.div(ctx, 4)
        self.a1 = self.pick(self.x, self.y)
        self.a2 = self.pick(self.y, self.z)
        self.a3 = self.pick(self.z, self.x)
        self.twin_a3 = self.pick(self.x, self.z)

    def pick(self, first, second):
        return first + self.core * (second - first)

    def device(self, x, y, z, core):
        return (z * 4 + lax.div(y, 2) * 2 + core, x * 2 + lax.rem(y, 2))

    def shifted(self, dx, dy, dz):
        return self.device(rem4(self.x + dx), rem4(self.y + dy), rem4(self.z + dz), self.core)

    def in_plane(self, d2, d1):
        return self.shifted(d1 * (1 - self.core), self.pick(d2, d1), d2 * self.core)

    def across(self, d3):
        return self.shifted(d3 * self.core, 0, d3 * (1 - self.core))

    def beside(self, d):
        return self.shifted(d * self.core, self.pick(2, 5 - 2 * self.y_lo), d * (1 - self.core))

    def twin(self):
        return self.device(self.x, self.y, self.z, 1 - self.core)


def remote(src, dst, send_sem, recv_sem, device):
    return pltpu.make_async_remote_copy(
        src_ref=src, dst_ref=dst, send_sem=send_sem, recv_sem=recv_sem, device_id=device, device_id_type=MESH
    )


def swap_halves(tail):
    lane = lax.broadcasted_iota(jnp.int32, tail.shape, 1)
    return jnp.where(lane < 32, pltpu.roll(tail, 96, 1), pltpu.roll(tail, 32, 1))


def block_rows(block):
    return pl.ds(pl.multiple_of(block * BLOCK, BLOCK), BLOCK)


PLANE_SHIFTS = [(d2, d1) for d2 in range(4) for d1 in range(4) if d2 or d1]

SUM_RAW = 0
KEYS_PLANE = 7
KEYS_ACROSS = 22
KEYS_TWIN = 34
HIDDEN = 38
HIDDEN_TWIN = 45
GRADS_TWIN = 46
GRADS_ACROSS = 50
GRADS_PLANE = 62
ROWS_PLANE = 77
ROWS_ACROSS = 92
ROWS_TWIN = 104
GAIN_PLANE = 108
GAIN_ACROSS = 123
GAIN_TWIN = 126
SEMAPHORES = 127


def whole_kernel(
    hidden_in,
    kv_in,
    gain,
    rope,
    queries,
    grads,
    span,
    query_out,
    gain_out,
    hidden_grad,
    down_grad,
    hidden,
    kv_turned,
    hidden_rows,
    part,
    landed,
    raw_rows,
    rope_part,
    angles,
    rows,
    keys_t,
    query_cols,
    grad_rows,
    bias,
    scores,
    prob_grads,
    tops,
    masses,
    dots,
    weights,
    score_grads,
    key_total,
    twin_in,
    packed,
    from_near,
    from_far,
    from_plane,
    back_rows,
    gains,
    gain_plane,
    gain_across,
    gain_twin,
    send,
    recv,
    local,
):
    place = Place()
    core, a1, a2, a3 = place.core, place.a1, place.a2, place.a3
    twin = place.twin()
    devices = [place.in_plane(d2, d1) for d2, d1 in PLANE_SHIFTS]
    devices += [place.across(d) for d in (1, 2, 3)] + [place.beside(d) for d in (1, 2, 3)] + [twin]
    barrier = pltpu.get_barrier_semaphore()
    for device in devices:
        pl.semaphore_signal(barrier, inc=1, device_id=device, device_id_type=MESH)

    inputs = [pltpu.make_async_copy(hidden_in, hidden, local.at[4]), pltpu.make_async_copy(kv_in, kv_turned, local.at[6])]
    for copy in inputs:
        copy.start()

    sent = []

    def copy_of(src, dst, slot, device):
        return remote(src, dst, send.at[slot], recv.at[slot], device)

    def go(src, dst, slot, device):
        copy = copy_of(src, dst, slot, device)
        copy.start()
        sent.append(copy)
        return copy

    def later(src, dst, slot, device):
        copy = copy_of(src, dst, slot, device)
        sent.append(copy)
        return copy

    fetched = [
        pltpu.make_async_copy(queries.at[h], query_cols.at[:, pl.ds(h * 128, 128)], local.at[0]) for h in range(HEADS)
    ]
    for copy in fetched:
        copy.start()
    raw_grads = score_grads.at[:, pl.ds(0, LATENT)]
    grads_fetch = pltpu.make_async_copy(grads, raw_grads, local.at[1])
    grads_fetch.start()

    def hidden_parts():
        first = 2 * place.y_hi
        by_core = [[(hidden.at[:, k], hidden_rows.at[0, place.z, first + k]) for k in range(2)]]
        by_core.append([(hidden.at[k], hidden_rows.at[1, k, place.z, pl.ds(first, 2)]) for k in range(4)])
        return by_core

    rope_fetch = pltpu.make_async_copy(rope.at[rem4(place.head)], rope_part, local.at[5])
    rope_fetch.start()

    for copy in inputs:
        copy.wait()

    product = nt_dot(hidden[...].reshape(128, MODEL), kv_turned[...])
    part[:, :, :WIDTH] = product.reshape(8, PIECE, WIDTH)
    part[:, :, WIDTH:] = jnp.zeros((8, PIECE, PAD - WIDTH), F32)
    landed[place.head] = part[place.head]
    pl.semaphore_wait(barrier, len(devices))
    raw_copies = []
    for d in range(1, 8):
        other = lax.rem(place.head + d, 8)
        raw_copies.append(go(part.at[other], landed.at[place.head], SUM_RAW + d - 1, (place.ctx, other)))

    for owner, parts in enumerate(hidden_parts()):

        @pl.when(core == owner)
        def _(parts=parts):
            copies = [pltpu.make_async_copy(src, dst, local.at[2]) for src, dst in parts]
            for copy in copies:
                copy.start()
            for copy in copies:
                copy.wait()

    token = lax.broadcasted_iota(jnp.int32, (1, 128), 1)
    query_pos = jnp.where(token < SPAN, span[2 * place.ctx] * SPAN, span[2 * place.ctx + 1] * SPAN) + lax.rem(token, SPAN)
    seen_from = query_pos - lax.broadcasted_iota(jnp.int32, (PIECE, 128), 0)
    starts = [span[slot] * SPAN for slot in range(SPANS)]
    for owner in range(2):
        for index in range(64):
            at3, at2, at1 = index // 16, index // 4 % 4, index % 4
            x, y, z = ((at1, at2, at3), (at3, at1, at2))[owner]
            head = x * 2 + y % 2
            start = starts[(z * 4 + y // 2 * 2 + owner) * 2 + head // 4] + head % 4 * PIECE
            bias[pl.ds((owner * 64 + index) * PIECE, PIECE), :] = jnp.where(seen_from >= start, 0.0, -1e30)
    rope_fetch.wait()
    mine = span[2 * place.ctx + lax.div(place.head, 4)]
    both = jnp.zeros((PIECE, 128), F32)
    for k in range(SPANS):
        both = jnp.where(mine == k, rope_part[k], both)
    lane = lax.broadcasted_iota(jnp.int32, (PIECE, 128), 1)
    angles[0] = jnp.where(lane < 64, both, 0.0)
    angles[1] = jnp.where(lane < 64, pltpu.roll(both, 64, 1), 0.0)
    to = lax.broadcasted_iota(jnp.int32, (256, 256), 0)
    at = lax.broadcasted_iota(jnp.int32, (256, 256), 1)
    swap = (lax.div(to, 16) == lax.rem(at, 16)) & (lax.rem(to, 16) == lax.div(at, 16))
    swap = jnp.where(swap, 1.0, 0.0).astype(BF16)
    grads_fetch.wait()

    def order_grads(index, carry):
        here = pl.ds(pl.multiple_of(index * 256, 256), 256)
        turned = jnp.dot(swap, score_grads[here, :LATENT], preferred_element_type=F32).astype(BF16)
        for h in range(HEADS):
            to_rows = pl.ds(pl.multiple_of(h * 128 + index * 16, 16), 16)
            grad_rows[to_rows, :] = turned[h * 16 : (h + 1) * 16, :]
        return carry

    lax.fori_loop(0, 8, order_grads, 0)

    for copy in raw_copies:
        copy.wait_recv()
    raw = landed[0]
    for k in range(1, 8):
        raw = raw + landed[k]
    raw_rows[...] = raw
    latent, tail = raw[:, :LATENT], raw[:, LATENT:]
    inv_rms = lax.rsqrt(jnp.mean(latent * latent, axis=1, keepdims=True) + EPS)
    turned = tail * angles[0] + swap_halves(tail) * angles[1]
    rows[core, a3, a2, a1, :, :LATENT] = (latent * inv_rms * gain[...]).astype(BF16)
    rows[core, a3, a2, a1, :, LATENT:] = turned.astype(BF16)

    before, after, opposite = rem4(a3 + 3), rem4(a3 + 1), rem4(a3 + 2)
    twin_a3 = place.twin_a3
    own_planes = [a3, before, after, opposite]
    twin_planes = [twin_a3, rem4(twin_a3 + 3), rem4(twin_a3 + 1), rem4(twin_a3 + 2)]

    def spread(ref, plane_sem, across_sem, twin_sem):
        piece = ref.at[core, a3, a2, a1]
        copies = [go(piece, piece, plane_sem + k, place.in_plane(*d)) for k, d in enumerate(PLANE_SHIFTS)]

        def rest():
            across = {d: [] for d in (1, 2, 3)}
            for r in (0, 1, 3, 2):
                for copy, (d2, _) in zip(copies, PLANE_SHIFTS):
                    if (d2 + r) % 4 == 0:
                        copy.wait_recv()
                line = ref.at[core, a3, rem4(a2 + r)]
                for d in (1, 3, 2):
                    make = later if d == 2 else go
                    across[d].append(make(line, line, across_sem + 4 * (d - 1) + r, place.across(d)))
            plane = ref.at[core, a3]
            pairs = [go(plane, plane, twin_sem, twin)]
            for k in (1, 2, 3):
                plane = ref.at[core, own_planes[k]]
                pairs.append(later(plane, plane, twin_sem + k, twin))

            def arrive(step):
                if step == 1:
                    pairs[0].wait_recv()
                    for copy in across[2]:
                        copy.start()
                if step in (2, 3, 6):
                    k = {2: 1, 3: 2, 6: 3}[step]
                    for copy in across[{1: 1, 2: 3, 3: 2}[k]]:
                        copy.wait_recv()
                    pairs[k].start()
                if step in (4, 5, 7):
                    pairs[{4: 1, 5: 2, 7: 3}[step]].wait_recv()

            return arrive

        return rest

    def plane_of(step):
        by_step = [(0, 0), (1, 0), (0, 3), (0, 1), (1, 3), (1, 1), (0, 2), (1, 2)]
        owner, shift = 0, 0
        for k, (twins, d) in enumerate(by_step):
            here = jnp.where(step == k, 1, 0)
            owner, shift = owner + here * twins, shift + here * d
        base = a3 + owner * (twin_a3 - a3)
        return core + owner * (1 - 2 * core), rem4(base + shift)

    arrive = spread(rows, KEYS_PLANE, KEYS_ACROSS, KEYS_TWIN)()
    for copy in fetched:
        copy.wait()

    def score_block(owner, plane, half):
        block = owner * 4 + plane
        here, one = block_rows(block), pl.ds(block, 1)
        keys = rows[owner, plane].reshape(BLOCK, PAD)
        seen = bias[here, :]
        seen = jnp.concatenate([seen] * (SUB // 128), axis=1)
        for k in range(HALF // SUB):
            first = half * HALF + k * SUB
            at = pl.ds(k * SUB, SUB)
            score = jnp.dot(keys[:, :WIDTH], query_cols[:, first : first + SUB], preferred_element_type=F32) + seen
            prob_grad = nt_dot(keys[:, :LATENT], grad_rows[first : first + SUB, :])
            top = jnp.max(score, axis=0, keepdims=True)
            weight = jnp.exp2((score - top) * FACTOR)
            scores[here, at] = weight
            prob_grads[here, at] = prob_grad
            tops[one, at] = top
            masses[one, at] = jnp.sum(weight, axis=0, keepdims=True)
            dots[one, at] = jnp.sum(weight * prob_grad, axis=0, keepdims=True)

    def finish_half(half):
        top = jnp.max(tops[...], axis=0, keepdims=True)
        level = jnp.exp2((tops[...] - top) * FACTOR)
        share = 1.0 / jnp.sum(level * masses[...], axis=0, keepdims=True)
        delta = jnp.sum(level * dots[...], axis=0, keepdims=True) * share
        tops[...] = level * share
        dots[...] = jnp.broadcast_to(delta, dots.shape)

        def grad_step(block, carry):
            here = block_rows(block)
            probability = scores[here, :] * tops[pl.ds(block, 1), :]
            weights[lax.div(block, 4), rem4(block)] = probability.astype(BF16).reshape(4, 4, PIECE, HALF)
            score_grad = probability * (prob_grads[here, :] - dots[pl.ds(0, 1), :])
            score_grads[here, half * HALF : (half + 1) * HALF] = score_grad.astype(BF16)
            return carry

        lax.fori_loop(0, BLOCKS, grad_step, 0)

    def key_terms(owner, plane, half):
        columns = slice(half * HALF, (half + 1) * HALF)
        here = block_rows(owner * 4 + plane)
        by_score = nt_dot(score_grads[here, columns], query_cols[:, columns]) * SCALE
        by_value = jnp.dot(
            weights[owner, plane].reshape(BLOCK, HALF), grad_rows[columns, :], preferred_element_type=F32
        )
        return by_score[:, :LATENT] + by_value, by_score[:, LATENT:]

    def first_score_step(step, carry):
        for k in range(1, 8):

            @pl.when(step == k)
            def _(k=k):
                arrive(k)

        owner, plane = plane_of(step)
        keys_t[:, block_rows(owner * 4 + plane)] = rows[owner, plane].reshape(BLOCK, PAD).T
        score_block(owner, plane, 0)
        return carry

    lax.fori_loop(0, BLOCKS, first_score_step, 0)

    hidden_copies = []
    for k in range(7):
        dz, flip = (k + 1) // 2, (k + 1) % 2
        device = place.shifted(0, 2 * flip, dz)
        for owner, parts in enumerate(hidden_parts()):

            @pl.when(core == owner)
            def _(parts=parts, k=k, device=device):
                for src, dst in parts:
                    copy_of(src, dst, HIDDEN + k, device).start()

        like = hidden_rows.at[0, 0, pl.ds(0, 2)]
        hidden_copies.append(later(like, like, HIDDEN + k, device))

    finish_half(0)

    def first_key_step(block, carry):
        owner, plane = lax.div(block, 4), rem4(block)
        latent_term, rope_term = key_terms(owner, plane, 0)
        key_total[owner, plane, :, :, :, :LATENT] = latent_term.reshape(4, 4, PIECE, LATENT)
        key_total[owner, plane, :, :, :, LATENT:WIDTH] = rope_term.reshape(4, 4, PIECE, WIDTH - LATENT)
        key_total[owner, plane, :, :, :, WIDTH:] = jnp.zeros((4, 4, PIECE, PAD - WIDTH), F32)
        return carry

    lax.fori_loop(0, BLOCKS, first_key_step, 0)

    def second_score_step(block, carry):
        score_block(lax.div(block, 4), rem4(block), 1)
        return carry

    lax.fori_loop(0, BLOCKS, second_score_step, 0, unroll=2)
    finish_half(1)

    def second_key(owner, plane):
        latent_term, rope_term = key_terms(owner, plane, 1)
        key_total[owner, plane, :, :, :, :LATENT] += latent_term.reshape(4, 4, PIECE, LATENT)
        key_total[owner, plane, :, :, :, LATENT:WIDTH] += rope_term.reshape(4, 4, PIECE, WIDTH - LATENT)

    pairs, across = [], []
    for k, d in enumerate((2, 1, 3, 0)):
        plane = rem4(twin_a3 + d)
        pairs.append(later(key_total.at[1 - core, plane], twin_in.at[plane], GRADS_TWIN + k, twin))
    lines = (2, 1, 3, 0)
    for k, d in enumerate((2, 1, 3)):
        by_line = []
        for r in lines:
            line = rem4(a2 + r)
            src = packed.at[line] if k == 0 else key_total.at[core, rem4(a3 + d), line]
            dst = from_far.at[line] if k == 0 else from_near.at[k - 1, line]
            by_line.append(later(src, dst, GRADS_ACROSS + 4 * k + r, place.across(d)))
        across.append(by_line)
    twins_turn = (1, 1, 0, 1, 0, 1, 0, 0)
    turn_shift = (2, 1, 2, 3, 1, 0, 3, 0)

    def second_key_step(step, carry):
        twins, shift = 0, 0
        for k in range(BLOCKS):
            here = jnp.where(step == k, 1, 0)
            twins, shift = twins + here * twins_turn[k], shift + here * turn_shift[k]
        owner = core + twins * (1 - 2 * core)
        plane = rem4(a3 + twins * (twin_a3 - a3) + shift)
        second_key(owner, plane)
        for k in range(BLOCKS):
            turn = (2, 1, 3, 0).index(turn_shift[k])

            @pl.when(step == k)
            def _(k=k, turn=turn):
                if twins_turn[k]:
                    pairs[turn].start()
                else:
                    pairs[turn].wait_recv()

        @pl.when(twins == 0)
        def _():
            for at2 in range(4):
                key_total[core, plane, at2] = key_total[core, plane, at2] + twin_in[plane, at2]

        @pl.when(step == 2)
        def _():
            packed[...] = key_total[core, plane].astype(BF16)
            for copy in across[0]:
                copy.start()

        for k, turn in ((4, 1), (6, 2)):

            @pl.when(step == k)
            def _(turn=turn):
                for copy in across[turn]:
                    copy.start()

        return carry

    lax.fori_loop(0, BLOCKS, second_key_step, 0)
    for copy in hidden_copies:
        copy.wait_recv()
    hidden_to_twin = go(hidden_rows.at[core], hidden_rows.at[core], HIDDEN_TWIN, twin)

    query_copies = []
    for k in range(4):
        columns = slice(k * SUB, (k + 1) * SUB)
        total = jnp.dot(keys_t[:WIDTH, :], score_grads[:, columns], preferred_element_type=F32)
        query_cols[:, columns] = (total * SCALE).astype(BF16)
        for h in range(4 * k, 4 * k + 4):
            copy = pltpu.make_async_copy(query_cols.at[:, pl.ds(h * 128, 128)], query_out.at[h], local.at[3])
            copy.start()
            query_copies.append(copy)

    plane_copies = []
    for k, r in enumerate(lines):
        line = rem4(a2 + r)
        for by_line in across:
            by_line[k].wait_recv()
        total = key_total[core, a3, line] + from_near[0, line] + from_near[1, line]
        key_total[core, a3, line] = total + from_far[line].astype(F32)
        for n, (d2, d1) in enumerate(PLANE_SHIFTS):
            if d2 == r:
                src = key_total.at[core, a3, line, rem4(a1 + d1)]
                plane_copies.append(go(src, from_plane.at[n], GRADS_PLANE + n, place.in_plane(d2, d1)))
    raw = raw_rows[...]
    latent = raw[:, :LATENT]
    inv_rms = lax.rsqrt(jnp.mean(latent * latent, axis=1, keepdims=True) + EPS)
    cube = inv_rms * inv_rms * inv_rms
    for copy in plane_copies:
        copy.wait_recv()
    key_grad = key_total[core, a3, a2, a1]
    for k in range(15):
        key_grad = key_grad + from_plane[k]
    latent_grad, tail = key_grad[:, :LATENT], key_grad[:, LATENT:]
    scaled = latent_grad * gain[...]
    latent_back = inv_rms * scaled - latent * cube * jnp.mean(scaled * latent, axis=1, keepdims=True)
    rope_back = tail * angles[0] - swap_halves(tail) * angles[1]
    back_rows[core, a3, a2, a1, :, :LATENT] = latent_back.astype(BF16)
    back_rows[core, a3, a2, a1, :, LATENT:] = rope_back.astype(BF16)
    spread_rest = spread(back_rows, ROWS_PLANE, ROWS_ACROSS, ROWS_TWIN)

    term = jnp.broadcast_to(jnp.sum(latent_grad * latent * inv_rms, axis=0, keepdims=True), (8, LATENT))
    gains[0] = term
    gain_plane[a2, a1] = term
    gain_copies = [
        go(gains.at[0], gain_plane.at[a2, a1], GAIN_PLANE + k, place.in_plane(*d)) for k, d in enumerate(PLANE_SHIFTS)
    ]
    hidden_to_twin.wait_recv()
    arrive_back = spread_rest()
    for copy in gain_copies:
        copy.wait_recv()
    term = gain_plane[0, 0]
    for k in range(1, 16):
        term = term + gain_plane[k // 4, k % 4]
    gains[1] = term
    gain_across[a3] = term
    gain_copies = [go(gains.at[1], gain_across.at[a3], GAIN_ACROSS + d - 1, place.across(d)) for d in (1, 2, 3)]
    last = later(gains.at[2], gain_twin.at[core], GAIN_TWIN, twin)
    down_grad[...] = jnp.zeros_like(down_grad)

    def down_step(step, carry):
        @pl.when(step == 4)
        def _():
            for copy in gain_copies:
                copy.wait_recv()
            term = gain_across[0] + gain_across[1] + gain_across[2] + gain_across[3]
            gains[2] = term
            gain_twin[core] = term
            last.start()

        @pl.when(step == BLOCKS - 1)
        def _():
            mine = []
            for head in range(8):
                x, y = head // 2, place.y_hi * 2 + head % 2
                mine.append(back_rows[core, place.pick(place.z, x), place.pick(y, place.z), place.pick(x, y)])
            mine = jnp.concatenate(mine, axis=0)
            hidden_grad[...] = jnp.dot(mine[:, :WIDTH], kv_turned[...], preferred_element_type=F32).astype(BF16)

        for k in range(1, 8):

            @pl.when(step == k)
            def _(k=k):
                arrive_back(k)

        owner, plane = plane_of(step)
        turned = back_rows[owner, plane].reshape(BLOCK, PAD).T
        down_grad[...] += jnp.dot(
            turned[:WIDTH], hidden_rows[owner, plane].reshape(BLOCK, MODEL), preferred_element_type=F32
        )
        return carry

    lax.fori_loop(0, BLOCKS, down_step, 0)
    last.wait_recv()
    gain_out[...] = (gain_twin[0] + gain_twin[1])[:1]
    for copy in query_copies:
        copy.wait()
    for copy in sent:
        copy.wait_send()


def whole(hidden, kv_turned, gain, rope, queries, grads, span_table):
    vmem = pl.BlockSpec(memory_space=pltpu.VMEM)
    smem = pl.BlockSpec(memory_space=pltpu.SMEM)
    anywhere = pl.BlockSpec(memory_space=pl.ANY)
    pieces = (2, 4, 4, 4, PIECE)
    return pl.pallas_call(
        whole_kernel,
        out_shape=(
            jax.ShapeDtypeStruct((HEADS, WIDTH, 128), BF16),
            jax.ShapeDtypeStruct((1, LATENT), F32),
            jax.ShapeDtypeStruct((128, MODEL), BF16),
            jax.ShapeDtypeStruct((WIDTH, MODEL), F32),
        ),
        in_specs=[anywhere, anywhere, vmem, anywhere, anywhere, anywhere, smem],
        out_specs=(anywhere, vmem, vmem, vmem),
        scratch_shapes=[
            pltpu.VMEM(hidden.shape, BF16),
            pltpu.VMEM(kv_turned.shape, BF16),
            pltpu.VMEM(pieces + (MODEL,), BF16),
            pltpu.VMEM((8, PIECE, PAD), F32),
            pltpu.VMEM((8, PIECE, PAD), F32),
            pltpu.VMEM((PIECE, PAD), F32),
            pltpu.VMEM((SPANS, PIECE, 128), F32),
            pltpu.VMEM((2, PIECE, 128), F32),
            pltpu.VMEM(pieces + (PAD,), BF16),
            pltpu.VMEM((PAD, TOKENS), BF16),
            pltpu.VMEM((WIDTH, ROWS), BF16),
            pltpu.VMEM((ROWS, LATENT), BF16),
            pltpu.VMEM((TOKENS, 128), F32),
            pltpu.VMEM((TOKENS, HALF), F32),
            pltpu.VMEM((TOKENS, HALF), F32),
            pltpu.VMEM((BLOCKS, HALF), F32),
            pltpu.VMEM((BLOCKS, HALF), F32),
            pltpu.VMEM((BLOCKS, HALF), F32),
            pltpu.VMEM(pieces + (HALF,), BF16),
            pltpu.VMEM((TOKENS, ROWS), BF16),
            pltpu.VMEM(pieces + (PAD,), F32),
            pltpu.VMEM(pieces[1:] + (PAD,), F32),
            pltpu.VMEM((4, 4, PIECE, PAD), BF16),
            pltpu.VMEM((2, 4, 4, PIECE, PAD), F32),
            pltpu.VMEM((4, 4, PIECE, PAD), BF16),
            pltpu.VMEM((15, PIECE, PAD), F32),
            pltpu.VMEM(pieces + (PAD,), BF16),
            pltpu.VMEM((3, 8, LATENT), F32),
            pltpu.VMEM((4, 4, 8, LATENT), F32),
            pltpu.VMEM((4, 8, LATENT), F32),
            pltpu.VMEM((2, 8, LATENT), F32),
            pltpu.SemaphoreType.DMA((SEMAPHORES,)),
            pltpu.SemaphoreType.DMA((SEMAPHORES,)),
            pltpu.SemaphoreType.DMA((7,)),
        ],
        compiler_params=pltpu.CompilerParams(
            collective_id=0, has_side_effects=True, vmem_limit_bytes=64 * 2**20 - 2**18
        ),
    )(hidden, kv_turned, gain, rope, queries, grads, span_table)


def hand_on_kernel(*refs):
    count = 4
    arrivals, departures = refs[-2:]
    steps = []
    for src, dst, held in zip(refs[:count], refs[count : 2 * count], refs[2 * count : 3 * count]):
        rows = src.shape[0]
        parts = 2 if rows in (WIDTH, HEADS) else 1
        for k in range(parts):
            at, n = pl.ds(k * (rows // parts), rows // parts), len(steps)
            steps.append(
                (
                    pltpu.make_async_copy(src.at[at], held.at[at], arrivals.at[n]),
                    pltpu.make_async_copy(held.at[at], dst.at[at], departures.at[n]),
                )
            )
    for arrival, _ in steps:
        arrival.start()
    for arrival, departure in steps:
        arrival.wait()
        departure.start()
    for _, departure in steps:
        departure.wait()


def hand_on(*arrays):
    anywhere = pl.BlockSpec(memory_space=pl.ANY)
    return pl.pallas_call(
        hand_on_kernel,
        out_shape=tuple(jax.ShapeDtypeStruct(a.shape, a.dtype) for a in arrays),
        in_specs=[anywhere] * len(arrays),
        out_specs=(anywhere,) * len(arrays),
        scratch_shapes=[pltpu.VMEM(a.shape, a.dtype) for a in arrays] + [pltpu.SemaphoreType.DMA((6,))] * 2,
        compiler_params=pltpu.CompilerParams(vmem_limit_bytes=63 * 2**20),
    )(*arrays)


def per_device(table, hidden, kv_down, kv_gain, queries, out_grad, span_table):
    query_grad, gain_grad, hidden_grad, down_grad = whole(
        hidden.reshape(4, 2, PIECE, MODEL),
        kv_down.T,
        kv_gain.reshape(1, LATENT),
        table,
        queries.transpose(1, 2, 0),
        out_grad.reshape(ROWS, LATENT),
        span_table,
    )
    query_grad, gain_grad, hidden_grad, down_grad = hand_on(query_grad, gain_grad, hidden_grad, down_grad)
    return (query_grad.transpose(2, 0, 1), hidden_grad, down_grad.T, gain_grad[0])


def solution(mesh):
    table = rope_rows()

    def run(hidden, kv_down, kv_gain, queries, out_grad, span_table):
        return jax.shard_map(
            per_device,
            mesh=mesh,
            in_specs=(
                P(),
                P("ctx", "head"),
                P("head", None),
                P(),
                P("ctx", "head", None),
                P("ctx", "head", None),
                P(),
            ),
            out_specs=(P("ctx", "head", None), P("ctx", "head"), P("head", None), P()),
            check_vma=False,
        )(jnp.asarray(table), hidden, kv_down, kv_gain, queries, out_grad, span_table)

    return run
```

```python
import functools
import math

import jax
import jax.numpy as jnp
import numpy as np
from jax import lax
from jax.experimental import pallas as pl
from jax.experimental.pallas import tpu as pltpu
from jax.sharding import PartitionSpec as P

MESH = pl.DeviceIdType.MESH
F32 = jnp.float32
BF16 = jnp.bfloat16
LATENT = 512
WIDTH = 576
PAD = 640
SPAN = 64
SPANS = 32
TOKENS = 2048
PIECE = 16
HEADS = 16
ROWS = 2048
MODEL = 896
EPS = 1e-06
SCALE = 1.0 / math.sqrt(192.0)
FACTOR = SCALE * math.log2(math.e)
BLOCK = 256
BLOCKS = TOKENS // BLOCK
HALF = ROWS // 2
SUB = 512


def rope_rows():
    half = (WIDTH - LATENT) // 2
    freq = np.exp(np.float32(-math.log(10000.0)) * np.arange(half, dtype=np.float32) / np.float32(half))
    angle = np.arange(TOKENS, dtype=np.float32)[:, None] * freq.astype(np.float32)[None, :]
    cos, sin = np.cos(angle.astype(np.float64)), np.sin(angle.astype(np.float64))
    both = np.concatenate([cos, cos, -sin, sin], axis=1).astype(np.float32)
    return np.ascontiguousarray(both.reshape(SPANS, 4, PIECE, 128).transpose(1, 0, 2, 3))


def nt_dot(left, right):
    return lax.dot_general(left, right, (((1,), (1,)), ((), ())), preferred_element_type=F32)


def rem4(value):
    return lax.rem(value, 4)


class Place:
    def __init__(self):
        ctx, head = lax.axis_index("ctx"), lax.axis_index("head")
        self.ctx, self.head = ctx, head
        self.core = lax.rem(ctx, 2)
        self.x = lax.div(head, 2)
        self.y_lo = lax.rem(head, 2)
        self.y_hi = lax.rem(lax.div(ctx, 2), 2)
        self.y = self.y_hi * 2 + self.y_lo
        self.z = lax.div(ctx, 4)
        self.a1 = self.pick(self.x, self.y)
        self.a2 = self.pick(self.y, self.z)
        self.a3 = self.pick(self.z, self.x)
        self.twin_a3 = self.pick(self.x, self.z)

    def pick(self, first, second):
        return first + self.core * (second - first)

    def device(self, x, y, z, core):
        return (z * 4 + lax.div(y, 2) * 2 + core, x * 2 + lax.rem(y, 2))

    def shifted(self, dx, dy, dz):
        return self.device(rem4(self.x + dx), rem4(self.y + dy), rem4(self.z + dz), self.core)

    def in_plane(self, d2, d1):
        return self.shifted(d1 * (1 - self.core), self.pick(d2, d1), d2 * self.core)

    def across(self, d3):
        return self.shifted(d3 * self.core, 0, d3 * (1 - self.core))

    def beside(self, d):
        return self.shifted(d * self.core, self.pick(2, 5 - 2 * self.y_lo), d * (1 - self.core))

    def twin(self):
        return self.device(self.x, self.y, self.z, 1 - self.core)


def remote(src, dst, send_sem, recv_sem, device):
    return pltpu.make_async_remote_copy(
        src_ref=src, dst_ref=dst, send_sem=send_sem, recv_sem=recv_sem, device_id=device, device_id_type=MESH
    )


def swap_halves(tail):
    lane = lax.broadcasted_iota(jnp.int32, tail.shape, 1)
    return jnp.where(lane < 32, pltpu.roll(tail, 96, 1), pltpu.roll(tail, 32, 1))


def block_rows(block):
    return pl.ds(pl.multiple_of(block * BLOCK, BLOCK), BLOCK)


PLANE_SHIFTS = [(d2, d1) for d2 in range(4) for d1 in range(4) if d2 or d1]

SUM_RAW = 0
KEYS_PLANE = 7
KEYS_ACROSS = 22
KEYS_TWIN = 34
HIDDEN = 38
HIDDEN_TWIN = 45
GRADS_TWIN = 46
GRADS_ACROSS = 50
GRADS_PLANE = 62
ROWS_PLANE = 77
ROWS_ACROSS = 92
ROWS_TWIN = 104
GAIN_PLANE = 108
GAIN_ACROSS = 123
GAIN_TWIN = 126
SEMAPHORES = 127


def whole_kernel(
    hidden_in,
    kv_in,
    gain,
    rope,
    queries,
    grads,
    span,
    query_out,
    gain_out,
    hidden_grad,
    down_grad,
    hidden,
    kv_turned,
    hidden_rows,
    part,
    landed,
    raw_rows,
    rope_part,
    angles,
    rows,
    keys_t,
    query_cols,
    grad_rows,
    bias,
    scores,
    prob_grads,
    tops,
    masses,
    dots,
    score_grads,
    key_total,
    twin_in,
    packed,
    from_near,
    from_far,
    from_plane,
    back_rows,
    gains,
    gain_plane,
    gain_across,
    gain_twin,
    send,
    recv,
    local,
):
    place = Place()
    core, a1, a2, a3 = place.core, place.a1, place.a2, place.a3
    twin = place.twin()
    devices = [place.in_plane(d2, d1) for d2, d1 in PLANE_SHIFTS]
    devices += [place.across(d) for d in (1, 2, 3)] + [place.beside(d) for d in (1, 2, 3)] + [twin]
    barrier = pltpu.get_barrier_semaphore()
    for device in devices:
        pl.semaphore_signal(barrier, inc=1, device_id=device, device_id_type=MESH)

    inputs = [pltpu.make_async_copy(hidden_in, hidden, local.at[4]), pltpu.make_async_copy(kv_in, kv_turned, local.at[6])]
    for copy in inputs:
        copy.start()

    sent = []

    def copy_of(src, dst, slot, device):
        return remote(src, dst, send.at[slot], recv.at[slot], device)

    def go(src, dst, slot, device):
        copy = copy_of(src, dst, slot, device)
        copy.start()
        sent.append(copy)
        return copy

    def later(src, dst, slot, device):
        copy = copy_of(src, dst, slot, device)
        sent.append(copy)
        return copy

    fetched = [
        pltpu.make_async_copy(queries.at[h], query_cols.at[:, pl.ds(h * 128, 128)], local.at[0]) for h in range(HEADS)
    ]
    for copy in fetched:
        copy.start()
    raw_grads = score_grads.at[:, pl.ds(0, LATENT)]
    grads_fetch = pltpu.make_async_copy(grads, raw_grads, local.at[1])
    grads_fetch.start()

    def hidden_parts():
        first = 2 * place.y_hi
        by_core = [[(hidden.at[:, k], hidden_rows.at[0, place.z, first + k]) for k in range(2)]]
        by_core.append([(hidden.at[k], hidden_rows.at[1, k, place.z, pl.ds(first, 2)]) for k in range(4)])
        return by_core

    rope_fetch = pltpu.make_async_copy(rope.at[rem4(place.head)], rope_part, local.at[5])
    rope_fetch.start()

    for copy in inputs:
        copy.wait()

    product = nt_dot(hidden[...].reshape(128, MODEL), kv_turned[...])
    part[:, :, :WIDTH] = product.reshape(8, PIECE, WIDTH)
    part[:, :, WIDTH:] = jnp.zeros((8, PIECE, PAD - WIDTH), F32)
    landed[place.head] = part[place.head]
    pl.semaphore_wait(barrier, len(devices))
    raw_copies = []
    for d in range(1, 8):
        other = lax.rem(place.head + d, 8)
        raw_copies.append(go(part.at[other], landed.at[place.head], SUM_RAW + d - 1, (place.ctx, other)))

    for owner, parts in enumerate(hidden_parts()):

        @pl.when(core == owner)
        def _(parts=parts):
            copies = [pltpu.make_async_copy(src, dst, local.at[2]) for src, dst in parts]
            for copy in copies:
                copy.start()
            for copy in copies:
                copy.wait()

    token = lax.broadcasted_iota(jnp.int32, (1, 128), 1)
    query_pos = jnp.where(token < SPAN, span[2 * place.ctx] * SPAN, span[2 * place.ctx + 1] * SPAN) + lax.rem(token, SPAN)
    seen_from = query_pos - lax.broadcasted_iota(jnp.int32, (PIECE, 128), 0)
    starts = [span[slot] * SPAN for slot in range(SPANS)]
    for owner in range(2):
        for index in range(64):
            at3, at2, at1 = index // 16, index // 4 % 4, index % 4
            x, y, z = ((at1, at2, at3), (at3, at1, at2))[owner]
            head = x * 2 + y % 2
            start = starts[(z * 4 + y // 2 * 2 + owner) * 2 + head // 4] + head % 4 * PIECE
            bias[pl.ds((owner * 64 + index) * PIECE, PIECE), :] = jnp.where(seen_from >= start, 0.0, -1e30)
    rope_fetch.wait()
    mine = span[2 * place.ctx + lax.div(place.head, 4)]
    both = jnp.zeros((PIECE, 128), F32)
    for k in range(SPANS):
        both = jnp.where(mine == k, rope_part[k], both)
    lane = lax.broadcasted_iota(jnp.int32, (PIECE, 128), 1)
    angles[0] = jnp.where(lane < 64, both, 0.0)
    angles[1] = jnp.where(lane < 64, pltpu.roll(both, 64, 1), 0.0)
    to = lax.broadcasted_iota(jnp.int32, (256, 256), 0)
    at = lax.broadcasted_iota(jnp.int32, (256, 256), 1)
    swap = (lax.div(to, 16) == lax.rem(at, 16)) & (lax.rem(to, 16) == lax.div(at, 16))
    swap = jnp.where(swap, 1.0, 0.0).astype(BF16)
    grads_fetch.wait()

    def order_grads(index, carry):
        here = pl.ds(pl.multiple_of(index * 256, 256), 256)
        turned = jnp.dot(swap, score_grads[here, :LATENT], preferred_element_type=F32).astype(BF16)
        for h in range(HEADS):
            to_rows = pl.ds(pl.multiple_of(h * 128 + index * 16, 16), 16)
            grad_rows[to_rows, :] = turned[h * 16 : (h + 1) * 16, :]
        return carry

    lax.fori_loop(0, 8, order_grads, 0)

    for copy in raw_copies:
        copy.wait_recv()
    raw = landed[0]
    for k in range(1, 8):
        raw = raw + landed[k]
    raw_rows[...] = raw
    latent, tail = raw[:, :LATENT], raw[:, LATENT:]
    inv_rms = lax.rsqrt(jnp.mean(latent * latent, axis=1, keepdims=True) + EPS)
    turned = tail * angles[0] + swap_halves(tail) * angles[1]
    rows[core, a3, a2, a1, :, :LATENT] = (latent * inv_rms * gain[...]).astype(BF16)
    rows[core, a3, a2, a1, :, LATENT:] = turned.astype(BF16)

    before, after, opposite = rem4(a3 + 3), rem4(a3 + 1), rem4(a3 + 2)
    twin_a3 = place.twin_a3
    own_planes = [a3, before, after, opposite]
    twin_planes = [twin_a3, rem4(twin_a3 + 3), rem4(twin_a3 + 1), rem4(twin_a3 + 2)]

    def spread(ref, plane_sem, across_sem, twin_sem):
        piece = ref.at[core, a3, a2, a1]
        copies = [go(piece, piece, plane_sem + k, place.in_plane(*d)) for k, d in enumerate(PLANE_SHIFTS)]

        def rest():
            across = {d: [] for d in (1, 2, 3)}
            for r in (0, 1, 3, 2):
                for copy, (d2, _) in zip(copies, PLANE_SHIFTS):
                    if (d2 + r) % 4 == 0:
                        copy.wait_recv()
                line = ref.at[core, a3, rem4(a2 + r)]
                for d in (1, 3, 2):
                    make = later if d == 2 else go
                    across[d].append(make(line, line, across_sem + 4 * (d - 1) + r, place.across(d)))
            plane = ref.at[core, a3]
            pairs = [go(plane, plane, twin_sem, twin)]
            for k in (1, 2, 3):
                plane = ref.at[core, own_planes[k]]
                pairs.append(later(plane, plane, twin_sem + k, twin))

            def arrive(step):
                if step == 1:
                    pairs[0].wait_recv()
                    for copy in across[2]:
                        copy.start()
                if step in (2, 3, 6):
                    k = {2: 1, 3: 2, 6: 3}[step]
                    for copy in across[{1: 1, 2: 3, 3: 2}[k]]:
                        copy.wait_recv()
                    pairs[k].start()
                if step in (4, 5, 7):
                    pairs[{4: 1, 5: 2, 7: 3}[step]].wait_recv()

            return arrive

        return rest

    def plane_of(step):
        by_step = [(0, 0), (1, 0), (0, 3), (0, 1), (1, 3), (1, 1), (0, 2), (1, 2)]
        owner, shift = 0, 0
        for k, (twins, d) in enumerate(by_step):
            here = jnp.where(step == k, 1, 0)
            owner, shift = owner + here * twins, shift + here * d
        base = a3 + owner * (twin_a3 - a3)
        return core + owner * (1 - 2 * core), rem4(base + shift)

    arrive = spread(rows, KEYS_PLANE, KEYS_ACROSS, KEYS_TWIN)()
    for copy in fetched:
        copy.wait()

    def score_block(owner, plane, half):
        block = owner * 4 + plane
        here, one = block_rows(block), pl.ds(block, 1)
        keys = rows[owner, plane].reshape(BLOCK, PAD)
        seen = bias[here, :]
        seen = jnp.concatenate([seen] * (SUB // 128), axis=1)
        for k in range(HALF // SUB):
            first = half * HALF + k * SUB
            at = pl.ds(k * SUB, SUB)
            score = jnp.dot(keys[:, :WIDTH], query_cols[:, first : first + SUB], preferred_element_type=F32) + seen
            prob_grad = nt_dot(keys[:, :LATENT], grad_rows[first : first + SUB, :])
            top = jnp.max(score, axis=0, keepdims=True)
            weight = jnp.exp2((score - top) * FACTOR)
            scores[here, at] = weight
            prob_grads[here, at] = prob_grad
            tops[one, at] = top
            masses[one, at] = jnp.sum(weight, axis=0, keepdims=True)
            dots[one, at] = jnp.sum(weight * prob_grad, axis=0, keepdims=True)

    def finish_half():
        top = jnp.max(tops[...], axis=0, keepdims=True)
        level = jnp.exp2((tops[...] - top) * FACTOR)
        share = 1.0 / jnp.sum(level * masses[...], axis=0, keepdims=True)
        delta = jnp.sum(level * dots[...], axis=0, keepdims=True) * share
        tops[...] = level * share
        dots[...] = jnp.broadcast_to(delta, dots.shape)

    def key_terms(owner, plane, half):
        columns = slice(half * HALF, (half + 1) * HALF)
        block = owner * 4 + plane
        here = block_rows(block)
        probability = scores[here, :] * tops[pl.ds(block, 1), :]
        score_grad = (probability * (prob_grads[here, :] - dots[pl.ds(0, 1), :])).astype(BF16)
        score_grads[here, columns] = score_grad
        by_score = nt_dot(score_grad, query_cols[:, columns]) * SCALE
        by_value = jnp.dot(probability.astype(BF16), grad_rows[columns, :], preferred_element_type=F32)
        return by_score[:, :LATENT] + by_value, by_score[:, LATENT:]

    def first_score_step(step, carry):
        for k in range(1, 8):

            @pl.when(step == k)
            def _(k=k):
                arrive(k)

        owner, plane = plane_of(step)
        keys_t[:, block_rows(owner * 4 + plane)] = rows[owner, plane].reshape(BLOCK, PAD).T
        score_block(owner, plane, 0)
        return carry

    lax.fori_loop(0, BLOCKS, first_score_step, 0)

    hidden_copies = []
    for k in range(7):
        dz, flip = (k + 1) // 2, (k + 1) % 2
        device = place.shifted(0, 2 * flip, dz)
        for owner, parts in enumerate(hidden_parts()):

            @pl.when(core == owner)
            def _(parts=parts, k=k, device=device):
                for src, dst in parts:
                    copy_of(src, dst, HIDDEN + k, device).start()

        like = hidden_rows.at[0, 0, pl.ds(0, 2)]
        hidden_copies.append(later(like, like, HIDDEN + k, device))

    finish_half()

    def first_key_step(block, carry):
        owner, plane = lax.div(block, 4), rem4(block)
        latent_term, rope_term = key_terms(owner, plane, 0)
        key_total[owner, plane, :, :, :, :LATENT] = latent_term.reshape(4, 4, PIECE, LATENT)
        key_total[owner, plane, :, :, :, LATENT:WIDTH] = rope_term.reshape(4, 4, PIECE, WIDTH - LATENT)
        key_total[owner, plane, :, :, :, WIDTH:] = jnp.zeros((4, 4, PIECE, PAD - WIDTH), F32)
        return carry

    lax.fori_loop(0, BLOCKS, first_key_step, 0)

    def second_score_step(block, carry):
        score_block(lax.div(block, 4), rem4(block), 1)
        return carry

    lax.fori_loop(0, BLOCKS, second_score_step, 0, unroll=2)
    finish_half()

    def second_key(owner, plane):
        latent_term, rope_term = key_terms(owner, plane, 1)
        key_total[owner, plane, :, :, :, :LATENT] += latent_term.reshape(4, 4, PIECE, LATENT)
        key_total[owner, plane, :, :, :, LATENT:WIDTH] += rope_term.reshape(4, 4, PIECE, WIDTH - LATENT)

    pairs, across = [], []
    for k, d in enumerate((2, 1, 3, 0)):
        plane = rem4(twin_a3 + d)
        pairs.append(later(key_total.at[1 - core, plane], twin_in.at[plane], GRADS_TWIN + k, twin))
    lines = (2, 1, 3, 0)
    for k, d in enumerate((2, 1, 3)):
        by_line = []
        for r in lines:
            line = rem4(a2 + r)
            src = packed.at[line] if k == 0 else key_total.at[core, rem4(a3 + d), line]
            dst = from_far.at[line] if k == 0 else from_near.at[k - 1, line]
            by_line.append(later(src, dst, GRADS_ACROSS + 4 * k + r, place.across(d)))
        across.append(by_line)
    twins_turn = (1, 1, 0, 1, 0, 1, 0, 0)
    turn_shift = (2, 1, 2, 3, 1, 0, 3, 0)

    def second_key_step(step, carry):
        twins, shift = 0, 0
        for k in range(BLOCKS):
            here = jnp.where(step == k, 1, 0)
            twins, shift = twins + here * twins_turn[k], shift + here * turn_shift[k]
        owner = core + twins * (1 - 2 * core)
        plane = rem4(a3 + twins * (twin_a3 - a3) + shift)
        second_key(owner, plane)
        for k in range(BLOCKS):
            turn = (2, 1, 3, 0).index(turn_shift[k])

            @pl.when(step == k)
            def _(k=k, turn=turn):
                if twins_turn[k]:
                    pairs[turn].start()
                else:
                    pairs[turn].wait_recv()

        @pl.when(twins == 0)
        def _():
            for at2 in range(4):
                key_total[core, plane, at2] = key_total[core, plane, at2] + twin_in[plane, at2]

        @pl.when(step == 2)
        def _():
            packed[...] = key_total[core, plane].astype(BF16)
            for copy in across[0]:
                copy.start()

        for k, turn in ((4, 1), (6, 2)):

            @pl.when(step == k)
            def _(turn=turn):
                for copy in across[turn]:
                    copy.start()

        return carry

    lax.fori_loop(0, BLOCKS, second_key_step, 0)
    for copy in hidden_copies:
        copy.wait_recv()
    hidden_to_twin = go(hidden_rows.at[core], hidden_rows.at[core], HIDDEN_TWIN, twin)

    query_copies = []
    for k in range(4):
        columns = slice(k * SUB, (k + 1) * SUB)
        total = jnp.dot(keys_t[:WIDTH, :], score_grads[:, columns], preferred_element_type=F32)
        query_cols[:, columns] = (total * SCALE).astype(BF16)
        for h in range(4 * k, 4 * k + 4):
            copy = pltpu.make_async_copy(query_cols.at[:, pl.ds(h * 128, 128)], query_out.at[h], local.at[3])
            copy.start()
            query_copies.append(copy)

    plane_copies = []
    for k, r in enumerate(lines):
        line = rem4(a2 + r)
        for by_line in across:
            by_line[k].wait_recv()
        total = key_total[core, a3, line] + from_near[0, line] + from_near[1, line]
        key_total[core, a3, line] = total + from_far[line].astype(F32)
        for n, (d2, d1) in enumerate(PLANE_SHIFTS):
            if d2 == r:
                src = key_total.at[core, a3, line, rem4(a1 + d1)]
                plane_copies.append(go(src, from_plane.at[n], GRADS_PLANE + n, place.in_plane(d2, d1)))
    raw = raw_rows[...]
    latent = raw[:, :LATENT]
    inv_rms = lax.rsqrt(jnp.mean(latent * latent, axis=1, keepdims=True) + EPS)
    cube = inv_rms * inv_rms * inv_rms
    for copy in plane_copies:
        copy.wait_recv()
    key_grad = key_total[core, a3, a2, a1]
    for k in range(15):
        key_grad = key_grad + from_plane[k]
    latent_grad, tail = key_grad[:, :LATENT], key_grad[:, LATENT:]
    scaled = latent_grad * gain[...]
    latent_back = inv_rms * scaled - latent * cube * jnp.mean(scaled * latent, axis=1, keepdims=True)
    rope_back = tail * angles[0] - swap_halves(tail) * angles[1]
    back_rows[core, a3, a2, a1, :, :LATENT] = latent_back.astype(BF16)
    back_rows[core, a3, a2, a1, :, LATENT:] = rope_back.astype(BF16)
    spread_rest = spread(back_rows, ROWS_PLANE, ROWS_ACROSS, ROWS_TWIN)

    term = jnp.broadcast_to(jnp.sum(latent_grad * latent * inv_rms, axis=0, keepdims=True), (8, LATENT))
    gains[0] = term
    gain_plane[a2, a1] = term
    gain_copies = [
        go(gains.at[0], gain_plane.at[a2, a1], GAIN_PLANE + k, place.in_plane(*d)) for k, d in enumerate(PLANE_SHIFTS)
    ]
    hidden_to_twin.wait_recv()
    arrive_back = spread_rest()
    for copy in gain_copies:
        copy.wait_recv()
    term = gain_plane[0, 0]
    for k in range(1, 16):
        term = term + gain_plane[k // 4, k % 4]
    gains[1] = term
    gain_across[a3] = term
    gain_copies = [go(gains.at[1], gain_across.at[a3], GAIN_ACROSS + d - 1, place.across(d)) for d in (1, 2, 3)]
    last = later(gains.at[2], gain_twin.at[core], GAIN_TWIN, twin)
    down_grad[...] = jnp.zeros_like(down_grad)

    def down_step(step, carry):
        @pl.when(step == 4)
        def _():
            for copy in gain_copies:
                copy.wait_recv()
            term = gain_across[0] + gain_across[1] + gain_across[2] + gain_across[3]
            gains[2] = term
            gain_twin[core] = term
            last.start()

        @pl.when(step == BLOCKS - 1)
        def _():
            mine = []
            for head in range(8):
                x, y = head // 2, place.y_hi * 2 + head % 2
                mine.append(back_rows[core, place.pick(place.z, x), place.pick(y, place.z), place.pick(x, y)])
            mine = jnp.concatenate(mine, axis=0)
            hidden_grad[...] = jnp.dot(mine[:, :WIDTH], kv_turned[...], preferred_element_type=F32).astype(BF16)

        for k in range(1, 8):

            @pl.when(step == k)
            def _(k=k):
                arrive_back(k)

        owner, plane = plane_of(step)
        turned = back_rows[owner, plane].reshape(BLOCK, PAD).T
        down_grad[...] += jnp.dot(
            turned[:WIDTH], hidden_rows[owner, plane].reshape(BLOCK, MODEL), preferred_element_type=F32
        )
        return carry

    lax.fori_loop(0, BLOCKS, down_step, 0)
    last.wait_recv()
    gain_out[...] = (gain_twin[0] + gain_twin[1])[:1]
    for copy in query_copies:
        copy.wait()
    for copy in sent:
        copy.wait_send()


def whole(hidden, kv_turned, gain, rope, queries, grads, span_table):
    vmem = pl.BlockSpec(memory_space=pltpu.VMEM)
    smem = pl.BlockSpec(memory_space=pltpu.SMEM)
    anywhere = pl.BlockSpec(memory_space=pl.ANY)
    pieces = (2, 4, 4, 4, PIECE)
    return pl.pallas_call(
        whole_kernel,
        out_shape=(
            jax.ShapeDtypeStruct((HEADS, WIDTH, 128), BF16),
            jax.ShapeDtypeStruct((1, LATENT), F32),
            jax.ShapeDtypeStruct((128, MODEL), BF16),
            jax.ShapeDtypeStruct((WIDTH, MODEL), F32),
        ),
        in_specs=[anywhere, anywhere, vmem, anywhere, anywhere, anywhere, smem],
        out_specs=(anywhere, vmem, vmem, vmem),
        scratch_shapes=[
            pltpu.VMEM(hidden.shape, BF16),
            pltpu.VMEM(kv_turned.shape, BF16),
            pltpu.VMEM(pieces + (MODEL,), BF16),
            pltpu.VMEM((8, PIECE, PAD), F32),
            pltpu.VMEM((8, PIECE, PAD), F32),
            pltpu.VMEM((PIECE, PAD), F32),
            pltpu.VMEM((SPANS, PIECE, 128), F32),
            pltpu.VMEM((2, PIECE, 128), F32),
            pltpu.VMEM(pieces + (PAD,), BF16),
            pltpu.VMEM((PAD, TOKENS), BF16),
            pltpu.VMEM((WIDTH, ROWS), BF16),
            pltpu.VMEM((ROWS, LATENT), BF16),
            pltpu.VMEM((TOKENS, 128), F32),
            pltpu.VMEM((TOKENS, HALF), F32),
            pltpu.VMEM((TOKENS, HALF), F32),
            pltpu.VMEM((BLOCKS, HALF), F32),
            pltpu.VMEM((BLOCKS, HALF), F32),
            pltpu.VMEM((BLOCKS, HALF), F32),
            pltpu.VMEM((TOKENS, ROWS), BF16),
            pltpu.VMEM(pieces + (PAD,), F32),
            pltpu.VMEM(pieces[1:] + (PAD,), F32),
            pltpu.VMEM((4, 4, PIECE, PAD), BF16),
            pltpu.VMEM((2, 4, 4, PIECE, PAD), F32),
            pltpu.VMEM((4, 4, PIECE, PAD), BF16),
            pltpu.VMEM((15, PIECE, PAD), F32),
            pltpu.VMEM(pieces + (PAD,), BF16),
            pltpu.VMEM((3, 8, LATENT), F32),
            pltpu.VMEM((4, 4, 8, LATENT), F32),
            pltpu.VMEM((4, 8, LATENT), F32),
            pltpu.VMEM((2, 8, LATENT), F32),
            pltpu.SemaphoreType.DMA((SEMAPHORES,)),
            pltpu.SemaphoreType.DMA((SEMAPHORES,)),
            pltpu.SemaphoreType.DMA((7,)),
        ],
        compiler_params=pltpu.CompilerParams(
            collective_id=0, has_side_effects=True, vmem_limit_bytes=64 * 2**20 - 2**18
        ),
    )(hidden, kv_turned, gain, rope, queries, grads, span_table)


def hand_on_kernel(*refs):
    count = 4
    arrivals, departures = refs[-2:]
    steps = []
    for src, dst, held in zip(refs[:count], refs[count : 2 * count], refs[2 * count : 3 * count]):
        rows = src.shape[0]
        parts = 2 if rows in (WIDTH, HEADS) else 1
        for k in range(parts):
            at, n = pl.ds(k * (rows // parts), rows // parts), len(steps)
            steps.append(
                (
                    pltpu.make_async_copy(src.at[at], held.at[at], arrivals.at[n]),
                    pltpu.make_async_copy(held.at[at], dst.at[at], departures.at[n]),
                )
            )
    for arrival, _ in steps:
        arrival.start()
    for arrival, departure in steps:
        arrival.wait()
        departure.start()
    for _, departure in steps:
        departure.wait()


def hand_on(*arrays):
    anywhere = pl.BlockSpec(memory_space=pl.ANY)
    return pl.pallas_call(
        hand_on_kernel,
        out_shape=tuple(jax.ShapeDtypeStruct(a.shape, a.dtype) for a in arrays),
        in_specs=[anywhere] * len(arrays),
        out_specs=(anywhere,) * len(arrays),
        scratch_shapes=[pltpu.VMEM(a.shape, a.dtype) for a in arrays] + [pltpu.SemaphoreType.DMA((6,))] * 2,
        compiler_params=pltpu.CompilerParams(vmem_limit_bytes=63 * 2**20),
    )(*arrays)


def per_device(table, hidden, kv_down, kv_gain, queries, out_grad, span_table):
    query_grad, gain_grad, hidden_grad, down_grad = whole(
        hidden.reshape(4, 2, PIECE, MODEL),
        kv_down.T,
        kv_gain.reshape(1, LATENT),
        table,
        queries.transpose(1, 2, 0),
        out_grad.reshape(ROWS, LATENT),
        span_table,
    )
    query_grad, gain_grad, hidden_grad, down_grad = hand_on(query_grad, gain_grad, hidden_grad, down_grad)
    return (query_grad.transpose(2, 0, 1), hidden_grad, down_grad.T, gain_grad[0])


def solution(mesh):
    table = rope_rows()

    def run(hidden, kv_down, kv_gain, queries, out_grad, span_table):
        return jax.shard_map(
            per_device,
            mesh=mesh,
            in_specs=(
                P(),
                P("ctx", "head"),
                P("head", None),
                P(),
                P("ctx", "head", None),
                P("ctx", "head", None),
                P(),
            ),
            out_specs=(P("ctx", "head", None), P("ctx", "head"), P("head", None), P()),
            check_vma=False,
        )(jnp.asarray(table), hidden, kv_down, kv_gain, queries, out_grad, span_table)

    return run
```

```python
import functools
import math

import jax
import jax.numpy as jnp
import numpy as np
from jax import lax
from jax.experimental import pallas as pl
from jax.experimental.pallas import tpu as pltpu
from jax.sharding import PartitionSpec as P

MESH = pl.DeviceIdType.MESH
F32 = jnp.float32
BF16 = jnp.bfloat16
LATENT = 512
WIDTH = 576
PAD = 640
SPAN = 64
SPANS = 32
TOKENS = 2048
PIECE = 16
HEADS = 16
ROWS = 2048
MODEL = 896
EPS = 1e-06
SCALE = 1.0 / math.sqrt(192.0)
FACTOR = SCALE * math.log2(math.e)
BLOCK = 256
BLOCKS = TOKENS // BLOCK
HALF = ROWS // 2
SUB = 512


def rope_rows():
    half = (WIDTH - LATENT) // 2
    freq = np.exp(np.float32(-math.log(10000.0)) * np.arange(half, dtype=np.float32) / np.float32(half))
    angle = np.arange(TOKENS, dtype=np.float32)[:, None] * freq.astype(np.float32)[None, :]
    cos, sin = np.cos(angle.astype(np.float64)), np.sin(angle.astype(np.float64))
    both = np.concatenate([cos, cos, -sin, sin], axis=1).astype(np.float32)
    return np.ascontiguousarray(both.reshape(SPANS, 4, PIECE, 128).transpose(1, 0, 2, 3))


def nt_dot(left, right):
    return lax.dot_general(left, right, (((1,), (1,)), ((), ())), preferred_element_type=F32)


def rem4(value):
    return lax.rem(value, 4)


class Place:
    def __init__(self):
        ctx, head = lax.axis_index("ctx"), lax.axis_index("head")
        self.ctx, self.head = ctx, head
        self.core = lax.rem(ctx, 2)
        self.x = lax.div(head, 2)
        self.y_lo = lax.rem(head, 2)
        self.y_hi = lax.rem(lax.div(ctx, 2), 2)
        self.y = self.y_hi * 2 + self.y_lo
        self.z = lax.div(ctx, 4)
        self.a1 = self.pick(self.x, self.y)
        self.a2 = self.pick(self.y, self.z)
        self.a3 = self.pick(self.z, self.x)
        self.twin_a3 = self.pick(self.x, self.z)

    def pick(self, first, second):
        return first + self.core * (second - first)

    def device(self, x, y, z, core):
        return (z * 4 + lax.div(y, 2) * 2 + core, x * 2 + lax.rem(y, 2))

    def shifted(self, dx, dy, dz):
        return self.device(rem4(self.x + dx), rem4(self.y + dy), rem4(self.z + dz), self.core)

    def in_plane(self, d2, d1):
        return self.shifted(d1 * (1 - self.core), self.pick(d2, d1), d2 * self.core)

    def across(self, d3):
        return self.shifted(d3 * self.core, 0, d3 * (1 - self.core))

    def beside(self, d):
        return self.shifted(d * self.core, self.pick(2, 5 - 2 * self.y_lo), d * (1 - self.core))

    def twin(self):
        return self.device(self.x, self.y, self.z, 1 - self.core)


def remote(src, dst, send_sem, recv_sem, device):
    return pltpu.make_async_remote_copy(
        src_ref=src, dst_ref=dst, send_sem=send_sem, recv_sem=recv_sem, device_id=device, device_id_type=MESH
    )


def swap_halves(tail):
    lane = lax.broadcasted_iota(jnp.int32, tail.shape, 1)
    return jnp.where(lane < 32, pltpu.roll(tail, 96, 1), pltpu.roll(tail, 32, 1))


def block_rows(block):
    return pl.ds(pl.multiple_of(block * BLOCK, BLOCK), BLOCK)


PLANE_SHIFTS = [(d2, d1) for d2 in range(4) for d1 in range(4) if d2 or d1]

SUM_RAW = 0
KEYS_PLANE = 7
KEYS_ACROSS = 22
KEYS_TWIN = 34
HIDDEN = 38
HIDDEN_TWIN = 45
GRADS_TWIN = 46
GRADS_ACROSS = 50
GRADS_PLANE = 62
ROWS_PLANE = 77
ROWS_ACROSS = 92
ROWS_TWIN = 104
GAIN_PLANE = 108
GAIN_ACROSS = 123
GAIN_TWIN = 126
SEMAPHORES = 127


def whole_kernel(
    hidden_in,
    kv_in,
    gain,
    rope,
    queries,
    grads,
    span,
    query_out,
    gain_out,
    hidden_grad,
    down_grad,
    hidden,
    kv_turned,
    hidden_rows,
    part,
    landed,
    raw_rows,
    rope_part,
    angles,
    rows,
    keys_t,
    query_cols,
    grad_rows,
    bias,
    scores,
    prob_grads,
    tops,
    masses,
    dots,
    score_grads,
    key_total,
    twin_in,
    packed,
    from_near,
    from_far,
    from_plane,
    back_rows,
    gains,
    gain_plane,
    gain_across,
    gain_twin,
    send,
    recv,
    local,
):
    place = Place()
    core, a1, a2, a3 = place.core, place.a1, place.a2, place.a3
    twin = place.twin()
    devices = [place.in_plane(d2, d1) for d2, d1 in PLANE_SHIFTS]
    devices += [place.across(d) for d in (1, 2, 3)] + [place.beside(d) for d in (1, 2, 3)] + [twin]
    barrier = pltpu.get_barrier_semaphore()
    for device in devices:
        pl.semaphore_signal(barrier, inc=1, device_id=device, device_id_type=MESH)

    inputs = [pltpu.make_async_copy(hidden_in, hidden, local.at[4]), pltpu.make_async_copy(kv_in, kv_turned, local.at[6])]
    for copy in inputs:
        copy.start()

    sent = []

    def copy_of(src, dst, slot, device):
        return remote(src, dst, send.at[slot], recv.at[slot], device)

    def go(src, dst, slot, device):
        copy = copy_of(src, dst, slot, device)
        copy.start()
        sent.append(copy)
        return copy

    def later(src, dst, slot, device):
        copy = copy_of(src, dst, slot, device)
        sent.append(copy)
        return copy

    fetched = [
        pltpu.make_async_copy(queries.at[h], query_cols.at[:, pl.ds(h * 128, 128)], local.at[0]) for h in range(HEADS)
    ]
    for copy in fetched:
        copy.start()
    raw_grads = score_grads.at[:, pl.ds(0, LATENT)]
    grads_fetch = pltpu.make_async_copy(grads, raw_grads, local.at[1])
    grads_fetch.start()

    def hidden_parts():
        first = 2 * place.y_hi
        by_core = [[(hidden.at[:, k], hidden_rows.at[0, place.z, first + k]) for k in range(2)]]
        by_core.append([(hidden.at[k], hidden_rows.at[1, k, place.z, pl.ds(first, 2)]) for k in range(4)])
        return by_core

    rope_fetch = pltpu.make_async_copy(rope.at[rem4(place.head)], rope_part, local.at[5])
    rope_fetch.start()

    for copy in inputs:
        copy.wait()

    product = nt_dot(hidden[...].reshape(128, MODEL), kv_turned[...])
    part[:, :, :WIDTH] = product.reshape(8, PIECE, WIDTH)
    part[:, :, WIDTH:] = jnp.zeros((8, PIECE, PAD - WIDTH), F32)
    landed[place.head] = part[place.head]
    pl.semaphore_wait(barrier, len(devices))
    raw_copies = []
    for d in range(1, 8):
        other = lax.rem(place.head + d, 8)
        raw_copies.append(go(part.at[other], landed.at[place.head], SUM_RAW + d - 1, (place.ctx, other)))

    for owner, parts in enumerate(hidden_parts()):

        @pl.when(core == owner)
        def _(parts=parts):
            copies = [pltpu.make_async_copy(src, dst, local.at[2]) for src, dst in parts]
            for copy in copies:
                copy.start()
            for copy in copies:
                copy.wait()

    token = lax.broadcasted_iota(jnp.int32, (1, 128), 1)
    query_pos = jnp.where(token < SPAN, span[2 * place.ctx] * SPAN, span[2 * place.ctx + 1] * SPAN) + lax.rem(token, SPAN)
    seen_from = query_pos - lax.broadcasted_iota(jnp.int32, (PIECE, 128), 0)
    starts = [span[slot] * SPAN for slot in range(SPANS)]
    for owner in range(2):
        for index in range(64):
            at3, at2, at1 = index // 16, index // 4 % 4, index % 4
            x, y, z = ((at1, at2, at3), (at3, at1, at2))[owner]
            head = x * 2 + y % 2
            start = starts[(z * 4 + y // 2 * 2 + owner) * 2 + head // 4] + head % 4 * PIECE
            bias[pl.ds((owner * 64 + index) * PIECE, PIECE), :] = jnp.where(seen_from >= start, 0.0, -1e30)
    rope_fetch.wait()
    mine = span[2 * place.ctx + lax.div(place.head, 4)]
    both = jnp.zeros((PIECE, 128), F32)
    for k in range(SPANS):
        both = jnp.where(mine == k, rope_part[k], both)
    lane = lax.broadcasted_iota(jnp.int32, (PIECE, 128), 1)
    angles[0] = jnp.where(lane < 64, both, 0.0)
    angles[1] = jnp.where(lane < 64, pltpu.roll(both, 64, 1), 0.0)
    to = lax.broadcasted_iota(jnp.int32, (256, 256), 0)
    at = lax.broadcasted_iota(jnp.int32, (256, 256), 1)
    swap = (lax.div(to, 16) == lax.rem(at, 16)) & (lax.rem(to, 16) == lax.div(at, 16))
    swap = jnp.where(swap, 1.0, 0.0).astype(BF16)
    grads_fetch.wait()

    def order_grads(index, carry):
        here = pl.ds(pl.multiple_of(index * 256, 256), 256)
        turned = jnp.dot(swap, score_grads[here, :LATENT], preferred_element_type=F32).astype(BF16)
        for h in range(HEADS):
            to_rows = pl.ds(pl.multiple_of(h * 128 + index * 16, 16), 16)
            grad_rows[to_rows, :] = turned[h * 16 : (h + 1) * 16, :]
        return carry

    lax.fori_loop(0, 8, order_grads, 0)

    for copy in raw_copies:
        copy.wait_recv()
    raw = landed[0]
    for k in range(1, 8):
        raw = raw + landed[k]
    raw_rows[...] = raw
    latent, tail = raw[:, :LATENT], raw[:, LATENT:]
    inv_rms = lax.rsqrt(jnp.mean(latent * latent, axis=1, keepdims=True) + EPS)
    turned = tail * angles[0] + swap_halves(tail) * angles[1]
    rows[core, a3, a2, a1, :, :LATENT] = (latent * inv_rms * gain[...]).astype(BF16)
    rows[core, a3, a2, a1, :, LATENT:] = turned.astype(BF16)

    before, after, opposite = rem4(a3 + 3), rem4(a3 + 1), rem4(a3 + 2)
    twin_a3 = place.twin_a3
    own_planes = [a3, before, after, opposite]
    twin_planes = [twin_a3, rem4(twin_a3 + 3), rem4(twin_a3 + 1), rem4(twin_a3 + 2)]

    def spread(ref, plane_sem, across_sem, twin_sem):
        piece = ref.at[core, a3, a2, a1]
        copies = [go(piece, piece, plane_sem + k, place.in_plane(*d)) for k, d in enumerate(PLANE_SHIFTS)]

        def rest():
            across = {d: [] for d in (1, 2, 3)}
            for r in (0, 1, 3, 2):
                for copy, (d2, _) in zip(copies, PLANE_SHIFTS):
                    if (d2 + r) % 4 == 0:
                        copy.wait_recv()
                line = ref.at[core, a3, rem4(a2 + r)]
                for d in (1, 3, 2):
                    make = later if d == 2 else go
                    across[d].append(make(line, line, across_sem + 4 * (d - 1) + r, place.across(d)))
            plane = ref.at[core, a3]
            pairs = [go(plane, plane, twin_sem, twin)]
            for k in (1, 2, 3):
                plane = ref.at[core, own_planes[k]]
                pairs.append(later(plane, plane, twin_sem + k, twin))

            def arrive(step):
                if step == 1:
                    pairs[0].wait_recv()
                    for copy in across[2]:
                        copy.start()
                if step in (2, 3, 6):
                    k = {2: 1, 3: 2, 6: 3}[step]
                    for copy in across[{1: 1, 2: 3, 3: 2}[k]]:
                        copy.wait_recv()
                    pairs[k].start()
                if step in (4, 5, 7):
                    pairs[{4: 1, 5: 2, 7: 3}[step]].wait_recv()

            return arrive

        return rest

    def plane_of(step):
        by_step = [(0, 0), (1, 0), (0, 3), (0, 1), (1, 3), (1, 1), (0, 2), (1, 2)]
        owner, shift = 0, 0
        for k, (twins, d) in enumerate(by_step):
            here = jnp.where(step == k, 1, 0)
            owner, shift = owner + here * twins, shift + here * d
        base = a3 + owner * (twin_a3 - a3)
        return core + owner * (1 - 2 * core), rem4(base + shift)

    arrive = spread(rows, KEYS_PLANE, KEYS_ACROSS, KEYS_TWIN)()
    for copy in fetched:
        copy.wait()

    def score_block(owner, plane, half):
        block = owner * 4 + plane
        here, one = block_rows(block), pl.ds(block, 1)
        keys = rows[owner, plane].reshape(BLOCK, PAD)
        seen = bias[here, :]
        seen = jnp.concatenate([seen] * (SUB // 128), axis=1)
        for k in range(HALF // SUB):
            first = half * HALF + k * SUB
            at = pl.ds(k * SUB, SUB)
            score = jnp.dot(keys[:, :WIDTH], query_cols[:, first : first + SUB], preferred_element_type=F32) + seen
            prob_grad = nt_dot(keys[:, :LATENT], grad_rows[first : first + SUB, :])
            top = jnp.max(score, axis=0, keepdims=True)
            weight = jnp.exp2((score - top) * FACTOR)
            scores[here, at] = weight
            prob_grads[here, at] = prob_grad
            tops[one, at] = top
            masses[one, at] = jnp.sum(weight, axis=0, keepdims=True)
            dots[one, at] = jnp.sum(weight * prob_grad, axis=0, keepdims=True)

    def finish_half():
        top = jnp.max(tops[...], axis=0, keepdims=True)
        level = jnp.exp2((tops[...] - top) * FACTOR)
        share = 1.0 / jnp.sum(level * masses[...], axis=0, keepdims=True)
        delta = jnp.sum(level * dots[...], axis=0, keepdims=True) * share
        tops[...] = level * share
        dots[...] = jnp.broadcast_to(delta, dots.shape)

    def key_terms(owner, plane, half):
        columns = slice(half * HALF, (half + 1) * HALF)
        block = owner * 4 + plane
        here = block_rows(block)
        probability = scores[here, :] * tops[pl.ds(block, 1), :]
        score_grad = (probability * (prob_grads[here, :] - dots[pl.ds(0, 1), :])).astype(BF16)
        score_grads[here, columns] = score_grad
        by_score = nt_dot(score_grad, query_cols[:, columns]) * SCALE
        by_value = jnp.dot(probability.astype(BF16), grad_rows[columns, :], preferred_element_type=F32)
        return by_score[:, :LATENT] + by_value, by_score[:, LATENT:]

    def first_score_step(step, carry):
        for k in range(1, 8):

            @pl.when(step == k)
            def _(k=k):
                arrive(k)

        owner, plane = plane_of(step)
        keys_t[:, block_rows(owner * 4 + plane)] = rows[owner, plane].reshape(BLOCK, PAD).T
        score_block(owner, plane, 0)
        return carry

    lax.fori_loop(0, BLOCKS, first_score_step, 0)

    hidden_copies = []
    for k in range(7):
        dz, flip = (k + 1) // 2, (k + 1) % 2
        device = place.shifted(0, 2 * flip, dz)
        for owner, parts in enumerate(hidden_parts()):

            @pl.when(core == owner)
            def _(parts=parts, k=k, device=device):
                for src, dst in parts:
                    copy_of(src, dst, HIDDEN + k, device).start()

        like = hidden_rows.at[0, 0, pl.ds(0, 2)]
        hidden_copies.append(later(like, like, HIDDEN + k, device))

    finish_half()

    def first_key_step(block, carry):
        owner, plane = lax.div(block, 4), rem4(block)
        latent_term, rope_term = key_terms(owner, plane, 0)
        key_total[owner, plane, :, :, :, :LATENT] = latent_term.reshape(4, 4, PIECE, LATENT)
        key_total[owner, plane, :, :, :, LATENT:WIDTH] = rope_term.reshape(4, 4, PIECE, WIDTH - LATENT)
        key_total[owner, plane, :, :, :, WIDTH:] = jnp.zeros((4, 4, PIECE, PAD - WIDTH), F32)
        return carry

    lax.fori_loop(0, BLOCKS, first_key_step, 0)

    def second_score_step(block, carry):
        score_block(lax.div(block, 4), rem4(block), 1)
        return carry

    lax.fori_loop(0, BLOCKS, second_score_step, 0, unroll=2)
    finish_half()

    def second_key(owner, plane):
        latent_term, rope_term = key_terms(owner, plane, 1)
        key_total[owner, plane, :, :, :, :LATENT] += latent_term.reshape(4, 4, PIECE, LATENT)
        key_total[owner, plane, :, :, :, LATENT:WIDTH] += rope_term.reshape(4, 4, PIECE, WIDTH - LATENT)

    pairs, across = [], []
    for k, d in enumerate((2, 1, 3, 0)):
        plane = rem4(twin_a3 + d)
        pairs.append(later(key_total.at[1 - core, plane], twin_in.at[plane], GRADS_TWIN + k, twin))
    lines = (2, 1, 3, 0)
    for k, d in enumerate((2, 1, 3)):
        by_line = []
        for r in lines:
            line = rem4(a2 + r)
            src = packed.at[line] if k == 0 else key_total.at[core, rem4(a3 + d), line]
            dst = from_far.at[line] if k == 0 else from_near.at[k - 1, line]
            by_line.append(later(src, dst, GRADS_ACROSS + 4 * k + r, place.across(d)))
        across.append(by_line)
    twins_turn = (1, 1, 1, 1, 0, 0, 0, 0)
    turn_shift = (2, 1, 3, 0, 2, 1, 3, 0)

    def second_key_step(step, carry):
        twins, shift = 0, 0
        for k in range(BLOCKS):
            here = jnp.where(step == k, 1, 0)
            twins, shift = twins + here * twins_turn[k], shift + here * turn_shift[k]
        owner = core + twins * (1 - 2 * core)
        plane = rem4(a3 + twins * (twin_a3 - a3) + shift)
        second_key(owner, plane)
        for k in range(BLOCKS):
            turn = (2, 1, 3, 0).index(turn_shift[k])

            @pl.when(step == k)
            def _(k=k, turn=turn):
                if twins_turn[k]:
                    pairs[turn].start()
                else:
                    pairs[turn].wait_recv()

        @pl.when(twins == 0)
        def _():
            for at2 in range(4):
                key_total[core, plane, at2] = key_total[core, plane, at2] + twin_in[plane, at2]

        @pl.when(step == 4)
        def _():
            packed[...] = key_total[core, plane].astype(BF16)
            for copy in across[0]:
                copy.start()

        for k, turn in ((5, 1), (6, 2)):

            @pl.when(step == k)
            def _(turn=turn):
                for copy in across[turn]:
                    copy.start()

        return carry

    lax.fori_loop(0, BLOCKS, second_key_step, 0)
    for copy in hidden_copies:
        copy.wait_recv()
    hidden_to_twin = go(hidden_rows.at[core], hidden_rows.at[core], HIDDEN_TWIN, twin)

    query_copies = []
    for k in range(4):
        columns = slice(k * SUB, (k + 1) * SUB)
        total = jnp.dot(keys_t[:WIDTH, :], score_grads[:, columns], preferred_element_type=F32)
        query_cols[:, columns] = (total * SCALE).astype(BF16)
        for h in range(4 * k, 4 * k + 4):
            copy = pltpu.make_async_copy(query_cols.at[:, pl.ds(h * 128, 128)], query_out.at[h], local.at[3])
            copy.start()
            query_copies.append(copy)

    plane_copies = []
    for k, r in enumerate(lines):
        line = rem4(a2 + r)
        for by_line in across:
            by_line[k].wait_recv()
        total = key_total[core, a3, line] + from_near[0, line] + from_near[1, line]
        key_total[core, a3, line] = total + from_far[line].astype(F32)
        for n, (d2, d1) in enumerate(PLANE_SHIFTS):
            if d2 == r:
                src = key_total.at[core, a3, line, rem4(a1 + d1)]
                plane_copies.append(go(src, from_plane.at[n], GRADS_PLANE + n, place.in_plane(d2, d1)))
    raw = raw_rows[...]
    latent = raw[:, :LATENT]
    inv_rms = lax.rsqrt(jnp.mean(latent * latent, axis=1, keepdims=True) + EPS)
    cube = inv_rms * inv_rms * inv_rms
    for copy in plane_copies:
        copy.wait_recv()
    key_grad = key_total[core, a3, a2, a1]
    for k in range(15):
        key_grad = key_grad + from_plane[k]
    latent_grad, tail = key_grad[:, :LATENT], key_grad[:, LATENT:]
    scaled = latent_grad * gain[...]
    latent_back = inv_rms * scaled - latent * cube * jnp.mean(scaled * latent, axis=1, keepdims=True)
    rope_back = tail * angles[0] - swap_halves(tail) * angles[1]
    back_rows[core, a3, a2, a1, :, :LATENT] = latent_back.astype(BF16)
    back_rows[core, a3, a2, a1, :, LATENT:] = rope_back.astype(BF16)
    spread_rest = spread(back_rows, ROWS_PLANE, ROWS_ACROSS, ROWS_TWIN)

    term = jnp.broadcast_to(jnp.sum(latent_grad * latent * inv_rms, axis=0, keepdims=True), (8, LATENT))
    gains[0] = term
    gain_plane[a2, a1] = term
    gain_copies = [
        go(gains.at[0], gain_plane.at[a2, a1], GAIN_PLANE + k, place.in_plane(*d)) for k, d in enumerate(PLANE_SHIFTS)
    ]
    hidden_to_twin.wait_recv()
    arrive_back = spread_rest()
    for copy in gain_copies:
        copy.wait_recv()
    term = gain_plane[0, 0]
    for k in range(1, 16):
        term = term + gain_plane[k // 4, k % 4]
    gains[1] = term
    gain_across[a3] = term
    gain_copies = [go(gains.at[1], gain_across.at[a3], GAIN_ACROSS + d - 1, place.across(d)) for d in (1, 2, 3)]
    last = later(gains.at[2], gain_twin.at[core], GAIN_TWIN, twin)
    down_grad[...] = jnp.zeros_like(down_grad)

    def down_step(step, carry):
        @pl.when(step == 4)
        def _():
            for copy in gain_copies:
                copy.wait_recv()
            term = gain_across[0] + gain_across[1] + gain_across[2] + gain_across[3]
            gains[2] = term
            gain_twin[core] = term
            last.start()

        @pl.when(step == BLOCKS - 1)
        def _():
            mine = []
            for head in range(8):
                x, y = head // 2, place.y_hi * 2 + head % 2
                mine.append(back_rows[core, place.pick(place.z, x), place.pick(y, place.z), place.pick(x, y)])
            mine = jnp.concatenate(mine, axis=0)
            hidden_grad[...] = jnp.dot(mine[:, :WIDTH], kv_turned[...], preferred_element_type=F32).astype(BF16)

        for k in range(1, 8):

            @pl.when(step == k)
            def _(k=k):
                arrive_back(k)

        owner, plane = plane_of(step)
        turned = back_rows[owner, plane].reshape(BLOCK, PAD).T
        down_grad[...] += jnp.dot(
            turned[:WIDTH], hidden_rows[owner, plane].reshape(BLOCK, MODEL), preferred_element_type=F32
        )
        return carry

    lax.fori_loop(0, BLOCKS, down_step, 0)
    last.wait_recv()
    gain_out[...] = (gain_twin[0] + gain_twin[1])[:1]
    for copy in query_copies:
        copy.wait()
    for copy in sent:
        copy.wait_send()


def whole(hidden, kv_turned, gain, rope, queries, grads, span_table):
    vmem = pl.BlockSpec(memory_space=pltpu.VMEM)
    smem = pl.BlockSpec(memory_space=pltpu.SMEM)
    anywhere = pl.BlockSpec(memory_space=pl.ANY)
    pieces = (2, 4, 4, 4, PIECE)
    return pl.pallas_call(
        whole_kernel,
        out_shape=(
            jax.ShapeDtypeStruct((HEADS, WIDTH, 128), BF16),
            jax.ShapeDtypeStruct((1, LATENT), F32),
            jax.ShapeDtypeStruct((128, MODEL), BF16),
            jax.ShapeDtypeStruct((WIDTH, MODEL), F32),
        ),
        in_specs=[anywhere, anywhere, vmem, anywhere, anywhere, anywhere, smem],
        out_specs=(anywhere, vmem, vmem, vmem),
        scratch_shapes=[
            pltpu.VMEM(hidden.shape, BF16),
            pltpu.VMEM(kv_turned.shape, BF16),
            pltpu.VMEM(pieces + (MODEL,), BF16),
            pltpu.VMEM((8, PIECE, PAD), F32),
            pltpu.VMEM((8, PIECE, PAD), F32),
            pltpu.VMEM((PIECE, PAD), F32),
            pltpu.VMEM((SPANS, PIECE, 128), F32),
            pltpu.VMEM((2, PIECE, 128), F32),
            pltpu.VMEM(pieces + (PAD,), BF16),
            pltpu.VMEM((PAD, TOKENS), BF16),
            pltpu.VMEM((WIDTH, ROWS), BF16),
            pltpu.VMEM((ROWS, LATENT), BF16),
            pltpu.VMEM((TOKENS, 128), F32),
            pltpu.VMEM((TOKENS, HALF), F32),
            pltpu.VMEM((TOKENS, HALF), F32),
            pltpu.VMEM((BLOCKS, HALF), F32),
            pltpu.VMEM((BLOCKS, HALF), F32),
            pltpu.VMEM((BLOCKS, HALF), F32),
            pltpu.VMEM((TOKENS, ROWS), BF16),
            pltpu.VMEM(pieces + (PAD,), F32),
            pltpu.VMEM(pieces[1:] + (PAD,), F32),
            pltpu.VMEM((4, 4, PIECE, PAD), BF16),
            pltpu.VMEM((2, 4, 4, PIECE, PAD), F32),
            pltpu.VMEM((4, 4, PIECE, PAD), BF16),
            pltpu.VMEM((15, PIECE, PAD), F32),
            pltpu.VMEM(pieces + (PAD,), BF16),
            pltpu.VMEM((3, 8, LATENT), F32),
            pltpu.VMEM((4, 4, 8, LATENT), F32),
            pltpu.VMEM((4, 8, LATENT), F32),
            pltpu.VMEM((2, 8, LATENT), F32),
            pltpu.SemaphoreType.DMA((SEMAPHORES,)),
            pltpu.SemaphoreType.DMA((SEMAPHORES,)),
            pltpu.SemaphoreType.DMA((7,)),
        ],
        compiler_params=pltpu.CompilerParams(
            collective_id=0, has_side_effects=True, vmem_limit_bytes=64 * 2**20 - 2**18
        ),
    )(hidden, kv_turned, gain, rope, queries, grads, span_table)


def hand_on_kernel(*refs):
    count = 4
    arrivals, departures = refs[-2:]
    steps = []
    for src, dst, held in zip(refs[:count], refs[count : 2 * count], refs[2 * count : 3 * count]):
        rows = src.shape[0]
        parts = 2 if rows in (WIDTH, HEADS) else 1
        for k in range(parts):
            at, n = pl.ds(k * (rows // parts), rows // parts), len(steps)
            steps.append(
                (
                    pltpu.make_async_copy(src.at[at], held.at[at], arrivals.at[n]),
                    pltpu.make_async_copy(held.at[at], dst.at[at], departures.at[n]),
                )
            )
    for arrival, _ in steps:
        arrival.start()
    for arrival, departure in steps:
        arrival.wait()
        departure.start()
    for _, departure in steps:
        departure.wait()


def hand_on(*arrays):
    anywhere = pl.BlockSpec(memory_space=pl.ANY)
    return pl.pallas_call(
        hand_on_kernel,
        out_shape=tuple(jax.ShapeDtypeStruct(a.shape, a.dtype) for a in arrays),
        in_specs=[anywhere] * len(arrays),
        out_specs=(anywhere,) * len(arrays),
        scratch_shapes=[pltpu.VMEM(a.shape, a.dtype) for a in arrays] + [pltpu.SemaphoreType.DMA((6,))] * 2,
        compiler_params=pltpu.CompilerParams(vmem_limit_bytes=63 * 2**20),
    )(*arrays)


def per_device(table, hidden, kv_down, kv_gain, queries, out_grad, span_table):
    query_grad, gain_grad, hidden_grad, down_grad = whole(
        hidden.reshape(4, 2, PIECE, MODEL),
        kv_down.T,
        kv_gain.reshape(1, LATENT),
        table,
        queries.transpose(1, 2, 0),
        out_grad.reshape(ROWS, LATENT),
        span_table,
    )
    query_grad, gain_grad, hidden_grad, down_grad = hand_on(query_grad, gain_grad, hidden_grad, down_grad)
    return (query_grad.transpose(2, 0, 1), hidden_grad, down_grad.T, gain_grad[0])


def solution(mesh):
    table = rope_rows()

    def run(hidden, kv_down, kv_gain, queries, out_grad, span_table):
        return jax.shard_map(
            per_device,
            mesh=mesh,
            in_specs=(
                P(),
                P("ctx", "head"),
                P("head", None),
                P(),
                P("ctx", "head", None),
                P("ctx", "head", None),
                P(),
            ),
            out_specs=(P("ctx", "head", None), P("ctx", "head"), P("head", None), P()),
            check_vma=False,
        )(jnp.asarray(table), hidden, kv_down, kv_gain, queries, out_grad, span_table)

    return run
```
